32 devices in a mesh: section: 2 (over x), tensor: 4 (over y, core), dp: 4 (over z).
Axes of the slice: x: 2, y: 2, z: 4, core: 2. Of those that a mesh axis runs over, the one named last changes fastest.
Arguments:
- boundary: bfloat16 [2, 8, 1024, 1536], P('section', 'dp', 'tensor'), may hold values from -6 to 6
- segments: int32 [8, 1024], P('dp'), may hold values from 0 to 4, as said below
- norm_gains: bfloat16 [2, 2, 1536], replicated, may hold values from 0.5 to 1.5
- qk_gains: bfloat16 [2, 64], replicated, may hold values from 0.5 to 1.5
- conv_in: bfloat16 [1536, 3, 1536], P(None, None, 'tensor'), may hold values from -0.15625 to 0.15625
- conv_kernel: bfloat16 [3, 1536], P(None, 'tensor'), may hold values from -3.5 to 3.5
- conv_out: bfloat16 [1536, 1536], P('tensor'), may hold values from -0.15625 to 0.15625
- attn_query: bfloat16 [1536, 1536], P(None, 'tensor'), may hold values from -0.15625 to 0.15625
- attn_keyval: bfloat16 [1536, 2, 512], P(None, None, 'tensor'), may hold values from -0.15625 to 0.15625
- attn_out: bfloat16 [1536, 1536], P('tensor'), may hold values from -1.25 to 1.25
- ffn_gate_up: bfloat16 [2, 1536, 2, 6912], P('section', None, None, 'tensor'), may hold values from -0.15625 to 0.15625
- ffn_down: bfloat16 [2, 1536, 6912], P('section', None, 'tensor'), may hold values from -0.078125 to 0.078125
Outputs:
- boundary_out: float32 [2, 8, 1024, 1536], P('section', 'dp', 'tensor')
- grad_norm_gains: float32 [2, 2, 1536], replicated
- grad_qk_gains: float32 [2, 64], replicated
- grad_conv_in: float32 [1536, 3, 1536], P(None, None, 'tensor')
- grad_conv_kernel: float32 [3, 1536], P(None, 'tensor')
- grad_conv_out: float32 [1536, 1536], P('tensor')
- grad_attn_query: float32 [1536, 1536], P(None, 'tensor')
- grad_attn_keyval: float32 [1536, 2, 512], P(None, None, 'tensor')
- grad_attn_out: float32 [1536, 1536], P('tensor')
- grad_ffn_gate_up: float32 [2, 1536, 2, 6912], P('section', None, None, 'tensor')
- grad_ffn_down: float32 [2, 1536, 6912], P('section', None, 'tensor')
The draws below stay inside these ranges and needn't reach their ends.
Inputs may be any that keep to these rules, and one draw needn't show every extreme that they name: `segments`: each row of 1024 positions holds five documents with ids 0 to 4 in order along the row; document 2 begins before position 66 and ends after position 957.
All inputs are finite; a program needn't handle non-finite values.
Results may differ from the reference program's by a relative error of at most 0.024.
Values may be sent and summed in bfloat16 or wider, within the bound.
A program may use at most 448 MiB of HBM per device.

```python
import jax
import jax.numpy as jnp
from jax import lax

D = 1536
FF = 6912
HEADS = 24
KV_HEADS = 8
HEAD_DIM = 64
KERNEL = 3
SEQ = 1024
ROWS = 8


def draw_segments(key, part):
    key = jax.random.fold_in(key, 7)
    subkeys = jax.random.split(key, 4)
    margin = SEQ // 16 + 2
    start_long = jax.random.randint(subkeys[0], (ROWS, 1), 2, margin)
    cut_early = jax.random.randint(subkeys[1], (ROWS, 1), 1, start_long)
    end_long = SEQ - jax.random.randint(subkeys[2], (ROWS, 1), 2, margin)
    cut_late = jax.random.randint(subkeys[3], (ROWS, 1), end_long + 1, SEQ)
    places = jnp.arange(SEQ, dtype=jnp.int32)[None, :]
    result = (places >= cut_early).astype(jnp.int32) + (places >= start_long).astype(jnp.int32)
    result = result + (places >= end_long).astype(jnp.int32) + (places >= cut_late).astype(jnp.int32)
    return result.astype(jnp.int32)


def block_levels(rng, extent, shards, least, high):
    level = 1.0
    for dim, shards_of in shards:
        heights = jax.random.uniform(jax.random.fold_in(jax.random.fold_in(rng, 6), dim), (shards_of,), jnp.float32, least / len(shards), high / len(shards))
        level = level * jnp.repeat(jnp.exp(heights), extent[dim] // shards_of).reshape((-1,) + (1,) * (len(extent) - 1 - dim))
    return level


def noise(key, extent, width, limit, pieces=(), kind=jnp.bfloat16):
    factor_of = block_levels(key, extent, pieces, -0.22, 0.18) if pieces else 1.0
    entries = jax.random.normal(key, extent, jnp.float32) * width * factor_of
    return jnp.minimum(jnp.maximum(entries, -limit), limit).astype(kind)


def setup_inputs(seed: int = 0) -> dict:
    splits = jax.random.split(jax.random.key(seed), 13)
    boundary = noise(splits[0], (2, ROWS, SEQ, D), 1.0, 6.0, ((0, 2), (1, 4), (2, 4)))
    segments = draw_segments(jax.random.fold_in(splits[12], 71), 0)
    norm_gains = jnp.clip(1.0 + 0.1 * jax.random.normal(splits[2], (2, 2, D), jnp.float32), 0.5, 1.5).astype(jnp.bfloat16)
    qk_gains = jnp.clip(1.0 + 0.1 * jax.random.normal(splits[3], (2, HEAD_DIM), jnp.float32), 0.5, 1.5).astype(jnp.bfloat16)
    conv_in = noise(splits[4], (D, 3, D), D ** -0.5, 0.15625, ((2, 4),))
    conv_kernel = noise(splits[5], (KERNEL, D), KERNEL ** -0.5, 3.5, ((1, 4),))
    conv_out = noise(splits[6], (D, D), D ** -0.5, 0.15625, ((0, 4),))
    attn_query = noise(splits[7], (D, HEADS * HEAD_DIM), D ** -0.5, 0.15625, ((1, 4),))
    attn_keyval = noise(splits[8], (D, 2, KV_HEADS * HEAD_DIM), D ** -0.5, 0.15625, ((2, 4),))
    attn_out = noise(splits[9], (HEADS * HEAD_DIM, D), (max(D // 64, 1)) ** -0.5, 1.25, ((0, 4),))
    ffn_gate_up = noise(splits[10], (2, D, 2, FF), D ** -0.5, 0.15625, ((0, 2), (3, 4)))
    ffn_down = noise(splits[11], (2, D, FF), FF ** -0.5, 0.078125, ((0, 2), (2, 4)))
    return dict(boundary=boundary, segments=segments, norm_gains=norm_gains, qk_gains=qk_gains, conv_in=conv_in, conv_kernel=conv_kernel, conv_out=conv_out, attn_query=attn_query, attn_keyval=attn_keyval, attn_out=attn_out, ffn_gate_up=ffn_gate_up, ffn_down=ffn_down)


EPSILON = 1e-05
THETA = 1000000.0
NEGATIVE = -1e+30
HIGHEST = lax.Precision.HIGHEST

@jax.custom_vjp
def low(v):
    return lax.optimization_barrier(v.astype(jnp.bfloat16)).astype(jnp.float32)

@jax.custom_vjp
def low_back(v):
    return v

def low_keep(v):
    return (low(v), None)

def low_pass(kept, grad):
    return (grad,)

def back_keep(v):
    return (v, None)

def back_low(kept, grad):
    return (low(grad),)
low.defvjp(low_keep, low_pass)
low_back.defvjp(back_keep, back_low)

def matmul(spec, left, right):
    return jnp.einsum(spec, left, right, precision=HIGHEST)

def rms_norm(values, gain):
    return values * lax.rsqrt(lax.optimization_barrier(jnp.mean(values * values, axis=-1, keepdims=True)) + EPSILON) * gain

def delay_rows(values, lag):
    widths = ((0, 0), (lag, 0)) + ((0, 0),) * (values.ndim - 2)
    return jnp.pad(values, widths)[:, :values.shape[1]]

def lag_masks(seg_ids, kernel_len):
    masks_list = []
    for lag in range(1, kernel_len):
        shifted = jnp.pad(seg_ids, ((0, 0), (lag, 0)), constant_values=-1)[:, :seg_ids.shape[1]]
        masks_list.append((shifted == seg_ids).astype(jnp.float32)[..., None])
    return masks_list

def conv_mixer(project, kernel, masks_list):
    gate_in = project[:, :, 0] * project[:, :, 2]
    running = kernel[0] * gate_in
    for lag in range(1, kernel.shape[0]):
        running = running + kernel[lag] * delay_rows(gate_in, lag) * masks_list[lag - 1]
    return project[:, :, 1] * running

def rope_tables(seg_ids, half_dim):
    starts = lax.optimization_barrier(jnp.sum((seg_ids[:, None, :] < seg_ids[:, :, None]).astype(jnp.int32), axis=2))
    places = jnp.arange(seg_ids.shape[1], dtype=jnp.int32)[None, :] - starts
    freqs = jnp.power(THETA, -(2.0 * jnp.arange(half_dim, dtype=jnp.float32)) / (2.0 * half_dim))
    angles = places.astype(jnp.float32)[..., None] * freqs
    return (jnp.cos(angles), jnp.sin(angles))

def head_prep(values, gain, cosine, sine):
    normed = rms_norm(values, gain)
    half_dim = values.shape[-1] // 2
    low_half = normed[..., :half_dim]
    high_half = normed[..., half_dim:]
    cos_b = cosine[..., None, :]
    sin_b = sine[..., None, :]
    return jnp.concatenate([low_half * cos_b - high_half * sin_b, high_half * cos_b + low_half * sin_b], axis=-1)

def allowed_mask(seg_row, start, block_len):
    length = seg_row.shape[0]
    query_pos = start + jnp.arange(block_len, dtype=jnp.int32)
    key_pos = jnp.arange(length, dtype=jnp.int32)
    seg_query = lax.dynamic_slice_in_dim(seg_row, start, block_len)
    return (key_pos[None, :] <= query_pos[:, None]) & (seg_row[None, :] == seg_query[:, None])

def attend_block(index, query, keyed, valued, seg_row, block_len):
    scaling = query.shape[3] ** (-0.5)
    start = (index * block_len).astype(jnp.int32)
    q_block = lax.dynamic_slice_in_dim(query, start, block_len, 2)
    scores = low_back(matmul('kgqd,ksd->kgqs', q_block, keyed) * scaling)
    probs = jax.nn.softmax(jnp.where(allowed_mask(seg_row, start, block_len), scores, NEGATIVE), axis=-1)
    return low_back(low(matmul('kgqs,ksd->kgqd', low(probs), valued)))

def ffn_part(hidden, gain, gate_up, down):
    normed = low(rms_norm(hidden, gain))
    mixed = low_back(matmul('td,dcf->tcf', normed, gate_up))
    active = low(jax.nn.silu(mixed[:, 0]) * mixed[:, 1])
    return hidden + low_back(matmul('tf,df->td', active, down))

def row_forward(params, row_in, seg_ids):
    norm_gains, qk_gains, conv_in, conv_kernel, conv_out, attn_query, attn_keyval, attn_out, ffn_gate_up, ffn_down = params
    length = row_in.shape[0]
    normed = low(rms_norm(row_in, norm_gains[0, 0]))
    project = low_back(matmul('td,dce->tce', normed, conv_in))
    mixed = low(conv_mixer(project[None], conv_kernel, lag_masks(seg_ids[None], conv_kernel.shape[0]))[0])
    hidden = row_in + low_back(matmul('te,ed->td', mixed, conv_out))
    hidden = ffn_part(hidden, norm_gains[0, 1], ffn_gate_up[0], ffn_down[0])
    second = low_back(low(hidden))
    normed = low(rms_norm(second, norm_gains[1, 0]))
    head_dim = qk_gains.shape[1]
    heads = attn_query.shape[1] // head_dim
    kv_heads = attn_keyval.shape[2] // head_dim
    groups = heads // kv_heads
    query_raw = low_back(matmul('td,de->te', normed, attn_query)).reshape(length, heads, head_dim)
    keyval_raw = low_back(matmul('td,dce->tce', normed, attn_keyval))
    cosine, sine = rope_tables(seg_ids[None], head_dim // 2)
    cosine = cosine[0]
    sine = sine[0]
    query = low(head_prep(query_raw, qk_gains[0], cosine, sine))
    query = query.reshape(length, kv_heads, groups, head_dim).transpose(1, 2, 0, 3)
    keyed = low(head_prep(keyval_raw[:, 0].reshape(length, kv_heads, head_dim), qk_gains[1], cosine, sine))
    keyed = keyed.transpose(1, 0, 2)
    valued = low(keyval_raw[:, 1].reshape(length, kv_heads, head_dim)).transpose(1, 0, 2)
    block_len = min(512, length)
    count = length // block_len
    blocks = lax.map(jax.checkpoint(lambda index: attend_block(index, query, keyed, valued, seg_ids, block_len)), jnp.arange(count, dtype=jnp.int32))
    attended = blocks.transpose(0, 3, 1, 2, 4).reshape(length, heads * head_dim)
    hidden = second + low_back(matmul('te,ed->td', attended, attn_out))
    return ffn_part(hidden, norm_gains[1, 1], ffn_gate_up[1], ffn_down[1])

def reference(boundary, segments, norm_gains, qk_gains, conv_in, conv_kernel, conv_out, attn_query, attn_keyval, attn_out, ffn_gate_up, ffn_down):
    params = tuple((weight.astype(jnp.float32) for weight in (norm_gains, qk_gains, conv_in, conv_kernel, conv_out, attn_query, attn_keyval, attn_out, ffn_gate_up, ffn_down)))
    inputs = boundary[0].astype(jnp.float32)
    cotangent = boundary[1].astype(jnp.float32)
    row_fn = jax.checkpoint(row_forward)

    def whole(weights, values):
        return lax.map(lambda paired: row_fn(weights, paired[0], paired[1]), (values, segments))
    outputs, pull = jax.vjp(whole, params, inputs)
    grads, grad_inputs = pull(cotangent)
    return (jnp.stack([grad_inputs, outputs]), grads[0], grads[1], grads[2], grads[3], grads[4], grads[5], grads[6], grads[7], grads[8], grads[9])
```

```python
import jax
import jax.numpy as jnp
from jax import lax
from jax.sharding import PartitionSpec as P

EPSILON = 1e-05
THETA = 1000000.0
NEGATIVE = -1e30
BF = jnp.bfloat16
F32 = jnp.float32


def mm(spec, left, right, kind=F32):
    return jnp.einsum(spec, left, right, preferred_element_type=F32).astype(kind)


def inverse_rms(values):
    return lax.rsqrt(jnp.mean(values * values, axis=-1, keepdims=True) + EPSILON)


def norm(values, gain):
    return (values * inverse_rms(values) * gain).astype(BF)


def norm_back(values, gain, grad):
    scale = inverse_rms(values)
    normed = values * scale
    weighted = grad * gain
    grad_in = scale * (weighted - normed * jnp.mean(weighted * normed, axis=-1, keepdims=True))
    return grad_in, grad * normed


def section_pairs(section, size, function):
    return [
        (section * size + i, section * size + function(i))
        for i in range(size)
        if 0 <= function(i) < size
    ]


def permute(values, section, axis, function):
    pairs = section_pairs(section, lax.axis_size(axis), function)
    return lax.ppermute(values, ("section", axis), pairs)


def pick(values, index, axis):
    return lax.dynamic_index_in_dim(values, index, axis, keepdims=False)


def delay_rows(values, lag):
    widths = ((0, 0), (lag, 0)) + ((0, 0),) * (values.ndim - 2)
    return jnp.pad(values, widths)[:, : values.shape[1]]


def advance_rows(values, lag):
    widths = ((0, 0), (0, lag)) + ((0, 0),) * (values.ndim - 2)
    return jnp.pad(values, widths)[:, lag:]


def lag_masks(seg_ids, kernel_len):
    masks_list = []
    for lag in range(1, kernel_len):
        shifted = jnp.pad(seg_ids, ((0, 0), (lag, 0)), constant_values=-1)[:, : seg_ids.shape[1]]
        masks_list.append((shifted == seg_ids).astype(F32)[..., None])
    return masks_list


def rope_tables(seg_ids, half_dim):
    starts = jnp.sum((seg_ids[:, None, :] < seg_ids[:, :, None]).astype(jnp.int32), axis=2)
    places = jnp.arange(seg_ids.shape[1], dtype=jnp.int32)[None, :] - starts
    freqs = jnp.power(THETA, -(2.0 * jnp.arange(half_dim, dtype=F32)) / (2.0 * half_dim))
    angles = places.astype(F32)[..., None] * freqs
    return (jnp.cos(angles), jnp.sin(angles))


def head_prep(values, gain, cosine, sine):
    normed = values * inverse_rms(values) * gain
    half_dim = values.shape[-1] // 2
    low_half = normed[..., :half_dim]
    high_half = normed[..., half_dim:]
    cos_b = cosine[..., None, :]
    sin_b = sine[..., None, :]
    return jnp.concatenate(
        [low_half * cos_b - high_half * sin_b, high_half * cos_b + low_half * sin_b], axis=-1
    )


def allowed_mask(seg_row, start, block_len):
    length = seg_row.shape[0]
    query_pos = start + jnp.arange(block_len, dtype=jnp.int32)
    key_pos = jnp.arange(length, dtype=jnp.int32)
    seg_query = lax.dynamic_slice_in_dim(seg_row, start, block_len)
    return (key_pos[None, :] <= query_pos[:, None]) & (seg_row[None, :] == seg_query[:, None])


def regroup(blocks):
    moved = jnp.moveaxis(blocks, 0, 2)
    return moved.reshape(moved.shape[:2] + (moved.shape[2] * moved.shape[3],) + moved.shape[4:])


def attend_row(query, keyed, valued, seg_row):
    length = query.shape[2]
    block_len = min(512, length)
    scaling = query.shape[3] ** (-0.5)

    def one_block(index):
        start = index * block_len
        q_block = lax.dynamic_slice_in_dim(query, start, block_len, 2)
        scores = mm("kgqd,ksd->kgqs", q_block, keyed) * scaling
        scores = jnp.where(allowed_mask(seg_row, start, block_len), scores, NEGATIVE)
        largest = jnp.max(scores, axis=-1)
        expon = jnp.exp(scores - largest[..., None])
        totals = jnp.sum(expon, axis=-1)
        probs = (expon / totals[..., None]).astype(BF)
        attended = mm("kgqs,ksd->kgqd", probs, valued, BF)
        return (attended, largest + jnp.log(totals))

    attended, logsum = lax.map(one_block, jnp.arange(length // block_len, dtype=jnp.int32))
    return (regroup(attended), regroup(logsum))


def attend_back(query, keyed, valued, seg_row, logsum, grad_out):
    length = query.shape[2]
    block_len = min(512, length)
    scaling = query.shape[3] ** (-0.5)

    def one_block(carry, index):
        grad_key, grad_val = carry
        start = index * block_len
        q_block = lax.dynamic_slice_in_dim(query, start, block_len, 2)
        g_block = lax.dynamic_slice_in_dim(grad_out, start, block_len, 2)
        l_block = lax.dynamic_slice_in_dim(logsum, start, block_len, 2)
        scores = mm("kgqd,ksd->kgqs", q_block, keyed) * scaling
        scores = jnp.where(allowed_mask(seg_row, start, block_len), scores, NEGATIVE)
        probs = jnp.exp(scores - l_block[..., None])
        probs_low = probs.astype(BF)
        grad_probs = mm("kgqd,ksd->kgqs", g_block, valued)
        inner = jnp.sum(probs * grad_probs, axis=-1, keepdims=True)
        grad_scores = (probs * (grad_probs - inner)).astype(BF)
        grad_query = mm("kgqs,ksd->kgqd", grad_scores, keyed) * scaling
        grad_key = grad_key + mm("kgqs,kgqd->ksd", grad_scores, q_block) * scaling
        grad_val = grad_val + mm("kgqs,kgqd->ksd", probs_low, g_block)
        return ((grad_key, grad_val), grad_query)

    zeros_kv = jnp.zeros(keyed.shape, F32)
    carried, stacked = lax.scan(
        one_block, (zeros_kv, zeros_kv), jnp.arange(length // block_len, dtype=jnp.int32)
    )
    return (regroup(stacked), carried[0], carried[1])


def on_device(
    boundary,
    segments,
    norm_gains,
    qk_gains,
    conv_in,
    conv_kernel,
    conv_out,
    attn_query,
    attn_keyval,
    attn_out,
    ffn_gate_up,
    ffn_down,
):
    is_first = lax.axis_index("section") == 0
    place = lax.axis_index("tensor")
    tensor = lax.axis_size("tensor")
    dp = lax.axis_size("dp")
    core = place % 2
    chip = place // 2
    chips = tensor // 2
    steps = [1 << k for k in range(chips.bit_length() - 1)]
    local = boundary[0]
    rows, seq_local, width = local.shape
    seq = segments.shape[1]
    head_dim = qk_gains.shape[1]
    heads_here = attn_query.shape[1] // head_dim
    kv_here = attn_keyval.shape[2] // head_dim
    groups = heads_here // kv_here
    gains = norm_gains.astype(F32)
    head_gains = qk_gains.astype(F32)
    kernel = conv_kernel.astype(F32)
    hidden = ffn_down.shape[2]
    gate_up_w = ffn_gate_up[0].reshape(width, 2 * hidden)
    down_w = ffn_down[0]
    home = rows * chips * seq_local

    def mate(values, section):
        return permute(values, section, "tensor", lambda i: i ^ 1)

    def chip_gather(values, section):
        held = values[:, None]
        for step in steps:
            other = permute(held, section, "tensor", lambda i: i ^ (2 * step))
            upper = (chip // step) % 2 == 1
            held = jnp.where(
                upper,
                jnp.concatenate([other, held], axis=1),
                jnp.concatenate([held, other], axis=1),
            )
        return held

    def chip_sum(values, section):
        for step in steps:
            values = values + permute(
                values.astype(BF), section, "tensor", lambda i: i ^ (2 * step)
            ).astype(F32)
        return values

    def chip_scatter(values, section):
        for step in reversed(steps):
            halves = values.reshape((rows, 2, step) + values.shape[2:])
            upper = (chip // step) % 2
            kept = pick(halves, upper, 1)
            sent = pick(halves, 1 - upper, 1).astype(BF)
            values = kept + permute(sent, section, "tensor", lambda i: i ^ (2 * step)).astype(F32)
        return values[:, 0]

    def weave(mine, other):
        both = jnp.where(
            core == 0, jnp.stack([mine, other], axis=2), jnp.stack([other, mine], axis=2)
        )
        return both.reshape((rows, seq) + mine.shape[3:])

    def part(full, index):
        return pick(full.reshape((rows, chips, 2, seq_local) + full.shape[2:]), index, 2)

    def core_sum(mine, sent, section):
        return mine + mate(sent, section).astype(F32)

    def when(section, function, *args):
        shapes = jax.eval_shape(function, *args)
        zeros = lambda *unused: jax.tree.map(lambda s: jnp.zeros(s.shape, s.dtype), shapes)
        return lax.cond(is_first if section == 0 else ~is_first, function, zeros, *args)

    def conv_parts(project, masks_list):
        gate_in = project[:, :, 0] * project[:, :, 2]
        running = kernel[0] * gate_in
        for lag in range(1, kernel.shape[0]):
            running = running + kernel[lag] * delay_rows(gate_in, lag) * masks_list[lag - 1]
        return gate_in, running

    def outward(full_in, weight):
        mine = mm("rkte,ed->rktd", part(full_in, core), weight)
        sent = mm("rkte,ed->rktd", part(full_in, 1 - core), weight, BF)
        return mine, sent

    def conv_forward(mine, other):
        full = weave(mine, other)
        project = mm("rtd,dce->rtce", full, conv_in)
        unused, running = conv_parts(project, lag_masks(segments, kernel.shape[0]))
        mixed = (project[:, :, 1] * running).astype(BF)
        return outward(mixed, conv_out) + (project.astype(BF), mixed, full)

    def arrange(query, keyed, valued):
        q_all = query.reshape(rows, seq, kv_here, groups, head_dim).transpose(0, 2, 3, 1, 4)
        return (q_all, keyed.transpose(0, 2, 1, 3), valued.transpose(0, 2, 1, 3))

    def attn_forward(mine, other):
        full = weave(mine, other)
        query_raw = mm("rtd,de->rte", full, attn_query).reshape(rows, seq, heads_here, head_dim)
        keyval_raw = mm("rtd,dce->rtce", full, attn_keyval)
        key_raw = keyval_raw[:, :, 0].reshape(rows, seq, kv_here, head_dim)
        val_raw = keyval_raw[:, :, 1].reshape(rows, seq, kv_here, head_dim)
        cosine, sine = rope_tables(segments, head_dim // 2)
        query = head_prep(query_raw, head_gains[0], cosine, sine).astype(BF)
        keyed = head_prep(key_raw, head_gains[1], cosine, sine).astype(BF)
        q_all, k_all, v_all = arrange(query, keyed, val_raw.astype(BF))
        attended, logsum = lax.map(lambda item: attend_row(*item), (q_all, k_all, v_all, segments))
        flat = attended.transpose(0, 3, 1, 2, 4).reshape(rows, seq, heads_here * head_dim)
        saved = (query_raw, key_raw, q_all, k_all, v_all, logsum, flat, full)
        return outward(flat, attn_out) + saved

    def conv_backward(mine, other, project, mixed, full):
        grad_full = weave(mine, other)
        masks_list = lag_masks(segments, kernel.shape[0])
        project = project.astype(F32)
        gate_in, running = conv_parts(project, masks_list)
        grad_mixed = mm("rtd,ed->rte", grad_full, conv_out)
        grad_c = grad_mixed * running
        grad_run = grad_mixed * project[:, :, 1]
        grad_in = kernel[0] * grad_run
        grad_kernel = [jnp.sum(grad_run * gate_in, axis=(0, 1))]
        for lag in range(1, kernel.shape[0]):
            mask = masks_list[lag - 1]
            grad_in = grad_in + kernel[lag] * advance_rows(grad_run * mask, lag)
            grad_kernel.append(jnp.sum(grad_run * mask * delay_rows(gate_in, lag), axis=(0, 1)))
        grad_low = jnp.stack(
            [grad_in * project[:, :, 2], grad_c, grad_in * project[:, :, 0]], axis=2
        ).astype(BF)
        mine_in = mm("rktce,dce->rktd", part(grad_low, core), conv_in)
        sent_in = mm("rktce,dce->rktd", part(grad_low, 1 - core), conv_in, BF)
        grad_cout = mm("rte,rtd->ed", mixed, grad_full, BF)
        grad_cin = mm("rtd,rtce->dce", full, grad_low, BF)
        return mine_in, sent_in, (grad_cin, jnp.stack(grad_kernel).astype(BF), grad_cout)

    def attn_backward(mine, other, query_raw, key_raw, q_all, k_all, v_all, logsum, flat, full):
        grad_full = weave(mine, other)
        cosine, sine = rope_tables(segments, head_dim // 2)
        unused, query_pull = jax.vjp(
            lambda values, gain: head_prep(values, gain, cosine, sine), query_raw, head_gains[0]
        )
        unused, key_pull = jax.vjp(
            lambda values, gain: head_prep(values, gain, cosine, sine), key_raw, head_gains[1]
        )
        grad_flat = mm("rtd,ed->rte", grad_full, attn_out, BF)
        grad_heads = grad_flat.reshape(rows, seq, kv_here, groups, head_dim).transpose(
            0, 2, 3, 1, 4
        )
        grad_q, grad_k, grad_v = lax.map(
            lambda item: attend_back(*item), (q_all, k_all, v_all, segments, logsum, grad_heads)
        )
        grad_qraw, grad_qgain = query_pull(
            grad_q.transpose(0, 3, 1, 2, 4).reshape(rows, seq, heads_here, head_dim)
        )
        grad_kraw, grad_kgain = key_pull(grad_k.transpose(0, 2, 1, 3))
        query_low = grad_qraw.reshape(rows, seq, heads_here * head_dim).astype(BF)
        kv_low = jnp.stack(
            [
                grad_kraw.reshape(rows, seq, kv_here * head_dim),
                grad_v.transpose(0, 2, 1, 3).reshape(rows, seq, kv_here * head_dim),
            ],
            axis=2,
        ).astype(BF)

        def inward(index):
            return mm("rkte,de->rktd", part(query_low, index), attn_query) + mm(
                "rktce,dce->rktd", part(kv_low, index), attn_keyval
            )

        mine_in = inward(core)
        sent_in = inward(1 - core).astype(BF)
        grad_aout = mm("rte,rtd->ed", flat, grad_full, BF)
        grad_aq = mm("rtd,rte->de", full, query_low, BF)
        grad_akv = mm("rtd,rtce->dce", full, kv_low, BF)
        return (
            mine_in,
            sent_in,
            (grad_aq, grad_akv, grad_aout),
            jnp.stack([grad_qgain, grad_kgain]),
        )

    def flat_tokens(mine, other):
        return jnp.stack([mine, other]).reshape(2 * home, mine.shape[-1])

    def gate_up(both):
        return mm("td,df->tf", both, gate_up_w, BF)

    def activate(gu):
        gate = gu[:, :hidden].astype(F32)
        return (jax.nn.silu(gate) * gu[:, hidden:].astype(F32)).astype(BF)

    def shaped(tokens):
        return tokens.reshape(rows, chips, seq_local, width)

    def ffn_out(act):
        mine = mm("tf,df->td", act[:home], down_w)
        sent = mm("tf,df->td", act[home:], down_w, BF)
        return shaped(mine), shaped(sent)

    def ffn_back(grad_both, gu):
        grad_act = mm("td,df->tf", grad_both, down_w)
        gate = gu[:, :hidden].astype(F32)
        up = gu[:, hidden:].astype(F32)
        sig = jax.nn.sigmoid(gate)
        slope = sig * (1.0 + gate * (1.0 - sig))
        grad_gu = jnp.concatenate([grad_act * up * slope, grad_act * gate * sig], axis=1).astype(BF)
        mine = mm("tf,df->td", grad_gu[:home], gate_up_w)
        sent = mm("tf,df->td", grad_gu[home:], gate_up_w, BF)
        return grad_gu, shaped(mine), shaped(sent)

    def ffn_weights(both, gu, grad_both, grad_gu):
        act = activate(gu)
        grad_down = mm("td,tf->df", grad_both, act, BF)
        grad_up = mm("td,tf->df", both, grad_gu, BF)
        return grad_up, grad_down

    x_home = chip_gather(local, 0).astype(F32)
    cot_home = chip_gather(local, 1)
    cot_mate = mate(cot_home, 1)
    cot_both = flat_tokens(cot_home, cot_mate)

    z_home = norm(x_home, gains[0, 0])
    mine, sent, project, mixed, full1 = when(0, conv_forward, z_home, mate(z_home, 0))
    h1 = x_home + chip_sum(core_sum(mine, sent, 0), 0)
    z_home = norm(h1, gains[0, 1])
    both1 = flat_tokens(z_home, mate(z_home, 0))
    gu1 = gate_up(both1)
    mine, sent = ffn_out(activate(gu1))
    x2_local = pick(h1, chip, 1) + chip_scatter(core_sum(mine, sent, 0), 0)

    crossing = lax.ppermute(x2_local.astype(BF), "section", [(0, 1)])
    x2_home = chip_gather(crossing, 1).astype(F32)
    z_home = norm(x2_home, gains[1, 0])
    mine, sent, *saved = when(1, attn_forward, z_home, mate(z_home, 1))
    h3 = x2_home + chip_sum(core_sum(mine, sent, 1), 1)
    z_home = norm(h3, gains[1, 1])
    both2 = flat_tokens(z_home, mate(z_home, 1))
    gu2 = gate_up(both2)

    grad_gu2, mine, sent = ffn_back(cot_both, gu2)
    dz = chip_sum(core_sum(mine, sent, 1), 1)
    grad_norm, gain_terms = norm_back(h3, gains[1, 1], dz)
    gain_ffn2 = jnp.sum(pick(gain_terms, chip, 1), axis=(0, 1))
    gh3 = cot_home.astype(F32) + grad_norm
    gm_home = gh3.astype(BF)
    mine, sent, attn_grads, head_grads = when(
        1, attn_backward, gm_home, mate(gm_home, 1), *saved
    )
    dz = chip_scatter(core_sum(mine, sent, 1), 1)
    grad_norm, gain_terms = norm_back(pick(x2_home, chip, 1), gains[1, 0], dz)
    gain_mix2 = jnp.sum(gain_terms, axis=(0, 1))
    gx2_local = pick(gh3, chip, 1) + grad_norm

    crossing = lax.ppermute(gx2_local.astype(BF), "section", [(1, 0)])
    g_home = chip_gather(crossing, 0)
    g_both = flat_tokens(g_home, mate(g_home, 0))

    grad_gu1, mine, sent = ffn_back(g_both, gu1)
    late = (both1, gu1, g_both, grad_gu1, both2, gu2, cot_both, grad_gu2)
    grad_up, grad_down, mine_y, sent_y = lax.cond(
        is_first,
        lambda *args: ffn_weights(*args[:4])
        + (jnp.zeros((rows, chips, seq_local, width), F32), jnp.zeros((rows, chips, seq_local, width), BF)),
        lambda *args: ffn_weights(*args[4:]) + ffn_out(activate(args[5])),
        *late,
    )
    full_gu = lax.psum(grad_up, "dp")
    full_down = lax.psum(grad_down, "dp")
    y_local = pick(h3, chip, 1) + chip_scatter(core_sum(mine_y, sent_y, 1), 1)
    dz = chip_sum(core_sum(mine, sent, 0), 0)
    grad_norm, gain_terms = norm_back(h1, gains[0, 1], dz)
    gain_ffn1 = jnp.sum(pick(gain_terms, chip, 1), axis=(0, 1))
    gh1 = g_home.astype(F32) + grad_norm
    gm_home = gh1.astype(BF)
    mine, sent, conv_grads = when(
        0, conv_backward, gm_home, mate(gm_home, 0), project, mixed, full1
    )
    dz = chip_scatter(core_sum(mine, sent, 0), 0)
    grad_norm, gain_terms = norm_back(pick(x_home, chip, 1), gains[0, 0], dz)
    gain_mix1 = jnp.sum(gain_terms, axis=(0, 1))
    gx_local = pick(gh1, chip, 1) + grad_norm

    mixer_sums = jax.tree.map(
        lambda v: v.astype(F32), lax.psum(conv_grads + attn_grads, ("section", "dp"))
    )
    zero = jnp.zeros_like(gain_mix1)
    first_gains = jnp.stack([jnp.stack([gain_mix1, gain_ffn1]), jnp.stack([zero, zero])])
    second_gains = jnp.stack([jnp.stack([zero, zero]), jnp.stack([gain_mix2, gain_ffn2])])
    grad_gains = jnp.where(is_first, first_gains, second_gains)
    grad_gains, grad_heads = lax.psum((grad_gains, head_grads), ("section", "tensor", "dp"))
    boundary_out = jnp.where(is_first, gx_local, y_local)[None]
    return (boundary_out, grad_gains, grad_heads) + mixer_sums + (
        full_gu.astype(F32).reshape(ffn_gate_up.shape),
        full_down.astype(F32)[None],
    )


def solution(mesh):
    placed = (
        P("section", "dp", "tensor", None),
        P("dp", None),
        P(),
        P(),
        P(None, None, "tensor"),
        P(None, "tensor"),
        P("tensor", None),
        P(None, "tensor"),
        P(None, None, "tensor"),
        P("tensor", None),
        P("section", None, None, "tensor"),
        P("section", None, "tensor"),
    )
    return jax.shard_map(
        on_device,
        mesh=mesh,
        in_specs=placed,
        out_specs=(
            P("section", "dp", "tensor", None),
            P(),
            P(),
            P(None, None, "tensor"),
            P(None, "tensor"),
            P("tensor", None),
            P(None, "tensor"),
            P(None, None, "tensor"),
            P("tensor", None),
            P("section", None, None, "tensor"),
            P("section", None, "tensor"),
        ),
        check_vma=False,
    )
```

```python
import functools

import jax
import jax.numpy as jnp
from jax import lax
from jax.experimental import pallas as pl
from jax.experimental.pallas import tpu as pltpu
from jax.sharding import PartitionSpec as P

EPSILON = 1e-05
THETA = 1000000.0
NEGATIVE = -1e30
BF = jnp.bfloat16
F32 = jnp.float32
MESH = pl.DeviceIdType.MESH
TILE = 64
VMEM_BYTES = 60 * 1024 * 1024


def mm(spec, left, right, kind=F32):
    return jnp.einsum(spec, left, right, preferred_element_type=F32).astype(kind)


def inverse_rms(values):
    return lax.rsqrt(jnp.mean(values * values, axis=-1, keepdims=True) + EPSILON)


def norm(values, gain):
    return (values * inverse_rms(values) * gain).astype(BF)


def norm_back(values, gain, grad):
    scale = inverse_rms(values)
    normed = values * scale
    weighted = grad * gain
    grad_in = scale * (weighted - normed * jnp.mean(weighted * normed, axis=-1, keepdims=True))
    return grad_in, grad * normed


def section_pairs(section, size, function):
    return [
        (section * size + i, section * size + function(i))
        for i in range(size)
        if 0 <= function(i) < size
    ]


def permute(values, section, axis, function):
    pairs = section_pairs(section, lax.axis_size(axis), function)
    return lax.ppermute(values, ("section", axis), pairs)


def pick(values, index, axis):
    return lax.dynamic_index_in_dim(values, index, axis, keepdims=False)


def delay_rows(values, lag):
    widths = ((0, 0), (lag, 0)) + ((0, 0),) * (values.ndim - 2)
    return jnp.pad(values, widths)[:, : values.shape[1]]


def advance_rows(values, lag):
    widths = ((0, 0), (0, lag)) + ((0, 0),) * (values.ndim - 2)
    return jnp.pad(values, widths)[:, lag:]


def lag_masks(seg_ids, kernel_len):
    masks_list = []
    for lag in range(1, kernel_len):
        shifted = jnp.pad(seg_ids, ((0, 0), (lag, 0)), constant_values=-1)[:, : seg_ids.shape[1]]
        masks_list.append((shifted == seg_ids).astype(F32)[..., None])
    return masks_list


def rope_tables(seg_ids, half_dim):
    starts = jnp.sum((seg_ids[:, None, :] < seg_ids[:, :, None]).astype(jnp.int32), axis=2)
    places = jnp.arange(seg_ids.shape[1], dtype=jnp.int32)[None, :] - starts
    freqs = jnp.power(THETA, -(2.0 * jnp.arange(half_dim, dtype=F32)) / (2.0 * half_dim))
    angles = places.astype(F32)[..., None] * freqs
    return (jnp.cos(angles), jnp.sin(angles))


def head_prep(values, gain, cosine, sine):
    normed = values * inverse_rms(values) * gain
    half_dim = values.shape[-1] // 2
    low_half = normed[..., :half_dim]
    high_half = normed[..., half_dim:]
    cos_b = cosine[..., None, :]
    sin_b = sine[..., None, :]
    return jnp.concatenate(
        [low_half * cos_b - high_half * sin_b, high_half * cos_b + low_half * sin_b], axis=-1
    )


def allowed_mask(seg_row, start, block_len):
    length = seg_row.shape[0]
    query_pos = start + jnp.arange(block_len, dtype=jnp.int32)
    key_pos = jnp.arange(length, dtype=jnp.int32)
    seg_query = lax.dynamic_slice_in_dim(seg_row, start, block_len)
    return (key_pos[None, :] <= query_pos[:, None]) & (seg_row[None, :] == seg_query[:, None])


def regroup(blocks):
    moved = jnp.moveaxis(blocks, 0, 2)
    return moved.reshape(moved.shape[:2] + (moved.shape[2] * moved.shape[3],) + moved.shape[4:])


def attend_row(query, keyed, valued, seg_row):
    length = query.shape[2]
    block_len = min(512, length)
    scaling = query.shape[3] ** (-0.5)

    def one_block(index):
        start = index * block_len
        q_block = lax.dynamic_slice_in_dim(query, start, block_len, 2)
        scores = mm("kgqd,ksd->kgqs", q_block, keyed) * scaling
        scores = jnp.where(allowed_mask(seg_row, start, block_len), scores, NEGATIVE)
        largest = jnp.max(scores, axis=-1)
        expon = jnp.exp(scores - largest[..., None])
        totals = jnp.sum(expon, axis=-1)
        probs = (expon / totals[..., None]).astype(BF)
        attended = mm("kgqs,ksd->kgqd", probs, valued, BF)
        return (attended, largest + jnp.log(totals))

    attended, logsum = lax.map(one_block, jnp.arange(length // block_len, dtype=jnp.int32))
    return (regroup(attended), regroup(logsum))


def attend_back(query, keyed, valued, seg_row, logsum, grad_out):
    length = query.shape[2]
    block_len = min(512, length)
    scaling = query.shape[3] ** (-0.5)

    def one_block(carry, index):
        grad_key, grad_val = carry
        start = index * block_len
        q_block = lax.dynamic_slice_in_dim(query, start, block_len, 2)
        g_block = lax.dynamic_slice_in_dim(grad_out, start, block_len, 2)
        l_block = lax.dynamic_slice_in_dim(logsum, start, block_len, 2)
        scores = mm("kgqd,ksd->kgqs", q_block, keyed) * scaling
        scores = jnp.where(allowed_mask(seg_row, start, block_len), scores, NEGATIVE)
        probs = jnp.exp(scores - l_block[..., None])
        probs_low = probs.astype(BF)
        grad_probs = mm("kgqd,ksd->kgqs", g_block, valued)
        inner = jnp.sum(probs * grad_probs, axis=-1, keepdims=True)
        grad_scores = (probs * (grad_probs - inner)).astype(BF)
        grad_query = mm("kgqs,ksd->kgqd", grad_scores, keyed) * scaling
        grad_key = grad_key + mm("kgqs,kgqd->ksd", grad_scores, q_block) * scaling
        grad_val = grad_val + mm("kgqs,kgqd->ksd", probs_low, g_block)
        return ((grad_key, grad_val), grad_query)

    zeros_kv = jnp.zeros(keyed.shape, F32)
    carried, stacked = lax.scan(
        one_block, (zeros_kv, zeros_kv), jnp.arange(length // block_len, dtype=jnp.int32)
    )
    return (regroup(stacked), carried[0], carried[1])


class Peers:
    def __init__(self):
        self.section = lax.axis_index("section")
        place = lax.axis_index("tensor")
        core = place % 2
        self.chip = place // 2
        self.mate = {"tensor": place + 1 - 2 * core}
        self.beside = {"tensor": place + 2 - 4 * self.chip}
        self.across = {"section": 1 - self.section}
        self.corner = {"section": 1 - self.section, "tensor": place + 2 - 4 * self.chip}


def greet(signalled, count):
    barrier = pltpu.get_barrier_semaphore()
    for device in signalled:
        pl.semaphore_signal(barrier, inc=1, device_id=device, device_id_type=MESH)
    pl.semaphore_wait(barrier, count)


def remote(source, target, send, receive, device):
    return pltpu.make_async_remote_copy(
        src_ref=source,
        dst_ref=target,
        send_sem=send,
        recv_sem=receive,
        device_id=device,
        device_id_type=MESH,
    )


def loop(count, body):
    lax.fori_loop(0, count, lambda i, unused: (body(i), 0)[1], 0)


def tile_rows(index):
    return pl.ds(pl.multiple_of(index * TILE, TILE), TILE)


def home_tile(j, chip, per_chip):
    each = per_chip // TILE
    return ((j // each) * 2 + chip) * each + j % each


def rms_tile(values):
    return lax.rsqrt(jnp.mean(values * values, axis=-1, keepdims=True) + EPSILON)


def norm_back_tile(values, gain, grad):
    scale = rms_tile(values)
    normed = values * scale
    weighted = grad * gain
    inner = jnp.mean(weighted * normed, axis=-1, keepdims=True)
    return scale * (weighted - normed * inner), grad * normed


def comm_call(kernel, name, number, inputs, outs, scratch, where):
    return pl.pallas_call(
        kernel,
        name=name,
        out_shape=outs,
        in_specs=[pl.BlockSpec(memory_space=space) for space in where],
        out_specs=tuple(pl.BlockSpec(memory_space=pltpu.VMEM) for unused in outs),
        scratch_shapes=scratch,
        compiler_params=pltpu.CompilerParams(
            collective_id=number, has_side_effects=True, vmem_limit_bytes=VMEM_BYTES
        ),
    )(*inputs)


def sum_tiles(active, backward, per_chip, *refs):
    if backward:
        sent, mine, hidden, grad, gain, out, low, low_mate, gain_out = refs[:9]
        scratch = refs[9:]
    else:
        sent, mine, residual, gain, out, low, low_mate = refs[:7]
        scratch = refs[7:]
    from_mate, summed, from_chip, relayed = scratch[:4]
    mate_s, mate_r, chip_s, chip_r, relay_s, relay_r, low_s, low_r = scratch[4:]
    peers = Peers()
    count = mine.shape[0] // TILE
    pairs = count // 2

    def mate_copy(i):
        rows = tile_rows(i)
        return remote(sent.at[rows], from_mate.at[rows], mate_s.at[i], mate_r.at[i], peers.mate)

    def direct(i):
        rows = tile_rows(i)
        return remote(summed.at[rows], from_chip.at[rows], chip_s.at[i], chip_r.at[i], peers.beside)

    def detour(p):
        return remote(
            summed.at[tile_rows(2 * p)],
            relayed.at[tile_rows(p)],
            chip_s.at[2 * p],
            relay_r.at[p],
            peers.corner,
        )

    def back(p):
        return remote(
            relayed.at[tile_rows(p)],
            from_chip.at[tile_rows(2 * p)],
            relay_s.at[p],
            chip_r.at[2 * p],
            peers.across,
        )

    def low_copy(i):
        rows = tile_rows(i)
        return remote(low.at[rows], low_mate.at[rows], low_s.at[i], low_r.at[i], peers.mate)

    @pl.when(peers.section == active)
    def work():
        greet([peers.mate, peers.beside, peers.across], 3)
        loop(count, lambda i: mate_copy(i).start())

        def first(p):
            for k in range(2):
                i = 2 * p + k
                rows = tile_rows(i)
                mate_copy(i).wait_recv()
                total = mine[rows, :] + from_mate[rows, :].astype(F32)
                out[rows, :] = total
                summed[rows, :] = total.astype(BF)
                if k == 0:
                    detour(p).start()
                else:
                    direct(i).start()

        loop(pairs, first)
        if backward:
            gain_out[...] = jnp.zeros_like(gain_out)

        def second(i):
            rows = tile_rows(i)
            direct(i).wait_recv()
            total = out[rows, :] + from_chip[rows, :].astype(F32)
            if backward:
                change, terms = norm_back_tile(hidden[rows, :], gain[...], total)
                result = grad[rows, :].astype(F32) + change
                lower = result.astype(BF)
                ours = ((i * TILE) // per_chip) % 2 == peers.chip
                added = jnp.sum(terms, axis=0, keepdims=True)
                gain_out[...] += jnp.where(ours, added, jnp.zeros_like(added))
            else:
                result = residual[rows, :].astype(F32) + total
                lower = (result * rms_tile(result) * gain[...]).astype(BF)
            out[rows, :] = result
            low[rows, :] = lower
            low_copy(i).start()

        loop(count, second)

        def finish(i):
            mate_copy(i).wait_send()
            direct(i).wait_send()
            low_copy(i).wait()

        loop(count, finish)

    @pl.when(peers.section != active)
    def relay():
        greet([peers.corner], 1)

        def step(p):
            detour(p).wait_recv()
            back(p).start()

        loop(pairs, step)
        loop(pairs, lambda p: back(p).wait_send())


def sum_call(active, number, backward, per_chip, sent, mine, *rest):
    size, width = mine.shape
    count = size // TILE
    full = jax.ShapeDtypeStruct((size, width), F32)
    half = jax.ShapeDtypeStruct((size, width), BF)
    outs = (full, half, half)
    if backward:
        outs += (jax.ShapeDtypeStruct((1, width), F32),)
    scratch = [pltpu.VMEM((size, width), BF)] * 3 + [pltpu.VMEM((size // 2, width), BF)]
    sizes = [count, count, count, count, count // 2, count // 2, count, count]
    scratch += [pltpu.SemaphoreType.DMA((n,)) for n in sizes]
    return comm_call(
        functools.partial(sum_tiles, active, backward, per_chip),
        "sum_back" if backward else "sum_norm",
        number,
        (sent, mine) + rest,
        outs,
        scratch,
        [pl.ANY] + [pltpu.VMEM] * (1 + len(rest)),
    )


def spread_tiles(normed, peers, per_chip, gain, home, low, low_mate, sems, arrived, source):
    chip_s, chip_r, low_s, low_r = sems
    count = home.shape[0] // TILE
    half = count // 2

    def place(j, chip):
        return home_tile(j, chip, per_chip)

    def chip_copy(j):
        rows = tile_rows(place(j, peers.chip))
        return remote(source(j), home.at[rows], chip_s.at[j], chip_r.at[j], peers.beside)

    def chip_wait(j):
        rows = tile_rows(place(j, 1 - peers.chip))
        remote(source(j), home.at[rows], chip_s.at[j], chip_r.at[j], peers.beside).wait_recv()

    def low_copy(i, k):
        rows = tile_rows(i)
        return remote(low.at[rows], low_mate.at[rows], low_s.at[k], low_r.at[k], peers.mate)

    def lower(i, values):
        rows = tile_rows(i)
        wide = values.astype(F32)
        if normed == "all":
            wide = wide * rms_tile(wide) * gain[...]
        elif normed == "first":
            scale = rms_tile(wide)
            wide = wide * jnp.where(peers.section == 0, scale, jnp.ones_like(scale)) * gain[...]
        low[rows, :] = wide.astype(BF)

    def own(j):
        arrived(j)
        chip_copy(j).start()
        i = place(j, peers.chip)
        values = source(j)[...]
        home[tile_rows(i), :] = values
        lower(i, values)
        low_copy(i, j).start()

    loop(half, own)

    def other(j):
        chip_wait(j)
        i = place(j, 1 - peers.chip)
        lower(i, home[tile_rows(i), :])
        low_copy(i, half + j).start()

    loop(half, other)

    def finish(j):
        chip_copy(j).wait_send()
        low_copy(place(j, peers.chip), j).wait_send()
        low_copy(place(j, 1 - peers.chip), half + j).wait_send()
        low_copy(place(j, peers.chip), j).wait_recv()
        low_copy(place(j, 1 - peers.chip), half + j).wait_recv()

    loop(half, finish)


def start_tiles(per_chip, local, gain, home, low, low_mate, *sems):
    peers = Peers()
    greet([peers.mate, peers.beside], 2)
    spread_tiles(
        "first",
        peers,
        per_chip,
        gain,
        home,
        low,
        low_mate,
        sems,
        lambda j: None,
        lambda j: local.at[tile_rows(j)],
    )


def start_call(number, per_chip, local, gain):
    size, width = local.shape
    half = size // TILE
    out = jax.ShapeDtypeStruct((2 * size, width), BF)
    return comm_call(
        functools.partial(start_tiles, per_chip),
        "start",
        number,
        (local, gain),
        (out, out, out),
        [pltpu.SemaphoreType.DMA((n,)) for n in (half, half, 2 * half, 2 * half)],
        [pltpu.VMEM, pltpu.VMEM],
    )


def scatter_steps(peers, per_chip, sent, mine, from_mate, summed, kept, from_chip, sems, finished):
    mate_s, mate_r, chip_s, chip_r = sems
    count = mine.shape[0] // TILE
    half = count // 2

    def place(j, chip):
        return home_tile(j, chip, per_chip)

    def mate_copy(j, chip, k):
        rows = tile_rows(place(j, chip))
        return remote(sent.at[rows], from_mate.at[rows], mate_s.at[k], mate_r.at[k], peers.mate)

    def chip_copy(j):
        rows = tile_rows(j)
        return remote(summed.at[rows], from_chip.at[rows], chip_s.at[j], chip_r.at[j], peers.beside)

    loop(half, lambda j: mate_copy(j, 1 - peers.chip, j).start())
    loop(half, lambda j: mate_copy(j, peers.chip, half + j).start())

    def away(j):
        mate_copy(j, 1 - peers.chip, j).wait_recv()
        rows = tile_rows(place(j, 1 - peers.chip))
        total = mine[rows, :] + from_mate[rows, :].astype(F32)
        summed[tile_rows(j), :] = total.astype(BF)
        chip_copy(j).start()

    loop(half, away)

    def keep(j):
        mate_copy(j, peers.chip, half + j).wait_recv()
        rows = tile_rows(place(j, peers.chip))
        kept[tile_rows(j), :] = mine[rows, :] + from_mate[rows, :].astype(F32)

    loop(half, keep)

    def last(j):
        chip_copy(j).wait_recv()
        rows = tile_rows(j)
        finished(j, kept[rows, :] + from_chip[rows, :].astype(F32))

    loop(half, last)

    def finish(j):
        mate_copy(j, 1 - peers.chip, j).wait_send()
        mate_copy(j, peers.chip, half + j).wait_send()
        chip_copy(j).wait_send()

    loop(half, finish)


def end_tiles(per_chip, sent, mine, out, from_mate, summed, from_chip, *sems):
    peers = Peers()
    greet([peers.mate, peers.beside], 2)

    def finished(j, total):
        out[tile_rows(j), :] = total

    scatter_steps(peers, per_chip, sent, mine, from_mate, summed, out, from_chip, sems, finished)


def end_call(number, per_chip, sent, mine):
    size, width = mine.shape
    half = size // TILE // 2
    return comm_call(
        functools.partial(end_tiles, per_chip),
        "end",
        number,
        (sent, mine),
        (jax.ShapeDtypeStruct((size // 2, width), F32),),
        [pltpu.VMEM((size, width), BF)]
        + [pltpu.VMEM((size // 2, width), BF)] * 2
        + [pltpu.SemaphoreType.DMA((n,)) for n in (2 * half, 2 * half, half, half)],
        [pl.ANY, pltpu.VMEM],
    )[0]


def hop_tiles(source, backward, per_chip, *refs):
    if backward:
        sent, mine, values, grad, gain, next_gain, home, low, low_mate, result, gain_out = refs[:11]
        scratch = refs[11:]
    else:
        sent, mine, values, next_gain, home, low, low_mate, result = refs[:8]
        scratch = refs[8:]
    from_mate, summed, kept, from_chip, crossing, landed = scratch[:6]
    scatter_sems = scratch[6:10]
    spread_sems = scratch[10:14]
    cross_s, cross_r = scratch[14:]
    peers = Peers()
    half = result.shape[0] // TILE

    def cross_copy(j):
        rows = tile_rows(j)
        return remote(
            crossing.at[rows], landed.at[rows], cross_s.at[j], cross_r.at[j], peers.across
        )

    @pl.when(peers.section == source)
    def give():
        greet([peers.mate, peers.beside], 3)
        if backward:
            gain_out[...] = jnp.zeros_like(gain_out)

        def finished(j, total):
            rows = tile_rows(j)
            own = tile_rows(home_tile(j, peers.chip, per_chip))
            if backward:
                change, terms = norm_back_tile(values[own, :].astype(F32), gain[...], total)
                full = grad[own, :] + change
                gain_out[...] += jnp.sum(terms, axis=0, keepdims=True)
            else:
                full = values[own, :] + total
            result[rows, :] = full
            crossing[rows, :] = full.astype(BF)
            cross_copy(j).start()

        scatter_steps(
            peers,
            per_chip,
            sent,
            mine,
            from_mate,
            summed,
            kept,
            from_chip,
            scatter_sems,
            finished,
        )
        loop(half, lambda j: cross_copy(j).wait_send())

    @pl.when(peers.section != source)
    def take():
        greet([peers.mate, peers.beside, peers.across], 2)
        spread_tiles(
            None if backward else "all",
            peers,
            per_chip,
            next_gain,
            home,
            low,
            low_mate,
            spread_sems,
            lambda j: cross_copy(j).wait_recv(),
            lambda j: landed.at[tile_rows(j)],
        )


def hop_call(source, number, backward, per_chip, sent, mine, *rest):
    size, width = mine.shape
    half = size // TILE // 2
    out = jax.ShapeDtypeStruct((size, width), BF)
    outs = (out, out, out, jax.ShapeDtypeStruct((size // 2, width), F32))
    if backward:
        outs += (jax.ShapeDtypeStruct((1, width), F32),)
    scratch = [pltpu.VMEM((size, width), BF), pltpu.VMEM((size // 2, width), BF)]
    scratch += [pltpu.VMEM((size // 2, width), F32)] + [pltpu.VMEM((size // 2, width), BF)] * 3
    sizes = [2 * half, 2 * half, half, half, half, half, 2 * half, 2 * half, half, half]
    scratch += [pltpu.SemaphoreType.DMA((n,)) for n in sizes]
    return comm_call(
        functools.partial(hop_tiles, source, backward, per_chip),
        "hop_back" if backward else "hop",
        number,
        (sent, mine) + rest,
        outs,
        scratch,
        [pl.ANY] + [pltpu.VMEM] * (1 + len(rest)),
    )


def on_device(
    boundary,
    segments,
    norm_gains,
    qk_gains,
    conv_in,
    conv_kernel,
    conv_out,
    attn_query,
    attn_keyval,
    attn_out,
    ffn_gate_up,
    ffn_down,
):
    is_first = lax.axis_index("section") == 0
    place = lax.axis_index("tensor")
    tensor = lax.axis_size("tensor")
    dp = lax.axis_size("dp")
    core = place % 2
    chip = place // 2
    chips = tensor // 2
    steps = [1 << k for k in range(chips.bit_length() - 1)]
    local = boundary[0]
    rows, seq_local, width = local.shape
    seq = segments.shape[1]
    head_dim = qk_gains.shape[1]
    heads_here = attn_query.shape[1] // head_dim
    kv_here = attn_keyval.shape[2] // head_dim
    groups = heads_here // kv_here
    gains = norm_gains.astype(F32)
    head_gains = qk_gains.astype(F32)
    kernel = conv_kernel.astype(F32)
    hidden = ffn_down.shape[2]
    gate_up_w = ffn_gate_up[0].reshape(width, 2 * hidden)
    down_w = ffn_down[0]
    home = rows * chips * seq_local

    def mate(values, section):
        return permute(values, section, "tensor", lambda i: i ^ 1)

    def chip_gather(values, section):
        held = values[:, None]
        for step in steps:
            other = permute(held, section, "tensor", lambda i: i ^ (2 * step))
            upper = (chip // step) % 2 == 1
            held = jnp.where(
                upper,
                jnp.concatenate([other, held], axis=1),
                jnp.concatenate([held, other], axis=1),
            )
        return held

    def chip_sum(values, section):
        for step in steps:
            values = values + permute(
                values.astype(BF), section, "tensor", lambda i: i ^ (2 * step)
            ).astype(F32)
        return values

    def chip_scatter(values, section):
        for step in reversed(steps):
            halves = values.reshape((rows, 2, step) + values.shape[2:])
            upper = (chip // step) % 2
            kept = pick(halves, upper, 1)
            sent = pick(halves, 1 - upper, 1).astype(BF)
            values = kept + permute(sent, section, "tensor", lambda i: i ^ (2 * step)).astype(F32)
        return values[:, 0]

    def weave(mine, other):
        both = jnp.where(
            core == 0, jnp.stack([mine, other], axis=2), jnp.stack([other, mine], axis=2)
        )
        return both.reshape((rows, seq) + mine.shape[3:])

    def part(full, index):
        return pick(full.reshape((rows, chips, 2, seq_local) + full.shape[2:]), index, 2)

    def core_sum(mine, sent, section):
        return mine + mate(sent, section).astype(F32)

    def when(section, function, *args):
        shapes = jax.eval_shape(function, *args)
        zeros = lambda *unused: jax.tree.map(lambda s: jnp.zeros(s.shape, s.dtype), shapes)
        return lax.cond(is_first if section == 0 else ~is_first, function, zeros, *args)

    def conv_parts(project, masks_list):
        gate_in = project[:, :, 0] * project[:, :, 2]
        running = kernel[0] * gate_in
        for lag in range(1, kernel.shape[0]):
            running = running + kernel[lag] * delay_rows(gate_in, lag) * masks_list[lag - 1]
        return gate_in, running

    def outward(full_in, weight):
        mine = mm("rkte,ed->rktd", part(full_in, core), weight)
        sent = mm("rkte,ed->rktd", part(full_in, 1 - core), weight, BF)
        return mine, sent

    def conv_forward(mine, other):
        full = weave(mine, other)
        project = mm("rtd,dce->rtce", full, conv_in)
        unused, running = conv_parts(project, lag_masks(segments, kernel.shape[0]))
        mixed = (project[:, :, 1] * running).astype(BF)
        return outward(mixed, conv_out) + (project.astype(BF), mixed, full)

    def arrange(query, keyed, valued):
        q_all = query.reshape(rows, seq, kv_here, groups, head_dim).transpose(0, 2, 3, 1, 4)
        return (q_all, keyed.transpose(0, 2, 1, 3), valued.transpose(0, 2, 1, 3))

    def attn_forward(mine, other):
        full = weave(mine, other)
        query_raw = mm("rtd,de->rte", full, attn_query).reshape(rows, seq, heads_here, head_dim)
        keyval_raw = mm("rtd,dce->rtce", full, attn_keyval)
        key_raw = keyval_raw[:, :, 0].reshape(rows, seq, kv_here, head_dim)
        val_raw = keyval_raw[:, :, 1].reshape(rows, seq, kv_here, head_dim)
        cosine, sine = rope_tables(segments, head_dim // 2)
        query = head_prep(query_raw, head_gains[0], cosine, sine).astype(BF)
        keyed = head_prep(key_raw, head_gains[1], cosine, sine).astype(BF)
        q_all, k_all, v_all = arrange(query, keyed, val_raw.astype(BF))
        attended, logsum = lax.map(lambda item: attend_row(*item), (q_all, k_all, v_all, segments))
        flat = attended.transpose(0, 3, 1, 2, 4).reshape(rows, seq, heads_here * head_dim)
        saved = (query_raw, key_raw, q_all, k_all, v_all, logsum, flat, full)
        return outward(flat, attn_out) + saved

    def conv_backward(mine, other, project, mixed, full):
        grad_full = weave(mine, other)
        masks_list = lag_masks(segments, kernel.shape[0])
        project = project.astype(F32)
        gate_in, running = conv_parts(project, masks_list)
        grad_mixed = mm("rtd,ed->rte", grad_full, conv_out)
        grad_c = grad_mixed * running
        grad_run = grad_mixed * project[:, :, 1]
        grad_in = kernel[0] * grad_run
        grad_kernel = [jnp.sum(grad_run * gate_in, axis=(0, 1))]
        for lag in range(1, kernel.shape[0]):
            mask = masks_list[lag - 1]
            grad_in = grad_in + kernel[lag] * advance_rows(grad_run * mask, lag)
            grad_kernel.append(jnp.sum(grad_run * mask * delay_rows(gate_in, lag), axis=(0, 1)))
        grad_low = jnp.stack(
            [grad_in * project[:, :, 2], grad_c, grad_in * project[:, :, 0]], axis=2
        ).astype(BF)
        mine_in = mm("rktce,dce->rktd", part(grad_low, core), conv_in)
        sent_in = mm("rktce,dce->rktd", part(grad_low, 1 - core), conv_in, BF)
        grad_cout = mm("rte,rtd->ed", mixed, grad_full, BF)
        grad_cin = mm("rtd,rtce->dce", full, grad_low, BF)
        return mine_in, sent_in, (grad_cin, jnp.stack(grad_kernel).astype(BF), grad_cout)

    def attn_backward(mine, other, query_raw, key_raw, q_all, k_all, v_all, logsum, flat, full):
        grad_full = weave(mine, other)
        cosine, sine = rope_tables(segments, head_dim // 2)
        unused, query_pull = jax.vjp(
            lambda values, gain: head_prep(values, gain, cosine, sine), query_raw, head_gains[0]
        )
        unused, key_pull = jax.vjp(
            lambda values, gain: head_prep(values, gain, cosine, sine), key_raw, head_gains[1]
        )
        grad_flat = mm("rtd,ed->rte", grad_full, attn_out, BF)
        grad_heads = grad_flat.reshape(rows, seq, kv_here, groups, head_dim).transpose(
            0, 2, 3, 1, 4
        )
        grad_q, grad_k, grad_v = lax.map(
            lambda item: attend_back(*item), (q_all, k_all, v_all, segments, logsum, grad_heads)
        )
        grad_qraw, grad_qgain = query_pull(
            grad_q.transpose(0, 3, 1, 2, 4).reshape(rows, seq, heads_here, head_dim)
        )
        grad_kraw, grad_kgain = key_pull(grad_k.transpose(0, 2, 1, 3))
        query_low = grad_qraw.reshape(rows, seq, heads_here * head_dim).astype(BF)
        kv_low = jnp.stack(
            [
                grad_kraw.reshape(rows, seq, kv_here * head_dim),
                grad_v.transpose(0, 2, 1, 3).reshape(rows, seq, kv_here * head_dim),
            ],
            axis=2,
        ).astype(BF)

        def inward(index):
            return mm("rkte,de->rktd", part(query_low, index), attn_query) + mm(
                "rktce,dce->rktd", part(kv_low, index), attn_keyval
            )

        mine_in = inward(core)
        sent_in = inward(1 - core).astype(BF)
        grad_aout = mm("rte,rtd->ed", flat, grad_full, BF)
        grad_aq = mm("rtd,rte->de", full, query_low, BF)
        grad_akv = mm("rtd,rtce->dce", full, kv_low, BF)
        return (
            mine_in,
            sent_in,
            (grad_aq, grad_akv, grad_aout),
            jnp.stack([grad_qgain, grad_kgain]),
        )

    def flat_tokens(mine, other):
        return jnp.stack([mine, other]).reshape(2 * home, mine.shape[-1])

    def gate_up(both):
        return mm("td,df->tf", both, gate_up_w, BF)

    def activate(gu):
        gate = gu[:, :hidden].astype(F32)
        return (jax.nn.silu(gate) * gu[:, hidden:].astype(F32)).astype(BF)

    def shaped(tokens):
        return tokens.reshape(rows, chips, seq_local, width)

    def ffn_out(act):
        mine = mm("tf,df->td", act[:home], down_w)
        sent = mm("tf,df->td", act[home:], down_w, BF)
        return shaped(mine), shaped(sent)

    def ffn_back(grad_both, gu):
        grad_act = mm("td,df->tf", grad_both, down_w)
        gate = gu[:, :hidden].astype(F32)
        up = gu[:, hidden:].astype(F32)
        sig = jax.nn.sigmoid(gate)
        slope = sig * (1.0 + gate * (1.0 - sig))
        grad_gu = jnp.concatenate([grad_act * up * slope, grad_act * gate * sig], axis=1).astype(BF)
        mine = mm("tf,df->td", grad_gu[:home], gate_up_w)
        sent = mm("tf,df->td", grad_gu[home:], gate_up_w, BF)
        return grad_gu, shaped(mine), shaped(sent)

    def ffn_weights(both, gu, grad_both, grad_gu):
        act = activate(gu)
        grad_down = mm("td,tf->df", grad_both, act, BF)
        grad_up = mm("td,tf->df", both, grad_gu, BF)
        return grad_up, grad_down

    fused = chips == 2 and seq_local % TILE == 0
    home_shape = (rows, chips, seq_local, width)

    def tokens(values):
        return values.reshape(-1, width)

    def homed(values):
        return values.reshape(home_shape)

    def row(gain):
        return gain.reshape(1, width)

    def spread(own, section, lower):
        home_values = chip_gather(own, section)
        low = lower(home_values)
        return home_values, low, mate(low, section)

    def begin(gain):
        if fused:
            gain = jnp.where(is_first, gain, jnp.ones_like(gain))
            return map(homed, start_call(0, seq_local, tokens(local), row(gain)))
        first = spread(local, 0, lambda v: norm(v.astype(F32), gain))
        second = spread(local, 1, lambda v: v)
        return [jnp.where(is_first, one, two) for one, two in zip(first, second)]

    def sum_norm(section, number, mine, sent, residual, gain):
        if fused:
            outs = sum_call(
                section, number, False, seq_local, tokens(sent), tokens(mine), tokens(residual), row(gain)
            )
            return map(homed, outs)
        hidden_out = residual.astype(F32) + chip_sum(core_sum(mine, sent, section), section)
        low = norm(hidden_out, gain)
        return hidden_out, low, mate(low, section)

    def sum_back(section, number, mine, sent, hidden_in, grad, gain):
        if fused:
            *outs, terms = sum_call(
                section,
                number,
                True,
                seq_local,
                tokens(sent),
                tokens(mine),
                tokens(hidden_in),
                tokens(grad),
                row(gain),
            )
            return *map(homed, outs), terms[0]
        dz = chip_sum(core_sum(mine, sent, section), section)
        change, terms = norm_back(hidden_in, gain, dz)
        grad_in = grad.astype(F32) + change
        low = grad_in.astype(BF)
        return grad_in, low, mate(low, section), jnp.sum(pick(terms, chip, 1), axis=(0, 1))

    def hop(number, mine, sent, hidden_in, gain):
        if fused:
            *outs, result = hop_call(
                0, number, False, seq_local, tokens(sent), tokens(mine), tokens(hidden_in), row(gain)
            )
            return map(homed, outs)
        result = pick(hidden_in, chip, 1) + chip_scatter(core_sum(mine, sent, 0), 0)
        crossing = lax.ppermute(result.astype(BF), "section", [(0, 1)])
        return spread(crossing, 1, lambda v: norm(v.astype(F32), gain))

    def hop_back(number, mine, sent, values, grad, gain):
        if fused:
            *outs, result, terms = hop_call(
                1,
                number,
                True,
                seq_local,
                tokens(sent),
                tokens(mine),
                tokens(values),
                tokens(grad),
                row(gain),
                row(gain),
            )
            return *map(homed, outs), terms[0]
        dz = chip_scatter(core_sum(mine, sent, 1), 1)
        change, terms = norm_back(pick(values, chip, 1).astype(F32), gain, dz)
        result = pick(grad, chip, 1) + change
        crossing = lax.ppermute(result.astype(BF), "section", [(1, 0)])
        return *spread(crossing, 0, lambda v: v), jnp.sum(terms, axis=(0, 1))

    def end(number, mine, sent):
        if fused:
            out = end_call(number, seq_local, tokens(sent), tokens(mine))
            return out.reshape(rows, seq_local, width)
        return jnp.where(
            is_first,
            chip_scatter(core_sum(mine, sent, 0), 0),
            chip_scatter(core_sum(mine, sent, 1), 1),
        )

    start_home, start_low, start_mate = begin(gains[0, 0])
    cot_both = flat_tokens(start_home, start_mate)
    mine, sent, project, mixed, full1 = when(0, conv_forward, start_low, start_mate)
    h1, z_home, z_mate = sum_norm(0, 1, mine, sent, start_home, gains[0, 1])
    both1 = flat_tokens(z_home, z_mate)
    gu1 = gate_up(both1)
    mine, sent = ffn_out(activate(gu1))

    x2_home, z_home, z_mate = hop(2, mine, sent, h1, gains[1, 0])
    mine, sent, *saved = when(1, attn_forward, z_home, z_mate)
    h3, z_home, z_mate = sum_norm(1, 3, mine, sent, x2_home, gains[1, 1])
    both2 = flat_tokens(z_home, z_mate)
    gu2 = gate_up(both2)

    grad_gu2, mine, sent = ffn_back(cot_both, gu2)
    gh3, gm_home, gm_mate, gain_ffn2 = sum_back(1, 4, mine, sent, h3, start_home, gains[1, 1])
    mine, sent, attn_grads, head_grads = when(1, attn_backward, gm_home, gm_mate, *saved)
    g_home, unused, g_mate, gain_mix2 = hop_back(5, mine, sent, x2_home, gh3, gains[1, 0])

    g_both = flat_tokens(g_home, g_mate)
    grad_gu1, mine, sent = ffn_back(g_both, gu1)
    late = (both1, gu1, g_both, grad_gu1, both2, gu2, cot_both, grad_gu2)
    grad_up, grad_down = lax.cond(
        is_first, lambda *args: ffn_weights(*args[:4]), lambda *args: ffn_weights(*args[4:]), *late
    )
    full_gu = lax.psum(grad_up, "dp")
    full_down = lax.psum(grad_down, "dp")
    gh1, gm_home, gm_mate, gain_ffn1 = sum_back(0, 6, mine, sent, h1, g_home, gains[0, 1])

    def second_out(*args):
        shapes = jax.eval_shape(conv_backward, *args[:-1])
        zeros = jax.tree.map(lambda one: jnp.zeros(one.shape, one.dtype), shapes)
        return ffn_out(activate(args[-1])) + zeros[2:]

    mine, sent, conv_grads = lax.cond(
        is_first,
        lambda *args: conv_backward(*args[:-1]),
        second_out,
        gm_home,
        gm_mate,
        project,
        mixed,
        full1,
        gu2,
    )
    total = end(7, mine, sent)
    change, terms = norm_back(local.astype(F32), gains[0, 0], total)
    gain_mix1 = jnp.sum(terms, axis=(0, 1))
    boundary_out = jnp.where(is_first, pick(gh1, chip, 1) + change, pick(h3, chip, 1) + total)[None]

    mixer_sums = jax.tree.map(
        lambda v: v.astype(F32), lax.psum(conv_grads + attn_grads, ("section", "dp"))
    )
    zero = jnp.zeros_like(gain_mix1)
    first_gains = jnp.stack([jnp.stack([gain_mix1, gain_ffn1]), jnp.stack([zero, zero])])
    second_gains = jnp.stack([jnp.stack([zero, zero]), jnp.stack([gain_mix2, gain_ffn2])])
    grad_gains = jnp.where(is_first, first_gains, second_gains)
    grad_gains, grad_heads = lax.psum((grad_gains, head_grads), ("section", "tensor", "dp"))
    return (boundary_out, grad_gains, grad_heads) + mixer_sums + (
        full_gu.astype(F32).reshape(ffn_gate_up.shape),
        full_down.astype(F32)[None],
    )


def solution(mesh):
    placed = (
        P("section", "dp", "tensor", None),
        P("dp", None),
        P(),
        P(),
        P(None, None, "tensor"),
        P(None, "tensor"),
        P("tensor", None),
        P(None, "tensor"),
        P(None, None, "tensor"),
        P("tensor", None),
        P("section", None, None, "tensor"),
        P("section", None, "tensor"),
    )
    return jax.shard_map(
        on_device,
        mesh=mesh,
        in_specs=placed,
        out_specs=(
            P("section", "dp", "tensor", None),
            P(),
            P(),
            P(None, None, "tensor"),
            P(None, "tensor"),
            P("tensor", None),
            P(None, "tensor"),
            P(None, None, "tensor"),
            P("tensor", None),
            P("section", None, None, "tensor"),
            P("section", None, "tensor"),
        ),
        check_vma=False,
    )
```

```python
import functools

import jax
import jax.numpy as jnp
from jax import lax
from jax.experimental import pallas as pl
from jax.experimental.pallas import tpu as pltpu
from jax.sharding import PartitionSpec as P

EPSILON = 1e-05
THETA = 1000000.0
NEGATIVE = -1e30
BF = jnp.bfloat16
F32 = jnp.float32
MESH = pl.DeviceIdType.MESH
TILE = 64
VMEM_BYTES = 60 * 1024 * 1024


def mm(spec, left, right, kind=F32):
    return jnp.einsum(spec, left, right, preferred_element_type=F32).astype(kind)


def inverse_rms(values):
    return lax.rsqrt(jnp.mean(values * values, axis=-1, keepdims=True) + EPSILON)


def norm(values, gain):
    return (values * inverse_rms(values) * gain).astype(BF)


def norm_back(values, gain, grad):
    scale = inverse_rms(values)
    normed = values * scale
    weighted = grad * gain
    grad_in = scale * (weighted - normed * jnp.mean(weighted * normed, axis=-1, keepdims=True))
    return grad_in, grad * normed


def section_pairs(section, size, function):
    return [
        (section * size + i, section * size + function(i))
        for i in range(size)
        if 0 <= function(i) < size
    ]


def permute(values, section, axis, function):
    pairs = section_pairs(section, lax.axis_size(axis), function)
    return lax.ppermute(values, ("section", axis), pairs)


def pick(values, index, axis):
    return lax.dynamic_index_in_dim(values, index, axis, keepdims=False)


def delay_rows(values, lag):
    widths = ((0, 0), (lag, 0)) + ((0, 0),) * (values.ndim - 2)
    return jnp.pad(values, widths)[:, : values.shape[1]]


def advance_rows(values, lag):
    widths = ((0, 0), (0, lag)) + ((0, 0),) * (values.ndim - 2)
    return jnp.pad(values, widths)[:, lag:]


def lag_masks(seg_ids, kernel_len):
    masks_list = []
    for lag in range(1, kernel_len):
        shifted = jnp.pad(seg_ids, ((0, 0), (lag, 0)), constant_values=-1)[:, : seg_ids.shape[1]]
        masks_list.append((shifted == seg_ids).astype(F32)[..., None])
    return masks_list


def rope_tables(seg_ids, half_dim):
    starts = jnp.sum((seg_ids[:, None, :] < seg_ids[:, :, None]).astype(jnp.int32), axis=2)
    places = jnp.arange(seg_ids.shape[1], dtype=jnp.int32)[None, :] - starts
    freqs = jnp.power(THETA, -(2.0 * jnp.arange(half_dim, dtype=F32)) / (2.0 * half_dim))
    angles = places.astype(F32)[..., None] * freqs
    return (jnp.cos(angles), jnp.sin(angles))


class Peers:
    def __init__(self):
        self.section = lax.axis_index("section")
        place = lax.axis_index("tensor")
        self.core = place % 2
        self.chip = place // 2
        self.mate = {"tensor": place + 1 - 2 * self.core}
        self.beside = {"tensor": place + 2 - 4 * self.chip}
        self.across = {"section": 1 - self.section}
        self.corner = {"section": 1 - self.section, "tensor": place + 2 - 4 * self.chip}


def greet(signalled, count):
    barrier = pltpu.get_barrier_semaphore()
    for device in signalled:
        pl.semaphore_signal(barrier, inc=1, device_id=device, device_id_type=MESH)
    pl.semaphore_wait(barrier, count)


def remote(source, target, send, receive, device):
    return pltpu.make_async_remote_copy(
        src_ref=source,
        dst_ref=target,
        send_sem=send,
        recv_sem=receive,
        device_id=device,
        device_id_type=MESH,
    )


def loop(count, body):
    lax.fori_loop(0, count, lambda i, unused: (body(i), 0)[1], 0)


def tile_rows(index):
    return pl.ds(pl.multiple_of(index * TILE, TILE), TILE)


def home_tile(j, chip, per_chip):
    each = per_chip // TILE
    return ((j // each) * 2 + chip) * each + j % each


def rms_tile(values):
    return lax.rsqrt(jnp.mean(values * values, axis=-1, keepdims=True) + EPSILON)


def norm_back_tile(values, gain, grad):
    scale = rms_tile(values)
    normed = values * scale
    weighted = grad * gain
    inner = jnp.mean(weighted * normed, axis=-1, keepdims=True)
    return scale * (weighted - normed * inner), grad * normed


def comm_call(kernel, name, number, inputs, outs, scratch, where, micros=52):
    return pl.pallas_call(
        kernel,
        name=name,
        out_shape=outs,
        in_specs=[pl.BlockSpec(memory_space=space) for space in where],
        out_specs=tuple(pl.BlockSpec(memory_space=pltpu.VMEM) for unused in outs),
        scratch_shapes=scratch,
        cost_estimate=estimate(micros),
        compiler_params=pltpu.CompilerParams(
            collective_id=number, has_side_effects=True, vmem_limit_bytes=VMEM_BYTES
        ),
    )(*inputs)


def full_tile(i, core, per_chip):
    each = per_chip // TILE
    return ((i // each) * 2 + core) * each + i % each


def sum_tiles(active, backward, per_chip, *refs):
    if backward:
        part, hidden, grad, gain, out, full, gain_out = refs[:7]
        scratch = refs[7:]
    else:
        part, residual, gain, out, full, home_low = refs[:6]
        scratch = refs[6:]
    mine, from_mate, summed, from_chip, relayed = scratch[:5]
    own_s, mate_s, mate_r, chip_s, chip_r, relay_s, relay_r, low_s, low_r = scratch[5:]
    peers = Peers()
    count = mine.shape[0] // TILE
    pairs = count // 2

    def own_rows(i):
        return tile_rows(full_tile(i, peers.core, per_chip))

    def own_copy(i):
        return pltpu.make_async_copy(part.at[own_rows(i)], mine.at[tile_rows(i)], own_s.at[i])

    def mate_copy(i):
        theirs = tile_rows(full_tile(i, 1 - peers.core, per_chip))
        target = from_mate.at[tile_rows(i)]
        return remote(part.at[theirs], target, mate_s.at[i], mate_r.at[i], peers.mate)

    def direct(i):
        rows = tile_rows(i)
        return remote(summed.at[rows], from_chip.at[rows], chip_s.at[i], chip_r.at[i], peers.beside)

    def detour(p):
        return remote(
            summed.at[tile_rows(2 * p)],
            relayed.at[tile_rows(p)],
            chip_s.at[2 * p],
            relay_r.at[p],
            peers.corner,
        )

    def back(p):
        return remote(
            relayed.at[tile_rows(p)],
            from_chip.at[tile_rows(2 * p)],
            relay_s.at[p],
            chip_r.at[2 * p],
            peers.across,
        )

    def low_copy(i):
        rows = own_rows(i)
        return remote(full.at[rows], full.at[rows], low_s.at[i], low_r.at[i], peers.mate)

    def low_wait(i):
        rows = tile_rows(full_tile(i, 1 - peers.core, per_chip))
        remote(full.at[rows], full.at[rows], low_s.at[i], low_r.at[i], peers.mate).wait_recv()

    @pl.when(peers.section == active)
    def work():
        loop(count, lambda i: own_copy(i).start())
        greet([peers.mate, peers.beside, peers.across], 3)
        loop(count, lambda i: mate_copy(i).start())

        def first(p):
            for k in range(2):
                i = 2 * p + k
                rows = tile_rows(i)
                own_copy(i).wait()
                mate_copy(i).wait_recv()
                total = mine[rows, :].astype(F32) + from_mate[rows, :].astype(F32)
                out[rows, :] = total
                summed[rows, :] = total.astype(BF)
                if k == 0:
                    detour(p).start()
                else:
                    direct(i).start()

        loop(pairs, first)
        if backward:
            gain_out[...] = jnp.zeros_like(gain_out)

        def second(i):
            rows = tile_rows(i)
            direct(i).wait_recv()
            total = out[rows, :] + from_chip[rows, :].astype(F32)
            if backward:
                change, terms = norm_back_tile(hidden[rows, :], gain[...], total)
                result = grad[rows, :].astype(F32) + change
                lower = result.astype(BF)
                ours = ((i * TILE) // per_chip) % 2 == peers.chip
                added = jnp.sum(terms, axis=0, keepdims=True)
                gain_out[...] += jnp.where(ours, added, jnp.zeros_like(added))
            else:
                result = residual[rows, :].astype(F32) + total
                lower = (result * rms_tile(result) * gain[...]).astype(BF)
            out[rows, :] = result
            full[own_rows(i), :] = lower
            if not backward:
                home_low[rows, :] = lower
            low_copy(i).start()

        loop(count, second)

        def finish(i):
            mate_copy(i).wait_send()
            direct(i).wait_send()
            low_copy(i).wait_send()
            low_wait(i)

        loop(count, finish)

    @pl.when(peers.section != active)
    def relay():
        greet([peers.corner], 1)

        def step(p):
            detour(p).wait_recv()
            back(p).start()

        loop(pairs, step)
        if not backward:

            def keep(i):
                home_low[tile_rows(i), :] = residual[tile_rows(i), :].astype(BF)

            loop(count, keep)
        loop(pairs, lambda p: back(p).wait_send())


def sum_call(active, number, backward, per_chip, part, *rest):
    size, width = part.shape
    size //= 2
    count = size // TILE
    outs = (
        jax.ShapeDtypeStruct((size, width), F32),
        jax.ShapeDtypeStruct((2 * size, width), BF),
    )
    outs += (jax.ShapeDtypeStruct((1, width), F32) if backward else jax.ShapeDtypeStruct((size, width), BF),)
    scratch = [pltpu.VMEM((size, width), BF)] * 4 + [pltpu.VMEM((size // 2, width), BF)]
    sizes = [count, count, count, count, count, count // 2, count // 2, count, count]
    scratch += [pltpu.SemaphoreType.DMA((n,)) for n in sizes]
    return comm_call(
        functools.partial(sum_tiles, active, backward, per_chip),
        "sum_back" if backward else "sum_norm",
        number,
        (part,) + rest,
        outs,
        scratch,
        [pl.ANY] + [pltpu.VMEM] * len(rest),
    )


def spread_tiles(normed, peers, per_chip, gain, home, full, sems, arrived, source):
    chip_s, chip_r, low_s, low_r = sems
    half = home.shape[0] // TILE // 2

    def place(j, chip):
        return home_tile(j, chip, per_chip)

    def chip_copy(j):
        rows = tile_rows(place(j, peers.chip))
        return remote(source(j), home.at[rows], chip_s.at[j], chip_r.at[j], peers.beside)

    def chip_wait(j):
        rows = tile_rows(place(j, 1 - peers.chip))
        remote(source(j), home.at[rows], chip_s.at[j], chip_r.at[j], peers.beside).wait_recv()

    def low_copy(i, k, core):
        rows = tile_rows(full_tile(i, core, per_chip))
        return remote(full.at[rows], full.at[rows], low_s.at[k], low_r.at[k], peers.mate)

    def lower(i, values):
        wide = values.astype(F32)
        if normed == "all":
            wide = wide * rms_tile(wide) * gain[...]
        elif normed == "first":
            scale = rms_tile(wide)
            wide = wide * jnp.where(peers.section == 0, scale, jnp.ones_like(scale)) * gain[...]
        full[tile_rows(full_tile(i, peers.core, per_chip)), :] = wide.astype(BF)

    def own(j):
        arrived(j)
        chip_copy(j).start()
        i = place(j, peers.chip)
        values = source(j)[...]
        home[tile_rows(i), :] = values
        lower(i, values)
        low_copy(i, j, peers.core).start()

    loop(half, own)

    def other(j):
        chip_wait(j)
        i = place(j, 1 - peers.chip)
        lower(i, home[tile_rows(i), :])
        low_copy(i, half + j, peers.core).start()

    loop(half, other)

    def finish(j):
        chip_copy(j).wait_send()
        low_copy(place(j, peers.chip), j, peers.core).wait_send()
        low_copy(place(j, 1 - peers.chip), half + j, peers.core).wait_send()
        low_copy(place(j, peers.chip), j, 1 - peers.core).wait_recv()
        low_copy(place(j, 1 - peers.chip), half + j, 1 - peers.core).wait_recv()

    loop(half, finish)


def start_tiles(per_chip, local, gain, home, full, *sems):
    peers = Peers()
    greet([peers.mate, peers.beside], 2)
    spread_tiles(
        "first",
        peers,
        per_chip,
        gain,
        home,
        full,
        sems,
        lambda j: None,
        lambda j: local.at[tile_rows(j)],
    )


def start_call(number, per_chip, local, gain):
    size, width = local.shape
    half = size // TILE
    outs = (
        jax.ShapeDtypeStruct((2 * size, width), BF),
        jax.ShapeDtypeStruct((4 * size, width), BF),
    )
    return comm_call(
        functools.partial(start_tiles, per_chip),
        "start",
        number,
        (local, gain),
        outs,
        [pltpu.SemaphoreType.DMA((n,)) for n in (half, half, 2 * half, 2 * half)],
        [pltpu.VMEM, pltpu.VMEM],
    )


def scatter_steps(peers, per_chip, parts, mine, from_mate, summed, from_chip, sems, finished):
    own_s, mate_s, mate_r, chip_s, chip_r = sems
    half = mine.shape[0] // TILE // 2

    def rows_of(j, chip, core):
        return tile_rows(full_tile(home_tile(j, chip, per_chip), core, per_chip))

    def slot(j, k):
        return tile_rows(half * k + j)

    def chip_of(k):
        return 1 - peers.chip if k == 0 else peers.chip

    def own_copy(j, k, part=parts[0]):
        source = part.at[rows_of(j, chip_of(k), peers.core)]
        return pltpu.make_async_copy(source, mine.at[slot(j, k)], own_s.at[half * k + j])

    def mate_copy(j, k, part=parts[0]):
        source = part.at[rows_of(j, chip_of(k), 1 - peers.core)]
        index = half * k + j
        target = from_mate.at[slot(j, k)]
        return remote(source, target, mate_s.at[index], mate_r.at[index], peers.mate)

    def chip_copy(j):
        rows = tile_rows(j)
        return remote(summed.at[rows], from_chip.at[rows], chip_s.at[j], chip_r.at[j], peers.beside)

    def begin(part):
        for k in range(2):
            loop(half, lambda j: own_copy(j, k, part).start())
            loop(half, lambda j: mate_copy(j, k, part).start())

    if len(parts) == 1:
        begin(parts[0])
    else:
        for section, part in enumerate(parts):
            pl.when(peers.section == section)(functools.partial(begin, part))

    def both(j, k):
        own_copy(j, k).wait()
        mate_copy(j, k).wait_recv()
        return mine[slot(j, k), :].astype(F32) + from_mate[slot(j, k), :].astype(F32)

    def away(j):
        summed[tile_rows(j), :] = both(j, 0).astype(BF)
        chip_copy(j).start()

    loop(half, away)

    def last(j):
        total = both(j, 1)
        chip_copy(j).wait_recv()
        finished(j, total + from_chip[tile_rows(j), :].astype(F32))

    loop(half, last)

    def finish(j):
        mate_copy(j, 0).wait_send()
        mate_copy(j, 1).wait_send()
        chip_copy(j).wait_send()

    loop(half, finish)


def scatter_scratch(size, width):
    half = size // TILE // 2
    buffers = [pltpu.VMEM((size, width), BF)] * 2 + [pltpu.VMEM((size // 2, width), BF)] * 2
    counts = (2 * half, 2 * half, 2 * half, half, half)
    return buffers + [pltpu.SemaphoreType.DMA((n,)) for n in counts]


def end_tiles(per_chip, first, second, out, *scratch):
    peers = Peers()
    greet([peers.mate, peers.beside], 2)

    def finished(j, total):
        out[tile_rows(j), :] = total

    scatter_steps(peers, per_chip, (first, second), *scratch[:4], scratch[4:], finished)


def end_call(number, per_chip, first, second):
    size, width = first.shape
    size //= 2
    return comm_call(
        functools.partial(end_tiles, per_chip),
        "end",
        number,
        (first, second),
        (jax.ShapeDtypeStruct((size // 2, width), F32),),
        scatter_scratch(size, width),
        [pl.ANY, pl.ANY],
    )[0]


def hop_tiles(source, backward, per_chip, *refs):
    if backward:
        part, values, grad, gain, next_gain, home, full, gain_out = refs[:8]
        scratch = refs[8:]
    else:
        part, values, next_gain, home, full = refs[:5]
        scratch = refs[5:]
    crossing, landed, cross_s, cross_r = scratch[:4]
    spread_sems = scratch[4:8]
    buffers = scratch[8:12]
    scatter_sems = scratch[12:]
    peers = Peers()
    half = crossing.shape[0] // TILE

    def cross_copy(j):
        rows = tile_rows(j)
        return remote(
            crossing.at[rows], landed.at[rows], cross_s.at[j], cross_r.at[j], peers.across
        )

    @pl.when(peers.section == source)
    def give():
        greet([peers.mate, peers.beside], 3)
        if backward:
            gain_out[...] = jnp.zeros_like(gain_out)

        def finished(j, total):
            own = tile_rows(home_tile(j, peers.chip, per_chip))
            if backward:
                change, terms = norm_back_tile(values[own, :].astype(F32), gain[...], total)
                result = grad[own, :] + change
                gain_out[...] += jnp.sum(terms, axis=0, keepdims=True)
            else:
                result = values[own, :] + total
            crossing[tile_rows(j), :] = result.astype(BF)
            cross_copy(j).start()

        scatter_steps(peers, per_chip, (part,), *buffers, scatter_sems, finished)
        loop(half, lambda j: cross_copy(j).wait_send())

    @pl.when(peers.section != source)
    def take():
        greet([peers.mate, peers.beside, peers.across], 2)
        spread_tiles(
            None if backward else "all",
            peers,
            per_chip,
            next_gain,
            home,
            full,
            spread_sems,
            lambda j: cross_copy(j).wait_recv(),
            lambda j: landed.at[tile_rows(j)],
        )


def hop_call(source, number, backward, per_chip, part, *rest):
    size, width = part.shape
    size //= 2
    half = size // TILE // 2
    outs = (
        jax.ShapeDtypeStruct((size, width), BF),
        jax.ShapeDtypeStruct((2 * size, width), BF),
    )
    if backward:
        outs += (jax.ShapeDtypeStruct((1, width), F32),)
    scratch = [pltpu.VMEM((size // 2, width), BF)] * 2
    scratch += [pltpu.SemaphoreType.DMA((n,)) for n in (half, half, half, half, 2 * half, 2 * half)]
    return comm_call(
        functools.partial(hop_tiles, source, backward, per_chip),
        "hop_back" if backward else "hop",
        number,
        (part,) + rest,
        outs,
        scratch + scatter_scratch(size, width),
        [pl.ANY] + [pltpu.VMEM] * len(rest),
    )


def silu_parts(gu):
    lanes = gu.shape[1] // 2
    gate = gu[:, :lanes].astype(F32)
    up = gu[:, lanes:].astype(F32)
    return gate, up, 1.0 / (1.0 + jnp.exp(-gate))


def load_up(up_w, up_v, sems):
    hidden = up_w.shape[1]
    lanes = up_v.shape[0] // 2
    copies = [
        pltpu.make_async_copy(up_w.at[c], up_v.at[pl.ds(c * lanes, hidden)], sems.at[c])
        for c in range(2)
    ]
    for c, copy in enumerate(copies):
        copy.start()
        if lanes > hidden:
            up_v[c * lanes + hidden : (c + 1) * lanes, :] = jnp.zeros(
                (lanes - hidden, up_v.shape[1]), BF
            )
    return copies


def load_down(down_w, down_v, sems):
    hidden = down_w.shape[0]
    lanes = down_v.shape[0]
    copy = pltpu.make_async_copy(down_w, down_v.at[pl.ds(0, hidden)], sems.at[2])
    copy.start()
    if lanes > hidden:
        down_v[hidden:, :] = jnp.zeros((lanes - hidden, down_v.shape[1]), BF)
    return [copy]


def wait_all(copies):
    for copy in copies:
        copy.wait()


def only(active, run):
    if active is None:
        run()
    else:
        pl.when(lax.axis_index("section") == active)(run)


def stream(body, grid, inputs, outs):
    def spec(item):
        ref, rows, place = item
        return pl.BlockSpec((rows, ref.shape[1]), lambda *g: (place(*g), 0))

    pltpu.emit_pipeline(
        body,
        grid=grid,
        in_specs=[spec(item) for item in inputs],
        out_specs=[spec(item) for item in outs],
    )(*[item[0] for item in inputs + outs])


def gate_up_body(up_v):
    def body(z_t, gu_t):
        gu_t[...] = dot(z_t[...], up_v[...], (1, 1)).astype(BF)

    return body


def ffn_tiles(active, tile, with_down, *refs):
    if with_down:
        full, up_w, down_w, gu, part, up_v, down_v, sems = refs
    else:
        full, up_w, gu, up_v, sems = refs

    def run():
        copies = load_up(up_w, up_v, sems)
        if with_down:
            copies += load_down(down_w, down_v, sems)
        wait_all(copies)

        def body(z_t, gu_t, part_t):
            low = dot(z_t[...], up_v[...], (1, 1)).astype(BF)
            gu_t[...] = low
            gate, up, sig = silu_parts(low)
            act = (gate * sig * up).astype(BF)
            part_t[...] = dot(act, down_v[...], (1, 0)).astype(BF)

        here = lambda i: i
        grid = (full.shape[0] // tile,)
        if with_down:
            stream(body, grid, [(full, tile, here)], [(gu, tile, here), (part, tile, here)])
        else:
            stream(gate_up_body(up_v), grid, [(full, tile, here)], [(gu, tile, here)])

    only(active, run)


def down_tiles(active, tile, gu, down_w, *refs):
    part, down_v, sems = refs[-3:]

    def run():
        wait_all(load_down(down_w, down_v, sems))

        def body(gu_t, part_t):
            gate, up, sig = silu_parts(gu_t[...])
            part_t[...] = dot((gate * sig * up).astype(BF), down_v[...], (1, 0)).astype(BF)

        here = lambda i: i
        stream(body, (gu.shape[0] // tile,), [(gu, tile, here)], [(part, tile, here)])

    only(active, run)


def back_body(up_v, down_v):
    def body(g_t, gu_t, grad_t, act_t, *part_t):
        grad_act = dot(g_t[...], down_v[...], (1, 1))
        gate, up, sig = silu_parts(gu_t[...])
        silu = gate * sig
        act_t[...] = (silu * up).astype(BF)
        slope = sig + silu * (1.0 - sig)
        lanes = gate.shape[1]
        grad_t[:, :lanes] = (grad_act * up * slope).astype(BF)
        grad_t[:, lanes:] = (grad_act * silu).astype(BF)
        if part_t:
            part_t[0][...] = dot(grad_t[...], up_v[...], (1, 0)).astype(BF)

    return body


def ffn_back_tiles(active, tile, shards, *refs):
    grad, gu, up_w, down_w = refs[:4]
    up_v, down_v, sems = refs[-3:]
    outs = refs[-4 - (4 if shards > 1 else 2) : -3]

    def run():
        wait_all(load_up(up_w, up_v, sems) + load_down(down_w, down_v, sems))
        body = back_body(up_v, down_v)
        part = outs[-1]
        if shards == 1:
            here = lambda i: i
            items = [(out, tile, here) for out in outs]
            grid = (grad.shape[0] // tile,)
            stream(body, grid, [(grad, tile, here), (gu, tile, here)], items)
            return
        core = lax.axis_index("tensor") % 2
        spot = lax.axis_index("dp")
        count = grad.shape[0] // tile // 2
        for half in range(2):
            chosen = core if half == 0 else 1 - core
            here = lambda i: 2 * i + chosen
            there = lambda i: spot * count + i
            stream(
                body,
                (count,),
                [(grad, tile, here), (gu, tile, here)],
                [(outs[half], tile, there), (outs[2 + half], tile, there), (part, tile, here)],
            )

    only(active, run)


def others_up_tiles(active, tile, shards, source, up_w, *refs):
    out, up_v, sems = refs[-3:]

    def run():
        wait_all(load_up(up_w, up_v, sems))
        spot = lax.axis_index("dp")
        count = source.shape[0] // tile // shards
        place = lambda k, i: ((spot + 1 + k) % shards) * count + i
        items = [(source, tile, place)], [(out, tile, place)]
        stream(gate_up_body(up_v), (shards - 1, count), *items)

    only(active, run)


def others_back_tiles(tile, shards, first, second, down_w, gu, unused, grad_gu, act, down_v, sems):
    wait_all(load_down(down_w, down_v, sems))
    spot = lax.axis_index("dp")
    count = first.shape[0] // tile // shards
    place = lambda k, i: ((spot + 1 + k) % shards) * count + i

    def run(grad):
        stream(
            back_body(None, down_v),
            (shards - 1, count),
            [(grad, tile, place), (gu, tile, place)],
            [(grad_gu, tile, place), (act, tile, place)],
        )

    only(0, lambda: run(first))
    only(1, lambda: run(second))


def ffn_pallas(kernel, name, inputs, outs, weights, micros, aliases=None):
    return pl.pallas_call(
        kernel,
        name=name,
        out_shape=tuple(jax.ShapeDtypeStruct(shape, BF) for shape in outs),
        in_specs=[pl.BlockSpec(memory_space=pl.ANY)] * len(inputs),
        out_specs=tuple(pl.BlockSpec(memory_space=pl.ANY) for unused in outs),
        scratch_shapes=[pltpu.VMEM(shape, BF) for shape in weights]
        + [pltpu.SemaphoreType.DMA((3,))],
        input_output_aliases=aliases or {},
        cost_estimate=estimate(micros),
        compiler_params=pltpu.CompilerParams(vmem_limit_bytes=VMEM_BYTES),
    )(*inputs)


def estimate(micros):
    return pl.CostEstimate(flops=0, bytes_accessed=int(micros * 3.3e6), transcendentals=0)


def weight_shapes(up_w):
    lanes = padded(up_w.shape[1])
    return (2 * lanes, up_w.shape[2]), (lanes, up_w.shape[2])


def ffn_call(active, tile, full, up_w, down_w):
    up, down = weight_shapes(up_w)
    gu = (full.shape[0], up[0])
    if down_w is None:
        kernel = functools.partial(ffn_tiles, active, tile, False)
        return ffn_pallas(kernel, "gate_up", (full, up_w), (gu,), (up,), 30)[0]
    kernel = functools.partial(ffn_tiles, active, tile, True)
    return ffn_pallas(kernel, "ffn", (full, up_w, down_w), (gu, full.shape), (up, down), 44)


def down_call(active, tile, gu, down_w, *earlier):
    rows, lanes = gu.shape
    return ffn_pallas(
        functools.partial(down_tiles, active, tile),
        "down",
        (gu, down_w) + earlier,
        ((rows, down_w.shape[1]),),
        ((lanes // 2, down_w.shape[1]),),
        20,
    )[0]


def ffn_back_call(active, tile, shards, grad, gu, up_w, down_w, into=()):
    up, down = weight_shapes(up_w)
    if shards == 1:
        outs = ((grad.shape[0], up[0]), (grad.shape[0], down[0]))
    else:
        rows = grad.shape[0] // 2 * shards
        outs = ((rows, up[0]),) * 2 + ((rows, down[0]),) * 2
    return ffn_pallas(
        functools.partial(ffn_back_tiles, active, tile, shards),
        "ffn_back",
        (grad, gu, up_w, down_w) + tuple(into),
        outs + (grad.shape,),
        (up, down),
        48,
        {4 + i: i for i in range(len(into))},
    )


def others_up_call(active, tile, shards, source, up_w, into, *earlier):
    return ffn_pallas(
        functools.partial(others_up_tiles, active, tile, shards),
        "others_up",
        (source, up_w, into) + earlier,
        (into.shape,),
        (weight_shapes(up_w)[0],),
        42,
        {2: 0},
    )[0]


def others_back_call(tile, shards, first, second, down_w, gu, act):
    return ffn_pallas(
        functools.partial(others_back_tiles, tile, shards),
        "others_back",
        (first, second, down_w, gu, act),
        (gu.shape, act.shape),
        ((act.shape[1], down_w.shape[1]),),
        32,
        {3: 0, 4: 1},
    )


def hold_call(values, *others):
    if not others:
        return values
    return pl.pallas_call(
        lambda *refs: None,
        name="hold",
        out_shape=jax.ShapeDtypeStruct(values.shape, values.dtype),
        in_specs=[pl.BlockSpec(memory_space=pl.ANY)] * (1 + len(others)),
        out_specs=pl.BlockSpec(memory_space=pl.ANY),
        input_output_aliases={0: 0},
        cost_estimate=estimate(1),
        compiler_params=pltpu.CompilerParams(has_side_effects=True),
    )(values, *others)


def total_tiles(values, out, held, landed, sends, receives):
    peers = Peers()
    spot = lax.axis_index("dp")
    partners = [
        peers.mate,
        peers.beside,
        peers.across,
        {"dp": spot + 1 - 2 * (spot % 2)},
        {"dp": spot + 2 - 4 * (spot // 2)},
    ]
    greet(partners, len(partners))
    held[0] = values[...]
    for i, partner in enumerate(partners):
        copy = remote(held.at[i], landed.at[i], sends.at[i], receives.at[i], partner)
        copy.start()
        copy.wait()
        held[i + 1] = held[i] + landed[i]
    out[...] = held[len(partners)]


def total_call(number, values):
    count = 5
    return comm_call(
        total_tiles,
        "total",
        number,
        (values,),
        (jax.ShapeDtypeStruct(values.shape, F32),),
        [
            pltpu.VMEM((count + 1,) + values.shape, F32),
            pltpu.VMEM((count,) + values.shape, F32),
            pltpu.SemaphoreType.DMA((count,)),
            pltpu.SemaphoreType.DMA((count,)),
        ],
        [pltpu.VMEM],
    )[0]


def rotated(values):
    half = values.shape[-1] // 2
    return jnp.concatenate([-values[:, half:], values[:, :half]], axis=-1)


def dot(left, right, dims):
    return lax.dot_general(left, right, ((dims[:1], dims[1:]), ((), ())), preferred_element_type=F32)


def attend_tiles(groups, size, block, raw, cosine, sine, seg_col, seg_row, gains, out, probs, totals, turned, heads):
    length = raw.shape[1]
    cos_t = cosine[0]
    sin_t = sine[0]
    scaling = size ** (-0.5)

    def prepared(values, gain):
        normed = values * rms_tile(values) * gain
        return normed * cos_t + rotated(normed) * sin_t

    for g in range(groups):
        lanes = slice(g * size, (g + 1) * size)
        query = (prepared(raw[0, :, lanes], gains[0:1, :]).astype(BF) * scaling).astype(BF)
        heads[g] = query
        turned[0, :, lanes] = query
    lanes = slice(groups * size, (groups + 1) * size)
    keyed = prepared(raw[0, :, lanes], gains[1:2, :]).astype(BF)
    turned[0, :, lanes] = keyed
    lanes = slice((groups + 1) * size, (groups + 2) * size)
    valued = raw[0, :, lanes].astype(BF)
    turned[0, :, lanes] = valued
    ones = (lax.broadcasted_iota(jnp.int32, (length, size), 1) == 0).astype(BF)
    widened = jnp.concatenate([valued, ones], axis=1)
    used = (groups + 2) * size
    if used < turned.shape[2]:
        turned[0, :, used:] = jnp.zeros((length, turned.shape[2] - used), BF)
    for i in range(length // block):
        rows = slice(i * block, (i + 1) * block)
        span = (i + 1) * block
        query_pos = i * block + lax.broadcasted_iota(jnp.int32, (block, span), 0)
        key_pos = lax.broadcasted_iota(jnp.int32, (block, span), 1)
        allowed = (key_pos <= query_pos) & (seg_col[0, rows, :] == seg_row[0, :, :span])

        def head(g):
            scores = dot(heads[g, rows, :], keyed[:span], (1, 1))
            expon = jnp.exp(jnp.where(allowed, scores, NEGATIVE)).astype(BF)
            probs[0, 0, g, rows, :span] = expon
            summed = dot(expon, widened[:span], (1, 0))
            total = summed[:, size : size + 1]
            totals[0, 0, g, rows, :] = total
            heads[g, rows, :] = (summed[:, :size] * (1.0 / total)).astype(BF)

        for g in range(groups):
            head(g)
    for g in range(groups):
        out[0, :, g * size : (g + 1) * size] = heads[g]
    if groups * size < out.shape[2]:
        out[0, :, groups * size :] = jnp.zeros((length, out.shape[2] - groups * size), BF)


def attend_back_tiles(
    groups, size, block, raw, turned, probs, totals, out, grad_out, cosine, sine, gains, grad_raw, grad_gains, heads, grads, inner, query_grad, key_grad, val_grad
):
    length = raw.shape[1]
    cos_t = cosine[0]
    sin_t = sine[0]
    scaling = size ** (-0.5)

    @pl.when((pl.program_id(0) == 0) & (pl.program_id(1) == 0))
    def clear():
        grad_gains[...] = jnp.zeros_like(grad_gains)

    blocks = length // block
    for g in range(groups):
        lanes = slice(g * size, (g + 1) * size)
        shared = (grad_out[0, :, lanes].astype(F32) * (1.0 / totals[0, 0, g])).astype(BF)
        mean = jnp.sum(shared.astype(F32) * out[0, :, lanes].astype(F32), axis=-1, keepdims=True)
        for i in range(blocks):
            rows = slice(i * block, (i + 1) * block)
            into = slice(g * block, (g + 1) * block)
            heads[i, into, :] = turned[0, rows, lanes]
            grads[i, into, :] = shared[rows]
            inner[i, into, :] = mean[rows]
    keyed = turned[0, :, groups * size : (groups + 1) * size]
    valued = turned[0, :, (groups + 1) * size : (groups + 2) * size]
    key_grad[...] = jnp.zeros_like(key_grad)
    val_grad[...] = jnp.zeros_like(val_grad)
    for i in range(blocks):
        rows = slice(i * block, (i + 1) * block)
        span = (i + 1) * block
        low = jnp.concatenate([probs[0, 0, g, rows, :span] for g in range(groups)], axis=0)
        grad_probs = dot(grads[i], valued[:span], (1, 1))
        grad_scores = (low.astype(F32) * (grad_probs - inner[i])).astype(BF)
        back_q = dot(grad_scores, keyed[:span], (1, 0)) * scaling
        for g in range(groups):
            query_grad[g, rows, :] = back_q[g * block : (g + 1) * block]
        key_grad[:, :span] += dot(heads[i], grad_scores, (0, 0))
        val_grad[:, :span] += dot(grads[i], low, (0, 0))

    def back(values, gain, grad, which):
        grad = grad * cos_t - rotated(grad) * sin_t
        change, terms = norm_back_tile(values, gain, grad)
        grad_gains[which : which + 1, :] += jnp.sum(terms, axis=0, keepdims=True)
        return change.astype(BF)

    for g in range(groups):
        lanes = slice(g * size, (g + 1) * size)
        grad_raw[0, :, lanes] = back(raw[0, :, lanes], gains[0:1, :], query_grad[g], 0)
    lanes = slice(groups * size, (groups + 1) * size)
    grad_raw[0, :, lanes] = back(raw[0, :, lanes], gains[1:2, :], key_grad[...].T, 1)
    lanes = slice((groups + 1) * size, (groups + 2) * size)
    grad_raw[0, :, lanes] = val_grad[...].T.astype(BF)
    used = (groups + 2) * size
    if used < grad_raw.shape[2]:
        grad_raw[0, :, used:] = jnp.zeros((length, grad_raw.shape[2] - used), BF)


def attend_call(groups, size, kv_heads, raw, cosine, sine, segments, gains):
    rows, length, lanes = raw.shape
    lanes //= kv_heads
    out_lanes = padded(groups * size)
    block = min(256, length)
    whole = lambda r, k: (r, 0, 0)
    part = lambda r, k: (r, 0, k)
    return pl.pallas_call(
        functools.partial(attend_tiles, groups, size, block),
        name="attend",
        grid=(rows, kv_heads),
        in_specs=[
            pl.BlockSpec((1, length, lanes), part),
            pl.BlockSpec((1, length, size), whole),
            pl.BlockSpec((1, length, size), whole),
            pl.BlockSpec((1, length, 1), whole),
            pl.BlockSpec((1, 1, length), whole),
            pl.BlockSpec((2, size), lambda r, k: (0, 0)),
        ],
        out_specs=(
            pl.BlockSpec((1, length, out_lanes), part),
            pl.BlockSpec((1, 1, groups, length, length), lambda r, k: (r, k, 0, 0, 0)),
            pl.BlockSpec((1, 1, groups, length, 1), lambda r, k: (r, k, 0, 0, 0)),
            pl.BlockSpec((1, length, lanes), part),
        ),
        out_shape=(
            jax.ShapeDtypeStruct((rows, length, kv_heads * out_lanes), BF),
            jax.ShapeDtypeStruct((rows, kv_heads, groups, length, length), BF),
            jax.ShapeDtypeStruct((rows, kv_heads, groups, length, 1), F32),
            jax.ShapeDtypeStruct((rows, length, kv_heads * lanes), BF),
        ),
        scratch_shapes=[pltpu.VMEM((groups, length, size), BF)],
        cost_estimate=estimate(27),
        compiler_params=pltpu.CompilerParams(vmem_limit_bytes=VMEM_BYTES),
    )(raw, cosine, sine, segments[:, :, None], segments[:, None, :], gains)


def attend_back_call(groups, size, kv_heads, raw, turned, probs, totals, out, grad_out, cosine, sine, gains):
    rows, length, lanes = raw.shape
    lanes //= kv_heads
    out_lanes = padded(groups * size)
    block = min(256, length)
    whole = lambda r, k: (r, 0, 0)
    part = lambda r, k: (r, 0, k)
    fixed = lambda r, k: (0, 0)
    return pl.pallas_call(
        functools.partial(attend_back_tiles, groups, size, block),
        name="attend_back",
        grid=(rows, kv_heads),
        in_specs=[
            pl.BlockSpec((1, length, lanes), part),
            pl.BlockSpec((1, length, lanes), part),
            pl.BlockSpec((1, 1, groups, length, length), lambda r, k: (r, k, 0, 0, 0)),
            pl.BlockSpec((1, 1, groups, length, 1), lambda r, k: (r, k, 0, 0, 0)),
            pl.BlockSpec((1, length, out_lanes), part),
            pl.BlockSpec((1, length, out_lanes), part),
            pl.BlockSpec((1, length, size), whole),
            pl.BlockSpec((1, length, size), whole),
            pl.BlockSpec((2, size), fixed),
        ],
        out_specs=(
            pl.BlockSpec((1, length, lanes), part),
            pl.BlockSpec((2, size), fixed),
        ),
        out_shape=(
            jax.ShapeDtypeStruct((rows, length, kv_heads * lanes), BF),
            jax.ShapeDtypeStruct((2, size), F32),
        ),
        scratch_shapes=[
            pltpu.VMEM((length // block, groups * block, size), BF),
            pltpu.VMEM((length // block, groups * block, size), BF),
            pltpu.VMEM((length // block, groups * block, 1), F32),
            pltpu.VMEM((groups, length, size), F32),
            pltpu.VMEM((size, length), F32),
            pltpu.VMEM((size, length), F32),
        ],
        cost_estimate=estimate(43),
        compiler_params=pltpu.CompilerParams(vmem_limit_bytes=VMEM_BYTES),
    )(raw, turned, probs, totals, out, grad_out, cosine, sine, gains)


def padded(lanes):
    return (lanes + 127) // 128 * 128


def on_device(
    boundary,
    segments,
    norm_gains,
    qk_gains,
    conv_in,
    conv_kernel,
    conv_out,
    attn_query,
    attn_keyval,
    attn_out,
    ffn_gate_up,
    ffn_down,
):
    is_first = lax.axis_index("section") == 0
    place = lax.axis_index("tensor")
    chips = lax.axis_size("tensor") // 2
    core = place % 2
    chip = place // 2
    steps = [1 << k for k in range(chips.bit_length() - 1)]
    local = boundary[0]
    rows, seq_local, width = local.shape
    seq = segments.shape[1]
    head_dim = qk_gains.shape[1]
    kv_here = attn_keyval.shape[2] // head_dim
    groups = attn_query.shape[1] // head_dim // kv_here
    hidden = ffn_down.shape[2]
    dp = lax.axis_size("dp")
    channels = conv_out.shape[0]
    gains = norm_gains.astype(F32)
    head_gains = qk_gains.astype(F32)
    kernel = conv_kernel.astype(F32)
    up_w = ffn_gate_up[0].transpose(1, 2, 0)
    down_w = ffn_down[0].T
    conv_in_w = conv_in.reshape(width, 3 * channels)
    home_shape = (rows, chips, seq_local, width)
    fused = chips == 2 and dp == 4 and seq_local % TILE == 0

    def mate(values, section):
        return permute(values, section, "tensor", lambda i: i ^ 1)

    def chip_gather(values, section):
        held = values[:, None]
        for step in steps:
            other = permute(held, section, "tensor", lambda i: i ^ (2 * step))
            upper = (chip // step) % 2 == 1
            held = jnp.where(
                upper,
                jnp.concatenate([other, held], axis=1),
                jnp.concatenate([held, other], axis=1),
            )
        return held

    def chip_sum(values, section):
        for step in steps:
            values = values + permute(
                values.astype(BF), section, "tensor", lambda i: i ^ (2 * step)
            ).astype(F32)
        return values

    def chip_scatter(values, section):
        for step in reversed(steps):
            halves = values.reshape((rows, 2, step) + values.shape[2:])
            upper = (chip // step) % 2
            kept = pick(halves, upper, 1)
            sent = pick(halves, 1 - upper, 1).astype(BF)
            values = kept + permute(sent, section, "tensor", lambda i: i ^ (2 * step)).astype(F32)
        return values[:, 0]

    def share(mine, section):
        other = mate(mine, section)
        both = jnp.where(
            core == 0, jnp.stack([mine, other], axis=2), jnp.stack([other, mine], axis=2)
        )
        return both.reshape(rows * seq, width)

    def core_sum(part, section):
        parts = part.reshape(rows, chips, 2, seq_local, width)
        return pick(parts, core, 2).astype(F32) + mate(pick(parts, 1 - core, 2), section).astype(F32)

    def tokens(values):
        return values.reshape(-1, width)

    def homed(values):
        return values.reshape(home_shape)

    def row(gain):
        return gain.reshape(1, width)

    def begin(gain):
        if fused:
            gain = jnp.where(is_first, gain, jnp.ones_like(gain))
            home, full = start_call(0, seq_local, tokens(local), row(gain))
            return homed(home), full
        first = chip_gather(local, 0)
        second = chip_gather(local, 1)
        return (
            jnp.where(is_first, first, second),
            jnp.where(is_first, share(norm(first.astype(F32), gain), 0), share(second, 1)),
        )

    def sum_norm(section, number, part, residual, gain):
        if fused:
            out, full, low = sum_call(
                section, number, False, seq_local, part, tokens(residual), row(gain)
            )
            return homed(out), full, low
        out = residual.astype(F32) + chip_sum(core_sum(part, section), section)
        return out, share(norm(out, gain), section), None

    def sum_back(section, number, part, hidden_in, grad, gain):
        if fused:
            out, full, terms = sum_call(
                section,
                number,
                True,
                seq_local,
                part,
                tokens(hidden_in),
                tokens(grad),
                row(gain),
            )
            return homed(out), full, terms[0]
        dz = chip_sum(core_sum(part, section), section)
        change, terms = norm_back(hidden_in, gain, dz)
        out = grad.astype(F32) + change
        return out, share(out.astype(BF), section), jnp.sum(pick(terms, chip, 1), axis=(0, 1))

    def hop(number, part, hidden_in, gain):
        if fused:
            home, full = hop_call(
                0, number, False, seq_local, part, tokens(hidden_in), row(gain)
            )
            return homed(home), full
        result = pick(hidden_in, chip, 1) + chip_scatter(core_sum(part, 0), 0)
        home = chip_gather(lax.ppermute(result.astype(BF), "section", [(0, 1)]), 1)
        return home, share(norm(home.astype(F32), gain), 1)

    def hop_back(number, part, values, grad, gain):
        if fused:
            home, full, terms = hop_call(
                1,
                number,
                True,
                seq_local,
                part,
                tokens(values),
                tokens(grad),
                row(gain),
                row(gain),
            )
            return homed(home), full, terms[0]
        dz = chip_scatter(core_sum(part, 1), 1)
        change, terms = norm_back(pick(values, chip, 1).astype(F32), gain, dz)
        result = pick(grad, chip, 1) + change
        home = chip_gather(lax.ppermute(result.astype(BF), "section", [(1, 0)]), 0)
        return home, share(home, 0), jnp.sum(terms, axis=(0, 1))

    def end(number, first, second):
        if fused:
            return end_call(number, seq_local, first, second).reshape(rows, seq_local, width)
        return jnp.where(
            is_first,
            chip_scatter(core_sum(first, 0), 0),
            chip_scatter(core_sum(second, 1), 1),
        )

    def either(first, first_args, second, second_args):
        def zeros(function, args):
            shapes = jax.eval_shape(function, *args)
            return jax.tree.map(lambda one: jnp.zeros(one.shape, one.dtype), shapes)

        return lax.cond(
            is_first,
            lambda one, two: (first(*one), zeros(second, two)),
            lambda one, two: (zeros(first, one), second(*two)),
            first_args,
            second_args,
        )

    def nothing():
        return ()

    def by_row(values):
        return values.reshape(rows, seq, values.shape[-1])

    def conv_parts(project, masks_list):
        gate_in = project[..., :channels] * project[..., 2 * channels :]
        running = kernel[0] * gate_in
        for lag in range(1, kernel.shape[0]):
            running = running + kernel[lag] * delay_rows(gate_in, lag) * masks_list[lag - 1]
        return gate_in, running

    def conv_forward(full):
        project = by_row(mm("td,de->te", full, conv_in_w))
        unused, running = conv_parts(project, lag_masks(segments, kernel.shape[0]))
        mixed = (project[..., channels : 2 * channels] * running).astype(BF).reshape(-1, channels)
        return mm("te,ed->td", mixed, conv_out, BF), project.astype(BF), mixed

    def conv_backward(grad_full, project, mixed, full):
        masks_list = lag_masks(segments, kernel.shape[0])
        project = project.astype(F32)
        gate_in, running = conv_parts(project, masks_list)
        grad_mixed = by_row(mm("td,ed->te", grad_full, conv_out))
        grad_c = grad_mixed * running
        grad_run = grad_mixed * project[..., channels : 2 * channels]
        grad_in = kernel[0] * grad_run
        grad_kernel = [jnp.sum(grad_run * gate_in, axis=(0, 1))]
        for lag in range(1, kernel.shape[0]):
            mask = masks_list[lag - 1]
            grad_in = grad_in + kernel[lag] * advance_rows(grad_run * mask, lag)
            grad_kernel.append(jnp.sum(grad_run * mask * delay_rows(gate_in, lag), axis=(0, 1)))
        grad_low = jnp.concatenate(
            [grad_in * project[..., 2 * channels :], grad_c, grad_in * project[..., :channels]],
            axis=-1,
        )
        grad_low = grad_low.astype(BF).reshape(-1, 3 * channels)
        part = mm("te,de->td", grad_low, conv_in_w, BF)
        grad_cout = mm("te,td->ed", mixed, grad_full, BF)
        grad_cin = mm("td,te->de", full, grad_low, BF)
        taps = jnp.stack(grad_kernel).astype(BF)
        each = [grad_cin[:, i * channels : (i + 1) * channels] for i in range(3)]
        grad_cout = jnp.concatenate([grad_cout, jnp.pad(taps, ((0, 16 - taps.shape[0]), (0, width - channels)))])
        return part, each + [grad_cout]

    def by_kv(values, axis):
        shape = values.shape[:axis] + (kv_here, -1) + values.shape[axis + 1 :]
        return values.reshape(shape)

    def attn_setup():
        keyval = [by_kv(attn_keyval[:, i], 1) for i in range(2)]
        into = jnp.concatenate([by_kv(attn_query, 1)] + keyval, axis=2)
        used = into.shape[2]
        into = jnp.pad(into, ((0, 0), (0, 0), (0, padded(used) - used)))
        out = by_kv(attn_out, 0)
        used = out.shape[1]
        out = jnp.pad(out, ((0, 0), (0, padded(used) - used), (0, 0)))
        cosine, sine = rope_tables(segments, head_dim // 2)
        twice = lambda table: jnp.concatenate([table, table], axis=-1)
        return into.reshape(width, -1), out.reshape(-1, width), twice(cosine), twice(sine)

    def attn_forward(full, into, outof, cosine, sine):
        raw = by_row(mm("td,de->te", full, into))
        out, probs, totals, turned = attend_call(
            groups, head_dim, kv_here, raw, cosine, sine, segments, head_gains
        )
        flat = out.reshape(rows * seq, -1)
        return mm("te,ed->td", flat, outof, BF), raw, turned, probs, totals, out

    def attn_backward(grad_full, raw, turned, probs, totals, out, into, outof, cosine, sine):
        grad_out = by_row(mm("td,ed->te", grad_full, outof, BF))
        grad_raw, grad_gains = attend_back_call(
            groups,
            head_dim,
            kv_here,
            raw,
            turned,
            probs,
            totals,
            out,
            grad_out,
            cosine,
            sine,
            head_gains,
        )
        grad_raw = grad_raw.reshape(rows * seq, -1)
        return mm("te,de->td", grad_raw, into, BF), grad_raw, grad_gains

    def attn_weights(full, grad_raw, out, grad_full):
        grad_into = by_kv(mm("td,te->de", full, grad_raw, BF), 1)
        grad_out = by_kv(mm("te,td->ed", out.reshape(rows * seq, -1), grad_full, BF), 0)
        cut = groups * head_dim
        grad_keyval = [
            grad_into[:, :, cut + i * head_dim : cut + (i + 1) * head_dim].reshape(width, -1)
            for i in range(2)
        ]
        return (
            grad_into[:, :, :cut].reshape(attn_query.shape),
            jnp.stack(grad_keyval, axis=1),
            grad_out[:, :cut].reshape(attn_out.shape),
        )

    shards = dp if fused else 1

    def weights(full, grad_gu, grad_full, act):
        grad_up = sum(mm("tf,td->fd", one, two) for one, two in zip(grad_gu, full))
        grad_down = sum(mm("tf,td->fd", one, two) for one, two in zip(act, grad_full))
        return grad_up.reshape(2, -1, width)[:, :hidden], grad_down[:hidden]

    def choose(function, first_args, second_args):
        return lax.cond(
            is_first,
            lambda one, two: function(*one),
            lambda one, two: function(*two),
            first_args,
            second_args,
        )

    def gather_shards(home_tokens):
        return lax.all_gather(home_tokens, "dp", axis=0, tiled=True)

    def with_mate(mine, sections, *others):
        size = lax.axis_size("tensor")
        pairs = [p for one in sections for p in section_pairs(one, size, lambda i: i ^ 1)]
        mine = hold_call(mine, *others)
        return mine, lax.ppermute(mine, ("section", "tensor"), pairs)

    def after(values, *others):
        return lax.optimization_barrier((values, others))[0]

    start_home, start_full = begin(gains[0, 0])
    (part, project, mixed), setup = either(conv_forward, (start_full,), attn_setup, ())
    h1, full1, low1 = sum_norm(0, 1, part, start_home, gains[0, 1])
    if fused:
        all_a = gather_shards(low1)
    gu1, part = ffn_call(0, seq_local, full1, up_w, down_w)

    x2_home, z3 = hop(2, part, h1, gains[1, 0])
    unused, (part, *saved) = either(nothing, (), attn_forward, (z3,) + setup)
    h3, full2, low2 = sum_norm(1, 3, part, x2_home, gains[1, 1])
    if fused:
        all_b = gather_shards(low2)
    gu2 = ffn_call(1, seq_local, full2, up_w, None)

    *kept2, part = ffn_back_call(1, seq_local, shards, start_full, gu2, up_w, down_w)
    if fused:
        all_a = with_mate(all_a, (0, 1), gu2)
        kept2[0] = others_up_call(0, seq_local, dp, all_a[0], up_w, kept2[0])
        part = hold_call(part, kept2[0])
    gh3, gm3, gain_ffn2 = sum_back(1, 4, part, h3, start_home, gains[1, 1])
    if fused:
        kept2[1] = others_up_call(0, seq_local, dp, all_a[1], up_w, kept2[1], gm3)
        gm3 = hold_call(gm3, kept2[1])
    unused, (part, grad_raw, head_grads) = either(
        nothing, (), attn_backward, (gm3, *saved) + setup
    )
    g_home, g_full, gain_mix2 = hop_back(5, part, x2_home, gh3, gains[1, 0])
    if fused:
        all_c = gather_shards(tokens(g_home))

    *kept1, part = ffn_back_call(
        0, seq_local, shards, g_full, gu1, up_w, down_w, kept2 if fused else ()
    )
    part_out = down_call(1, seq_local, gu2, down_w, g_home)
    late = (hold_call(z3, part_out), grad_raw, saved[-1], gm3)
    unused, attn_grads = either(nothing, (), attn_weights, late)
    part = hold_call(part, attn_grads[0])
    if fused:
        all_b = with_mate(all_b, (1,), part_out)
        kept1[0] = others_up_call(1, seq_local, dp, all_b[0], up_w, kept1[0], attn_grads[0])
        part = hold_call(part, kept1[0])
    gh1, gm1, gain_ffn1 = sum_back(0, 6, part, h1, g_home, gains[0, 1])
    (part, conv_grads), unused = either(
        conv_backward, (gm1, project, mixed, start_full), nothing, ()
    )
    if fused:
        kept1[1] = others_up_call(1, seq_local, dp, all_b[1], up_w, kept1[1], gm1)
        part_out = hold_call(part_out, kept1[1])
    total = end(7, part, part_out)
    change, terms = norm_back(local.astype(F32), gains[0, 0], total)
    gain_mix1 = jnp.sum(terms, axis=(0, 1))
    boundary_out = jnp.where(is_first, pick(gh1, chip, 1) + change, pick(h3, chip, 1) + total)[None]

    if fused:
        all_c = with_mate(all_c, (0,), total)
        for half in range(2):
            kept1[half], kept1[2 + half] = others_back_call(
                seq_local,
                dp,
                all_c[half],
                all_a[half],
                down_w,
                kept1[half],
                kept1[2 + half],
            )
        grad_up, grad_down = choose(
            weights,
            (all_a, kept1[:2], all_c, kept1[2:]),
            (all_b, kept1[:2], all_a, kept1[2:]),
        )
    else:
        grad_up, grad_down = choose(
            weights,
            ((full1,), kept1[:1], (g_full,), kept1[1:]),
            ((full2,), kept2[:1], (start_full,), kept2[1:]),
        )
        grad_up, grad_down = lax.psum((grad_up.astype(BF), grad_down.astype(BF)), "dp")
    full_gu = grad_up.astype(F32).transpose(2, 0, 1)[None]
    full_down = grad_down.astype(F32).T[None]

    zero = jnp.zeros_like(gain_mix1)
    first_gains = jnp.concatenate([gain_mix1, gain_ffn1, zero, zero])
    second_gains = jnp.concatenate([zero, zero, gain_mix2, gain_ffn2])
    small = jnp.concatenate([jnp.where(is_first, first_gains, second_gains), head_grads.reshape(-1)])
    if fused:
        small = total_call(11, hold_call(small.reshape(1, -1), grad_down))[0]
    else:
        small = lax.psum(small, ("section", "tensor", "dp"))
    mixer_sums = lax.psum(tuple(conv_grads) + tuple(attn_grads), ("section", "dp"))
    mixer_sums = [hold_call(v, small) for v in mixer_sums]
    *sum_cin, sum_cout, sum_aq, sum_akv, sum_aout = [v.astype(F32) for v in mixer_sums]
    sum_kernel = sum_cout[channels : channels + conv_kernel.shape[0], :channels]
    sum_cin = jnp.stack(sum_cin).transpose(1, 0, 2)
    sum_cout = sum_cout[:channels]

    cut = 4 * width
    return (
        boundary_out,
        small[:cut].reshape(norm_gains.shape),
        small[cut:].reshape(qk_gains.shape),
        sum_cin,
        sum_kernel,
        sum_cout,
        sum_aq,
        sum_akv,
        sum_aout,
        full_gu,
        full_down,
    )


def solution(mesh):
    placed = (
        P("section", "dp", "tensor", None),
        P("dp", None),
        P(),
        P(),
        P(None, None, "tensor"),
        P(None, "tensor"),
        P("tensor", None),
        P(None, "tensor"),
        P(None, None, "tensor"),
        P("tensor", None),
        P("section", None, None, "tensor"),
        P("section", None, "tensor"),
    )
    def within(*args):
        with jax.sharding.use_abstract_mesh(mesh.abstract_mesh):
            return mapped(*args)

    mapped = jax.shard_map(
        on_device,
        mesh=mesh,
        in_specs=placed,
        out_specs=(
            P("section", "dp", "tensor", None),
            P(),
            P(),
            P(None, None, "tensor"),
            P(None, "tensor"),
            P("tensor", None),
            P(None, "tensor"),
            P(None, None, "tensor"),
            P("tensor", None),
            P("section", None, None, "tensor"),
            P("section", None, "tensor"),
        ),
        check_vma=False,
    )
    return within
```

```python
import functools

import jax
import jax.numpy as jnp
from jax import lax
from jax.experimental import pallas as pl
from jax.experimental.pallas import tpu as pltpu
from jax.sharding import PartitionSpec as P

EPSILON = 1e-05
THETA = 1000000.0
NEGATIVE = -1e30
BF = jnp.bfloat16
F32 = jnp.float32
MESH = pl.DeviceIdType.MESH
TILE = 64
VMEM_BYTES = 60 * 1024 * 1024
WEIGHT_BYTES = 62 * 1024 * 1024


def mm(spec, left, right, kind=F32):
    return jnp.einsum(spec, left, right, preferred_element_type=F32).astype(kind)


def inverse_rms(values):
    return lax.rsqrt(jnp.mean(values * values, axis=-1, keepdims=True) + EPSILON)


def norm(values, gain):
    return (values * inverse_rms(values) * gain).astype(BF)


def norm_back(values, gain, grad):
    scale = inverse_rms(values)
    normed = values * scale
    weighted = grad * gain
    grad_in = scale * (weighted - normed * jnp.mean(weighted * normed, axis=-1, keepdims=True))
    return grad_in, grad * normed


def section_pairs(section, size, function):
    return [
        (section * size + i, section * size + function(i))
        for i in range(size)
        if 0 <= function(i) < size
    ]


def permute(values, section, axis, function):
    pairs = section_pairs(section, lax.axis_size(axis), function)
    return lax.ppermute(values, ("section", axis), pairs)


def pick(values, index, axis):
    return lax.dynamic_index_in_dim(values, index, axis, keepdims=False)


def delay_rows(values, lag):
    widths = ((0, 0), (lag, 0)) + ((0, 0),) * (values.ndim - 2)
    return jnp.pad(values, widths)[:, : values.shape[1]]


def advance_rows(values, lag):
    widths = ((0, 0), (0, lag)) + ((0, 0),) * (values.ndim - 2)
    return jnp.pad(values, widths)[:, lag:]


def lag_masks(seg_ids, kernel_len):
    masks_list = []
    for lag in range(1, kernel_len):
        shifted = jnp.pad(seg_ids, ((0, 0), (lag, 0)), constant_values=-1)[:, : seg_ids.shape[1]]
        masks_list.append((shifted == seg_ids).astype(F32)[..., None])
    return masks_list


def rope_tables(seg_ids, half_dim):
    starts = jnp.sum((seg_ids[:, None, :] < seg_ids[:, :, None]).astype(jnp.int32), axis=2)
    places = jnp.arange(seg_ids.shape[1], dtype=jnp.int32)[None, :] - starts
    freqs = jnp.power(THETA, -(2.0 * jnp.arange(half_dim, dtype=F32)) / (2.0 * half_dim))
    angles = places.astype(F32)[..., None] * freqs
    return (jnp.cos(angles), jnp.sin(angles))


class Peers:
    def __init__(self):
        self.section = lax.axis_index("section")
        place = lax.axis_index("tensor")
        self.core = place % 2
        self.chip = place // 2
        self.mate = {"tensor": place + 1 - 2 * self.core}
        self.beside = {"tensor": place + 2 - 4 * self.chip}
        self.across = {"section": 1 - self.section}
        self.corner = {"section": 1 - self.section, "tensor": place + 2 - 4 * self.chip}


def greet(signalled, count):
    barrier = pltpu.get_barrier_semaphore()
    for device in signalled:
        pl.semaphore_signal(barrier, inc=1, device_id=device, device_id_type=MESH)
    pl.semaphore_wait(barrier, count)


def remote(source, target, send, receive, device):
    return pltpu.make_async_remote_copy(
        src_ref=source,
        dst_ref=target,
        send_sem=send,
        recv_sem=receive,
        device_id=device,
        device_id_type=MESH,
    )


def loop(count, body):
    lax.fori_loop(0, count, lambda i, unused: (body(i), 0)[1], 0)


def tile_rows(index):
    return pl.ds(pl.multiple_of(index * TILE, TILE), TILE)


def home_tile(j, chip, per_chip):
    each = per_chip // TILE
    return ((j // each) * 2 + chip) * each + j % each


def rms_tile(values):
    return lax.rsqrt(jnp.mean(values * values, axis=-1, keepdims=True) + EPSILON)


def norm_back_tile(values, gain, grad):
    scale = rms_tile(values)
    normed = values * scale
    weighted = grad * gain
    inner = jnp.mean(weighted * normed, axis=-1, keepdims=True)
    return scale * (weighted - normed * inner), grad * normed


def comm_call(kernel, name, number, inputs, outs, scratch, where, micros=52, to=None):
    return pl.pallas_call(
        kernel,
        name=name,
        out_shape=outs,
        in_specs=[pl.BlockSpec(memory_space=space) for space in where],
        out_specs=tuple(
            pl.BlockSpec(memory_space=space) for space in to or [pltpu.VMEM] * len(outs)
        ),
        scratch_shapes=scratch,
        cost_estimate=estimate(micros),
        compiler_params=pltpu.CompilerParams(
            collective_id=number, has_side_effects=True, vmem_limit_bytes=VMEM_BYTES
        ),
    )(*inputs)


def full_tile(i, core, per_chip):
    each = per_chip // TILE
    return ((i // each) * 2 + core) * each + i % each


def sum_tiles(active, backward, per_chip, *refs):
    if backward:
        part, gain, hidden_in, grad_in, out_to, full, gain_out = refs[:7]
        hidden, grad = refs[7:9]
        loads = [(hidden_in, hidden), (grad_in, grad)]
        scratch = refs[9:]
    else:
        part, gain, residual_in, out_to, full, home_low = refs[:6]
        residual = refs[6]
        loads = [(residual_in, residual)]
        scratch = refs[7:]
    out, low, mine, from_mate, summed, from_chip, relayed = scratch[:7]
    own_s, mate_s, mate_r, chip_s, chip_r, relay_s, relay_r, low_s, low_r = scratch[7:16]
    load_s, out_s, full_s, home_s = scratch[16:]
    peers = Peers()
    loads = [
        pltpu.make_async_copy(one, two, load_s.at[k]) for k, (one, two) in enumerate(loads)
    ]
    count = mine.shape[0] // TILE
    pairs = count // 2

    def own_rows(i):
        return tile_rows(full_tile(i, peers.core, per_chip))

    def own_copy(i):
        return pltpu.make_async_copy(part.at[own_rows(i)], mine.at[tile_rows(i)], own_s.at[i])

    def mate_copy(i):
        theirs = tile_rows(full_tile(i, 1 - peers.core, per_chip))
        target = from_mate.at[tile_rows(i)]
        return remote(part.at[theirs], target, mate_s.at[i], mate_r.at[i], peers.mate)

    def direct(i):
        rows = tile_rows(i)
        return remote(summed.at[rows], from_chip.at[rows], chip_s.at[i], chip_r.at[i], peers.beside)

    def detour(p):
        return remote(
            summed.at[tile_rows(2 * p)],
            relayed.at[tile_rows(p)],
            chip_s.at[2 * p],
            relay_r.at[p],
            peers.corner,
        )

    def back(p):
        return remote(
            relayed.at[tile_rows(p)],
            from_chip.at[tile_rows(2 * p)],
            relay_s.at[p],
            chip_r.at[2 * p],
            peers.across,
        )

    def low_copy(i):
        source = low.at[tile_rows(i)]
        return remote(source, full.at[own_rows(i)], low_s.at[i], low_r.at[i], peers.mate)

    def stores(i):
        rows = tile_rows(i)
        copies = [
            pltpu.make_async_copy(out.at[rows], out_to.at[rows], out_s.at[i]),
            pltpu.make_async_copy(low.at[rows], full.at[own_rows(i)], full_s.at[i]),
        ]
        if not backward:
            copies.append(pltpu.make_async_copy(low.at[rows], home_low.at[rows], home_s.at[i]))
        return copies

    def low_wait(i):
        rows = tile_rows(full_tile(i, 1 - peers.core, per_chip))
        source = low.at[tile_rows(i)]
        remote(source, full.at[rows], low_s.at[i], low_r.at[i], peers.mate).wait_recv()

    @pl.when(peers.section == active)
    def work():
        loop(count, lambda i: own_copy(i).start())
        for copy in loads:
            copy.start()
        greet([peers.mate, peers.beside, peers.across], 3)
        loop(count, lambda i: mate_copy(i).start())

        def first(p):
            for k in range(2):
                i = 2 * p + k
                rows = tile_rows(i)
                own_copy(i).wait()
                mate_copy(i).wait_recv()
                total = mine[rows, :].astype(F32) + from_mate[rows, :].astype(F32)
                out[rows, :] = total
                summed[rows, :] = total.astype(BF)
                if k == 0:
                    detour(p).start()
                else:
                    direct(i).start()

        loop(pairs, first)
        for copy in loads:
            copy.wait()
        if backward:
            gain_out[...] = jnp.zeros_like(gain_out)

        def second(i):
            rows = tile_rows(i)
            direct(i).wait_recv()
            total = out[rows, :] + from_chip[rows, :].astype(F32)
            if backward:
                change, terms = norm_back_tile(hidden[rows, :], gain[...], total)
                result = grad[rows, :].astype(F32) + change
                lower = result.astype(BF)
                ours = ((i * TILE) // per_chip) % 2 == peers.chip
                added = jnp.sum(terms, axis=0, keepdims=True)
                gain_out[...] += jnp.where(ours, added, jnp.zeros_like(added))
            else:
                result = residual[rows, :].astype(F32) + total
                lower = (result * rms_tile(result) * gain[...]).astype(BF)
            out[rows, :] = result
            low[rows, :] = lower
            low_copy(i).start()
            for copy in stores(i):
                copy.start()

        loop(count, second)

        def finish(i):
            mate_copy(i).wait_send()
            direct(i).wait_send()
            low_copy(i).wait_send()
            low_wait(i)
            for copy in stores(i):
                copy.wait()

        loop(count, finish)

    @pl.when(peers.section != active)
    def relay():
        greet([peers.corner], 1)

        def step(p):
            detour(p).wait_recv()
            back(p).start()

        loop(pairs, step)
        if not backward:
            for copy in loads:
                copy.start()
                copy.wait()
            copy = pltpu.make_async_copy(residual, home_low, home_s.at[0])
            copy.start()
            copy.wait()
        loop(pairs, lambda p: back(p).wait_send())


def sum_call(active, number, backward, per_chip, part, *rest):
    size, width = part.shape
    size //= 2
    count = size // TILE
    outs = (
        jax.ShapeDtypeStruct((size, width), F32),
        jax.ShapeDtypeStruct((2 * size, width), BF),
    )
    outs += (jax.ShapeDtypeStruct((1, width), F32) if backward else jax.ShapeDtypeStruct((size, width), BF),)
    part, gain, *others = (part,) + rest
    scratch = [pltpu.VMEM((size, width), one.dtype) for one in others]
    scratch += [pltpu.VMEM((size, width), F32)] + [pltpu.VMEM((size, width), BF)] * 5
    scratch += [pltpu.VMEM((size // 2, width), BF)]
    sizes = [count, count, count, count, count, count // 2, count // 2, count, count]
    sizes += [2, count, count, count]
    scratch += [pltpu.SemaphoreType.DMA((n,)) for n in sizes]
    return comm_call(
        functools.partial(sum_tiles, active, backward, per_chip),
        "sum_back" if backward else "sum_norm",
        number,
        (part,) + rest,
        outs,
        scratch,
        [pl.ANY, pltpu.VMEM] + [pl.ANY] * len(others),
        to=[pl.ANY] * 2 + [pltpu.VMEM if backward else pl.ANY],
    )


def spread_tiles(normed, peers, per_chip, gain, home, full, low, sems, arrived, source):
    chip_s, chip_r, low_s, low_r, full_s = sems
    half = home.shape[0] // TILE // 2

    def place(j, chip):
        return home_tile(j, chip, per_chip)

    def chip_copy(j):
        rows = tile_rows(place(j, peers.chip))
        return remote(source(j), home.at[rows], chip_s.at[j], chip_r.at[j], peers.beside)

    def chip_wait(j):
        rows = tile_rows(place(j, 1 - peers.chip))
        remote(source(j), home.at[rows], chip_s.at[j], chip_r.at[j], peers.beside).wait_recv()

    def low_copy(i, k, core):
        rows = tile_rows(full_tile(i, core, per_chip))
        return remote(low.at[tile_rows(i)], full.at[rows], low_s.at[k], low_r.at[k], peers.mate)

    def store(i):
        rows = tile_rows(full_tile(i, peers.core, per_chip))
        return pltpu.make_async_copy(low.at[tile_rows(i)], full.at[rows], full_s.at[i])

    def lower(i, values):
        wide = values.astype(F32)
        if normed == "all":
            wide = wide * rms_tile(wide) * gain[...]
        elif normed == "first":
            scale = rms_tile(wide)
            wide = wide * jnp.where(peers.section == 0, scale, jnp.ones_like(scale)) * gain[...]
        low[tile_rows(i), :] = wide.astype(BF)
        store(i).start()

    def own(j):
        arrived(j)
        chip_copy(j).start()
        i = place(j, peers.chip)
        values = source(j)[...]
        home[tile_rows(i), :] = values
        lower(i, values)
        low_copy(i, j, peers.core).start()

    loop(half, own)

    def other(j):
        chip_wait(j)
        i = place(j, 1 - peers.chip)
        lower(i, home[tile_rows(i), :])
        low_copy(i, half + j, peers.core).start()

    loop(half, other)

    def finish(j):
        chip_copy(j).wait_send()
        low_copy(place(j, peers.chip), j, peers.core).wait_send()
        low_copy(place(j, 1 - peers.chip), half + j, peers.core).wait_send()
        low_copy(place(j, peers.chip), j, 1 - peers.core).wait_recv()
        low_copy(place(j, 1 - peers.chip), half + j, 1 - peers.core).wait_recv()
        store(place(j, peers.chip)).wait()
        store(place(j, 1 - peers.chip)).wait()

    loop(half, finish)


def start_tiles(per_chip, local, gain, home, full, low, *sems):
    peers = Peers()
    greet([peers.mate, peers.beside], 2)
    spread_tiles(
        "first",
        peers,
        per_chip,
        gain,
        home,
        full,
        low,
        sems,
        lambda j: None,
        lambda j: local.at[tile_rows(j)],
    )


def start_call(number, per_chip, local, gain):
    size, width = local.shape
    half = size // TILE
    outs = (
        jax.ShapeDtypeStruct((2 * size, width), BF),
        jax.ShapeDtypeStruct((4 * size, width), BF),
    )
    return comm_call(
        functools.partial(start_tiles, per_chip),
        "start",
        number,
        (local, gain),
        outs,
        [pltpu.VMEM((2 * size, width), BF)]
        + [pltpu.SemaphoreType.DMA((n,)) for n in (half, half, 2 * half, 2 * half, 2 * half)],
        [pltpu.VMEM, pltpu.VMEM],
        to=[pltpu.VMEM, pl.ANY],
    )


def scatter_steps(peers, per_chip, parts, mine, from_mate, summed, from_chip, sems, finished, ready=None):
    own_s, mate_s, mate_r, chip_s, chip_r = sems
    half = mine.shape[0] // TILE // 2

    def rows_of(j, chip, core):
        return tile_rows(full_tile(home_tile(j, chip, per_chip), core, per_chip))

    def slot(j, k):
        return tile_rows(half * k + j)

    def chip_of(k):
        return 1 - peers.chip if k == 0 else peers.chip

    def own_copy(j, k, part=parts[0]):
        source = part.at[rows_of(j, chip_of(k), peers.core)]
        return pltpu.make_async_copy(source, mine.at[slot(j, k)], own_s.at[half * k + j])

    def mate_copy(j, k, part=parts[0]):
        source = part.at[rows_of(j, chip_of(k), 1 - peers.core)]
        index = half * k + j
        target = from_mate.at[slot(j, k)]
        return remote(source, target, mate_s.at[index], mate_r.at[index], peers.mate)

    def chip_copy(j):
        rows = tile_rows(j)
        return remote(summed.at[rows], from_chip.at[rows], chip_s.at[j], chip_r.at[j], peers.beside)

    def begin(part):
        for k in range(2):
            loop(half, lambda j: own_copy(j, k, part).start())
            loop(half, lambda j: mate_copy(j, k, part).start())

    if len(parts) == 1:
        begin(parts[0])
    else:
        for section, part in enumerate(parts):
            pl.when(peers.section == section)(functools.partial(begin, part))

    def both(j, k):
        own_copy(j, k).wait()
        mate_copy(j, k).wait_recv()
        return mine[slot(j, k), :].astype(F32) + from_mate[slot(j, k), :].astype(F32)

    def away(j):
        summed[tile_rows(j), :] = both(j, 0).astype(BF)
        chip_copy(j).start()

    loop(half, away)
    if ready:
        ready()

    def last(j):
        total = both(j, 1)
        chip_copy(j).wait_recv()
        finished(j, total + from_chip[tile_rows(j), :].astype(F32))

    loop(half, last)

    def finish(j):
        mate_copy(j, 0).wait_send()
        mate_copy(j, 1).wait_send()
        chip_copy(j).wait_send()

    loop(half, finish)


def scatter_scratch(size, width):
    half = size // TILE // 2
    buffers = [pltpu.VMEM((size, width), BF)] * 2 + [pltpu.VMEM((size // 2, width), BF)] * 2
    counts = (2 * half, 2 * half, 2 * half, half, half)
    return buffers + [pltpu.SemaphoreType.DMA((n,)) for n in counts]


def end_tiles(per_chip, first, second, out, *scratch):
    peers = Peers()
    greet([peers.mate, peers.beside], 2)

    def finished(j, total):
        out[tile_rows(j), :] = total

    scatter_steps(peers, per_chip, (first, second), *scratch[:4], scratch[4:], finished)


def end_call(number, per_chip, first, second):
    size, width = first.shape
    size //= 2
    return comm_call(
        functools.partial(end_tiles, per_chip),
        "end",
        number,
        (first, second),
        (jax.ShapeDtypeStruct((size // 2, width), F32),),
        scatter_scratch(size, width),
        [pl.ANY, pl.ANY],
    )[0]


def hop_tiles(source, backward, per_chip, *refs):
    if backward:
        part, gain, values_in, grad_in, home, full, gain_out = refs[:7]
        values, grad = refs[7:9]
        loads = [(values_in, values), (grad_in, grad)]
        scratch = refs[9:]
    else:
        part, gain, values_in, home, full = refs[:5]
        values = refs[5]
        loads = [(values_in, values)]
        scratch = refs[6:]
    load_s, low, crossing, landed, cross_s, cross_r = scratch[:6]
    spread_sems = scratch[6:11]
    buffers = scratch[11:15]
    scatter_sems = scratch[15:]
    loads = [
        pltpu.make_async_copy(one, two, load_s.at[k]) for k, (one, two) in enumerate(loads)
    ]
    peers = Peers()
    half = crossing.shape[0] // TILE

    def cross_copy(j):
        rows = tile_rows(j)
        return remote(
            crossing.at[rows], landed.at[rows], cross_s.at[j], cross_r.at[j], peers.across
        )

    @pl.when(peers.section == source)
    def give():
        for copy in loads:
            copy.start()
        greet([peers.mate, peers.beside], 3)
        if backward:
            gain_out[...] = jnp.zeros_like(gain_out)

        def ready():
            for copy in loads:
                copy.wait()

        def finished(j, total):
            own = tile_rows(home_tile(j, peers.chip, per_chip))
            if backward:
                change, terms = norm_back_tile(values[own, :].astype(F32), gain[...], total)
                result = grad[own, :] + change
                gain_out[...] += jnp.sum(terms, axis=0, keepdims=True)
            else:
                result = values[own, :] + total
            crossing[tile_rows(j), :] = result.astype(BF)
            cross_copy(j).start()

        scatter_steps(peers, per_chip, (part,), *buffers, scatter_sems, finished, ready)
        loop(half, lambda j: cross_copy(j).wait_send())

    @pl.when(peers.section != source)
    def take():
        greet([peers.mate, peers.beside, peers.across], 2)
        spread_tiles(
            None if backward else "all",
            peers,
            per_chip,
            gain,
            home,
            full,
            low,
            spread_sems,
            lambda j: cross_copy(j).wait_recv(),
            lambda j: landed.at[tile_rows(j)],
        )


def hop_call(source, number, backward, per_chip, part, *rest):
    size, width = part.shape
    size //= 2
    half = size // TILE // 2
    outs = (
        jax.ShapeDtypeStruct((size, width), BF),
        jax.ShapeDtypeStruct((2 * size, width), BF),
    )
    if backward:
        outs += (jax.ShapeDtypeStruct((1, width), F32),)
    gain, *others = rest
    scratch = [pltpu.VMEM((size, width), one.dtype) for one in others]
    scratch += [pltpu.SemaphoreType.DMA((2,)), pltpu.VMEM((size, width), BF)]
    scratch += [pltpu.VMEM((size // 2, width), BF)] * 2
    sizes = (half, half, half, half, 2 * half, 2 * half, 2 * half)
    scratch += [pltpu.SemaphoreType.DMA((n,)) for n in sizes]
    return comm_call(
        functools.partial(hop_tiles, source, backward, per_chip),
        "hop_back" if backward else "hop",
        number,
        (part,) + rest,
        outs,
        scratch + scatter_scratch(size, width),
        [pl.ANY, pltpu.VMEM] + [pl.ANY] * len(others),
        to=[pltpu.VMEM, pl.ANY] + [pltpu.VMEM] * backward,
    )


def silu_parts(gu):
    lanes = gu.shape[1] // 2
    gate = gu[:, :lanes].astype(F32)
    up = gu[:, lanes:].astype(F32)
    return gate, up, 1.0 / (1.0 + jnp.exp(-gate))


def load_up(up_w, up_v, sems):
    hidden = up_w.shape[1]
    lanes = up_v.shape[0] // 2
    copies = [
        pltpu.make_async_copy(up_w.at[c], up_v.at[pl.ds(c * lanes, hidden)], sems.at[c])
        for c in range(2)
    ]
    for c, copy in enumerate(copies):
        copy.start()
        if lanes > hidden:
            up_v[c * lanes + hidden : (c + 1) * lanes, :] = jnp.zeros(
                (lanes - hidden, up_v.shape[1]), BF
            )
    return copies


def load_down(down_w, down_v, sems):
    hidden = down_w.shape[0]
    lanes = down_v.shape[0]
    copy = pltpu.make_async_copy(down_w, down_v.at[pl.ds(0, hidden)], sems.at[2])
    copy.start()
    if lanes > hidden:
        down_v[hidden:, :] = jnp.zeros((lanes - hidden, down_v.shape[1]), BF)
    return [copy]


def wait_all(copies):
    for copy in copies:
        copy.wait()


def only(active, run):
    if active is None:
        run()
    else:
        pl.when(lax.axis_index("section") == active)(run)


def stream(body, grid, inputs, outs):
    def spec(item):
        ref, rows, place = item
        return pl.BlockSpec((rows, ref.shape[1]), lambda *g: (place(*g), 0))

    pltpu.emit_pipeline(
        body,
        grid=grid,
        in_specs=[spec(item) for item in inputs],
        out_specs=[spec(item) for item in outs],
    )(*[item[0] for item in inputs + outs])


def gate_up_body(up_v):
    def body(z_t, gu_t):
        gu_t[...] = dot(z_t[...], up_v[...], (1, 1)).astype(BF)

    return body


def ffn_tiles(active, tile, with_down, *refs):
    if with_down:
        full, up_w, down_w, gu, part, up_v, down_v, sems = refs
    else:
        full, up_w, gu, up_v, sems = refs

    def run():
        copies = load_up(up_w, up_v, sems)
        if with_down:
            copies += load_down(down_w, down_v, sems)
        wait_all(copies)

        def body(z_t, gu_t, part_t):
            low = dot(z_t[...], up_v[...], (1, 1)).astype(BF)
            gu_t[...] = low
            gate, up, sig = silu_parts(low)
            act = (gate * sig * up).astype(BF)
            part_t[...] = dot(act, down_v[...], (1, 0)).astype(BF)

        here = lambda i: i
        grid = (full.shape[0] // tile,)
        if with_down:
            stream(body, grid, [(full, tile, here)], [(gu, tile, here), (part, tile, here)])
        else:
            stream(gate_up_body(up_v), grid, [(full, tile, here)], [(gu, tile, here)])

    only(active, run)


def down_tiles(active, tile, gu, down_w, *refs):
    part, down_v, sems = refs[-3:]

    def run():
        wait_all(load_down(down_w, down_v, sems))

        def body(gu_t, part_t):
            gate, up, sig = silu_parts(gu_t[...])
            part_t[...] = dot((gate * sig * up).astype(BF), down_v[...], (1, 0)).astype(BF)

        here = lambda i: i
        stream(body, (gu.shape[0] // tile,), [(gu, tile, here)], [(part, tile, here)])

    only(active, run)


def back_body(up_v, down_v):
    def body(g_t, gu_t, grad_t, act_t, *part_t):
        grad_act = dot(g_t[...], down_v[...], (1, 1))
        gate, up, sig = silu_parts(gu_t[...])
        silu = gate * sig
        act_t[...] = (silu * up).astype(BF)
        slope = sig + silu * (1.0 - sig)
        lanes = gate.shape[1]
        grad_t[:, :lanes] = (grad_act * up * slope).astype(BF)
        grad_t[:, lanes:] = (grad_act * silu).astype(BF)
        if part_t:
            part_t[0][...] = dot(grad_t[...], up_v[...], (1, 0)).astype(BF)

    return body


def ffn_back_tiles(active, tile, grad, gu, up_w, down_w, grad_gu, act, part, up_v, down_v, sems):
    def run():
        wait_all(load_down(down_w, down_v, sems) + load_up(up_w, up_v, sems))
        here = lambda i: i
        stream(
            back_body(up_v, down_v),
            (grad.shape[0] // tile,),
            [(ref, tile, here) for ref in (grad, gu)],
            [(ref, tile, here) for ref in (grad_gu, act, part)],
        )

    only(active, run)


def others_up_tiles(active, tile, shards, source, up_w, *refs):
    out, up_v, sems = refs[-3:]

    def run():
        wait_all(load_up(up_w, up_v, sems))
        spot = lax.axis_index("dp")
        count = source.shape[0] // tile // shards
        place = lambda k, i: ((spot + 1 + k) % shards) * count + i
        items = [(source, tile, place)], [(out, tile, place)]
        stream(gate_up_body(up_v), (shards - 1, count), *items)

    only(active, run)


def weight_tiles(tile, shards, chunks, *refs):
    sides = refs[:8], refs[8:16]
    others_gu = refs[16:18]
    down_w, out_up, out_down, up_sum, down_sum, down_v, sems = refs[18:]
    hidden = out_down.shape[0]
    lanes = down_sum.shape[0]
    piece = lanes // chunks
    copies = load_down(down_w, down_v, sems)
    up_sum[...] = jnp.zeros_like(up_sum)
    down_sum[...] = jnp.zeros_like(down_sum)
    spot = lax.axis_index("dp")

    def add(c, z_t, g_t, grad_gate, grad_up, act):
        rows = slice(c * piece, (c + 1) * piece)
        more = slice(lanes + c * piece, lanes + (c + 1) * piece)
        up_sum[rows, :] += dot(grad_gate, z_t[...], (0, 0))
        up_sum[more, :] += dot(grad_up, z_t[...], (0, 0))
        down_sum[rows, :] += dot(act, g_t[...], (0, 0))

    def own_body(z_t, grad_t, g_t, act_t):
        for c in range(chunks):
            rows = slice(c * piece, (c + 1) * piece)
            more = slice(lanes + c * piece, lanes + (c + 1) * piece)
            add(c, z_t, g_t, grad_t[:, rows], grad_t[:, more], act_t[:, rows])

    def body(z_t, g_t, gu_t):
        for c in range(chunks):
            rows = slice(c * piece, (c + 1) * piece)
            more = slice(lanes + c * piece, lanes + (c + 1) * piece)
            grad_act = dot(g_t[...], down_v[rows, :], (1, 1))
            gate = gu_t[:, rows].astype(F32)
            up = gu_t[:, more].astype(F32)
            sig = 1.0 / (1.0 + jnp.exp(-gate))
            silu = gate * sig
            slope = sig + silu * (1.0 - sig)
            add(
                c,
                z_t,
                g_t,
                (grad_act * up * slope).astype(BF),
                (grad_act * silu).astype(BF),
                (silu * up).astype(BF),
            )

    def run(z_mine, z_mate, g_mine, g_mate, full, grad_gu, grad_full, act):
        here = lambda i: i
        items = [(ref, tile, here) for ref in (full, grad_gu, grad_full, act)]
        stream(own_body, (full.shape[0] // tile,), items, [])
        count = z_mine.shape[0] // tile // shards
        place = lambda k, i: ((spot + 1 + k) % shards) * count + i
        for z, g, gu in ((z_mine, g_mine, others_gu[0]), (z_mate, g_mate, others_gu[1])):
            items = [(ref, tile, place) for ref in (z, g, gu)]
            stream(body, (shards - 1, count), items, [])

    wait_all(copies)
    for section in range(2):
        only(section, functools.partial(run, *sides[section]))
    copies = [
        pltpu.make_async_copy(up_sum.at[pl.ds(c * lanes, hidden)], out_up.at[c], sems.at[c])
        for c in range(2)
    ]
    copies += [pltpu.make_async_copy(down_sum.at[pl.ds(0, hidden)], out_down, sems.at[2])]
    for copy in copies:
        copy.start()
    wait_all(copies)


def ffn_pallas(kernel, name, inputs, outs, weights, micros, aliases=None):
    return pl.pallas_call(
        kernel,
        name=name,
        out_shape=tuple(jax.ShapeDtypeStruct(shape, BF) for shape in outs),
        in_specs=[pl.BlockSpec(memory_space=pl.ANY)] * len(inputs),
        out_specs=tuple(pl.BlockSpec(memory_space=pl.ANY) for unused in outs),
        scratch_shapes=[pltpu.VMEM(shape, BF) for shape in weights]
        + [pltpu.SemaphoreType.DMA((3,))],
        input_output_aliases=aliases or {},
        cost_estimate=estimate(micros),
        compiler_params=pltpu.CompilerParams(vmem_limit_bytes=VMEM_BYTES),
    )(*inputs)


def estimate(micros):
    return pl.CostEstimate(flops=0, bytes_accessed=int(micros * 3.3e6), transcendentals=0)


def weight_shapes(up_w):
    lanes = padded(up_w.shape[1])
    return (2 * lanes, up_w.shape[2]), (lanes, up_w.shape[2])


def ffn_call(active, tile, full, up_w, down_w):
    up, down = weight_shapes(up_w)
    gu = (full.shape[0], up[0])
    if down_w is None:
        kernel = functools.partial(ffn_tiles, active, tile, False)
        return ffn_pallas(kernel, "gate_up", (full, up_w), (gu,), (up,), 30)[0]
    kernel = functools.partial(ffn_tiles, active, tile, True)
    return ffn_pallas(kernel, "ffn", (full, up_w, down_w), (gu, full.shape), (up, down), 44)


def down_call(active, tile, gu, down_w, *earlier):
    rows, lanes = gu.shape
    return ffn_pallas(
        functools.partial(down_tiles, active, tile),
        "down",
        (gu, down_w) + earlier,
        ((rows, down_w.shape[1]),),
        ((lanes // 2, down_w.shape[1]),),
        20,
    )[0]


def ffn_back_call(active, tile, grad, gu, up_w, down_w):
    up, down = weight_shapes(up_w)
    return ffn_pallas(
        functools.partial(ffn_back_tiles, active, tile),
        "ffn_back",
        (grad, gu, up_w, down_w),
        (gu.shape, (grad.shape[0], down[0]), grad.shape),
        (up, down),
        48,
    )


def others_up_call(active, tile, shards, source, up_w, into, *earlier):
    up = weight_shapes(up_w)[0]
    more = earlier if into is None else (into,) + earlier
    return ffn_pallas(
        functools.partial(others_up_tiles, active, tile, shards),
        "others_up",
        (source, up_w) + more,
        ((source.shape[0], up[0]),),
        (up,),
        42,
        {} if into is None else {2: 0},
    )[0]


def weight_call(tile, shards, first, second, others_gu, down_w):
    hidden, width = down_w.shape
    lanes = padded(hidden)
    inputs = tuple(first) + tuple(second) + tuple(others_gu) + (down_w,)
    return pl.pallas_call(
        functools.partial(weight_tiles, tile, shards, 1),
        name="weights",
        out_shape=(
            jax.ShapeDtypeStruct((2, hidden, width), F32),
            jax.ShapeDtypeStruct((hidden, width), F32),
        ),
        in_specs=[pl.BlockSpec(memory_space=pl.ANY)] * len(inputs),
        out_specs=(pl.BlockSpec(memory_space=pl.ANY),) * 2,
        scratch_shapes=[
            pltpu.VMEM((2 * lanes, width), F32),
            pltpu.VMEM((lanes, width), F32),
            pltpu.VMEM((lanes, width), BF),
            pltpu.SemaphoreType.DMA((3,)),
        ],
        cost_estimate=estimate(60),
        compiler_params=pltpu.CompilerParams(vmem_limit_bytes=WEIGHT_BYTES),
    )(*inputs)


def hold_call(values, *others):
    if not others:
        return values
    return pl.pallas_call(
        lambda *refs: None,
        name="hold",
        out_shape=jax.ShapeDtypeStruct(values.shape, values.dtype),
        in_specs=[pl.BlockSpec(memory_space=pl.ANY)] * (1 + len(others)),
        out_specs=pl.BlockSpec(memory_space=pl.ANY),
        input_output_aliases={0: 0},
        cost_estimate=estimate(1),
        compiler_params=pltpu.CompilerParams(has_side_effects=True),
    )(values, *others)


def total_tiles(values, out, near, far, sends, receives, far_sends, far_receives):
    section = lax.axis_index("section")
    place = lax.axis_index("tensor")
    spot = lax.axis_index("dp")
    size = near.shape[0]
    chips = size // 2
    shards = far.shape[0]
    own = section * chips + place
    steps = [(a, b) for a in range(2) for b in range(chips) if a + b > 0]
    peers = [{"section": (section + a) % 2, "tensor": (place + b) % chips} for a, b in steps]
    shard_peers = [{"dp": (spot + c) % shards} for c in range(1, shards)]
    greet(peers + shard_peers, len(peers) + len(shard_peers))
    near[own] = values[...]
    copies = [
        remote(near.at[own], near.at[own], sends.at[i], receives.at[own], peer)
        for i, peer in enumerate(peers)
    ]
    for copy in copies:
        copy.start()
    for (a, b), peer in zip(steps, peers):
        theirs = ((section + a) % 2) * chips + (place + b) % chips
        remote(near.at[theirs], near.at[theirs], sends.at[0], receives.at[theirs], peer).wait_recv()
    total = near[0]
    for i in range(1, size):
        total = total + near[i]
    far[spot] = total
    far_copies = [
        remote(far.at[spot], far.at[spot], far_sends.at[i], far_receives.at[spot], peer)
        for i, peer in enumerate(shard_peers)
    ]
    for copy in far_copies:
        copy.start()
    for c, peer in enumerate(shard_peers):
        theirs = (spot + c + 1) % shards
        remote(far.at[theirs], far.at[theirs], far_sends.at[0], far_receives.at[theirs], peer).wait_recv()
    total = far[0]
    for i in range(1, shards):
        total = total + far[i]
    out[...] = total
    for copy in copies + far_copies:
        copy.wait_send()


def total_call(number, values, size, shards):
    return comm_call(
        total_tiles,
        "total",
        number,
        (values,),
        (jax.ShapeDtypeStruct(values.shape, F32),),
        [
            pltpu.VMEM((size,) + values.shape, F32),
            pltpu.VMEM((shards,) + values.shape, F32),
            pltpu.SemaphoreType.DMA((size,)),
            pltpu.SemaphoreType.DMA((size,)),
            pltpu.SemaphoreType.DMA((shards,)),
            pltpu.SemaphoreType.DMA((shards,)),
        ],
        [pltpu.VMEM],
        10,
    )[0]


def rotated(values):
    half = values.shape[-1] // 2
    return jnp.concatenate([-values[:, half:], values[:, :half]], axis=-1)


def dot(left, right, dims):
    return lax.dot_general(left, right, ((dims[:1], dims[1:]), ((), ())), preferred_element_type=F32)


def attend_tiles(groups, size, block, raw, cosine, sine, seg_col, seg_row, gains, out, probs, totals, turned, heads):
    length = raw.shape[1]
    cos_t = cosine[0]
    sin_t = sine[0]
    scaling = size ** (-0.5)

    def prepared(values, gain):
        normed = values * rms_tile(values) * gain
        return normed * cos_t + rotated(normed) * sin_t

    for g in range(groups):
        lanes = slice(g * size, (g + 1) * size)
        query = (prepared(raw[0, :, lanes], gains[0:1, :]).astype(BF) * scaling).astype(BF)
        heads[g] = query
        turned[0, :, lanes] = query
    lanes = slice(groups * size, (groups + 1) * size)
    keyed = prepared(raw[0, :, lanes], gains[1:2, :]).astype(BF)
    turned[0, :, lanes] = keyed
    lanes = slice((groups + 1) * size, (groups + 2) * size)
    valued = raw[0, :, lanes].astype(BF)
    turned[0, :, lanes] = valued
    ones = (lax.broadcasted_iota(jnp.int32, (length, size), 1) == 0).astype(BF)
    widened = jnp.concatenate([valued, ones], axis=1)
    used = (groups + 2) * size
    if used < turned.shape[2]:
        turned[0, :, used:] = jnp.zeros((length, turned.shape[2] - used), BF)
    for i in range(length // block):
        rows = slice(i * block, (i + 1) * block)
        span = (i + 1) * block
        query_pos = i * block + lax.broadcasted_iota(jnp.int32, (block, span), 0)
        key_pos = lax.broadcasted_iota(jnp.int32, (block, span), 1)
        allowed = (key_pos <= query_pos) & (seg_col[0, rows, :] == seg_row[0, :, :span])

        def head(g):
            scores = dot(heads[g, rows, :], keyed[:span], (1, 1))
            expon = jnp.exp(jnp.where(allowed, scores, NEGATIVE)).astype(BF)
            probs[0, 0, g, rows, :span] = expon
            summed = dot(expon, widened[:span], (1, 0))
            total = summed[:, size : size + 1]
            totals[0, 0, g, rows, :] = total
            heads[g, rows, :] = (summed[:, :size] * (1.0 / total)).astype(BF)

        for g in range(groups):
            head(g)
    for g in range(groups):
        out[0, :, g * size : (g + 1) * size] = heads[g]
    if groups * size < out.shape[2]:
        out[0, :, groups * size :] = jnp.zeros((length, out.shape[2] - groups * size), BF)


def attend_back_tiles(
    groups, size, block, raw, turned, probs, totals, out, grad_out, cosine, sine, gains, grad_raw, grad_gains, heads, grads, inner, query_grad, key_grad, val_grad
):
    length = raw.shape[1]
    cos_t = cosine[0]
    sin_t = sine[0]
    scaling = size ** (-0.5)

    @pl.when((pl.program_id(0) == 0) & (pl.program_id(1) == 0))
    def clear():
        grad_gains[...] = jnp.zeros_like(grad_gains)

    blocks = length // block
    for g in range(groups):
        lanes = slice(g * size, (g + 1) * size)
        shared = (grad_out[0, :, lanes].astype(F32) * (1.0 / totals[0, 0, g])).astype(BF)
        mean = jnp.sum(shared.astype(F32) * out[0, :, lanes].astype(F32), axis=-1, keepdims=True)
        for i in range(blocks):
            rows = slice(i * block, (i + 1) * block)
            into = slice(g * block, (g + 1) * block)
            heads[i, into, :] = turned[0, rows, lanes]
            grads[i, into, :] = shared[rows]
            inner[i, into, :] = mean[rows]
    keyed = turned[0, :, groups * size : (groups + 1) * size]
    valued = turned[0, :, (groups + 1) * size : (groups + 2) * size]
    key_grad[...] = jnp.zeros_like(key_grad)
    val_grad[...] = jnp.zeros_like(val_grad)
    for i in range(blocks):
        rows = slice(i * block, (i + 1) * block)
        span = (i + 1) * block
        low = jnp.concatenate([probs[0, 0, g, rows, :span] for g in range(groups)], axis=0)
        grad_probs = dot(grads[i], valued[:span], (1, 1))
        grad_scores = (low.astype(F32) * (grad_probs - inner[i])).astype(BF)
        back_q = dot(grad_scores, keyed[:span], (1, 0)) * scaling
        for g in range(groups):
            query_grad[g, rows, :] = back_q[g * block : (g + 1) * block]
        key_grad[:, :span] += dot(heads[i], grad_scores, (0, 0))
        val_grad[:, :span] += dot(grads[i], low, (0, 0))

    def back(values, gain, grad, which):
        grad = grad * cos_t - rotated(grad) * sin_t
        change, terms = norm_back_tile(values, gain, grad)
        grad_gains[which : which + 1, :] += jnp.sum(terms, axis=0, keepdims=True)
        return change.astype(BF)

    for g in range(groups):
        lanes = slice(g * size, (g + 1) * size)
        grad_raw[0, :, lanes] = back(raw[0, :, lanes], gains[0:1, :], query_grad[g], 0)
    lanes = slice(groups * size, (groups + 1) * size)
    grad_raw[0, :, lanes] = back(raw[0, :, lanes], gains[1:2, :], key_grad[...].T, 1)
    lanes = slice((groups + 1) * size, (groups + 2) * size)
    grad_raw[0, :, lanes] = val_grad[...].T.astype(BF)
    used = (groups + 2) * size
    if used < grad_raw.shape[2]:
        grad_raw[0, :, used:] = jnp.zeros((length, grad_raw.shape[2] - used), BF)


def attend_call(groups, size, kv_heads, raw, cosine, sine, segments, gains):
    rows, length, lanes = raw.shape
    lanes //= kv_heads
    out_lanes = padded(groups * size)
    block = min(256, length)
    whole = lambda r, k: (r, 0, 0)
    part = lambda r, k: (r, 0, k)
    return pl.pallas_call(
        functools.partial(attend_tiles, groups, size, block),
        name="attend",
        grid=(rows, kv_heads),
        in_specs=[
            pl.BlockSpec((1, length, lanes), part),
            pl.BlockSpec((1, length, size), whole),
            pl.BlockSpec((1, length, size), whole),
            pl.BlockSpec((1, length, 1), whole),
            pl.BlockSpec((1, 1, length), whole),
            pl.BlockSpec((2, size), lambda r, k: (0, 0)),
        ],
        out_specs=(
            pl.BlockSpec((1, length, out_lanes), part),
            pl.BlockSpec((1, 1, groups, length, length), lambda r, k: (r, k, 0, 0, 0)),
            pl.BlockSpec((1, 1, groups, length, 1), lambda r, k: (r, k, 0, 0, 0)),
            pl.BlockSpec((1, length, lanes), part),
        ),
        out_shape=(
            jax.ShapeDtypeStruct((rows, length, kv_heads * out_lanes), BF),
            jax.ShapeDtypeStruct((rows, kv_heads, groups, length, length), BF),
            jax.ShapeDtypeStruct((rows, kv_heads, groups, length, 1), F32),
            jax.ShapeDtypeStruct((rows, length, kv_heads * lanes), BF),
        ),
        scratch_shapes=[pltpu.VMEM((groups, length, size), BF)],
        cost_estimate=estimate(27),
        compiler_params=pltpu.CompilerParams(vmem_limit_bytes=VMEM_BYTES),
    )(raw, cosine, sine, segments[:, :, None], segments[:, None, :], gains)


def attend_back_call(groups, size, kv_heads, raw, turned, probs, totals, out, grad_out, cosine, sine, gains):
    rows, length, lanes = raw.shape
    lanes //= kv_heads
    out_lanes = padded(groups * size)
    block = min(256, length)
    whole = lambda r, k: (r, 0, 0)
    part = lambda r, k: (r, 0, k)
    fixed = lambda r, k: (0, 0)
    return pl.pallas_call(
        functools.partial(attend_back_tiles, groups, size, block),
        name="attend_back",
        grid=(rows, kv_heads),
        in_specs=[
            pl.BlockSpec((1, length, lanes), part),
            pl.BlockSpec((1, length, lanes), part),
            pl.BlockSpec((1, 1, groups, length, length), lambda r, k: (r, k, 0, 0, 0)),
            pl.BlockSpec((1, 1, groups, length, 1), lambda r, k: (r, k, 0, 0, 0)),
            pl.BlockSpec((1, length, out_lanes), part),
            pl.BlockSpec((1, length, out_lanes), part),
            pl.BlockSpec((1, length, size), whole),
            pl.BlockSpec((1, length, size), whole),
            pl.BlockSpec((2, size), fixed),
        ],
        out_specs=(
            pl.BlockSpec((1, length, lanes), part),
            pl.BlockSpec((2, size), fixed),
        ),
        out_shape=(
            jax.ShapeDtypeStruct((rows, length, kv_heads * lanes), BF),
            jax.ShapeDtypeStruct((2, size), F32),
        ),
        scratch_shapes=[
            pltpu.VMEM((length // block, groups * block, size), BF),
            pltpu.VMEM((length // block, groups * block, size), BF),
            pltpu.VMEM((length // block, groups * block, 1), F32),
            pltpu.VMEM((groups, length, size), F32),
            pltpu.VMEM((size, length), F32),
            pltpu.VMEM((size, length), F32),
        ],
        cost_estimate=estimate(43),
        compiler_params=pltpu.CompilerParams(vmem_limit_bytes=VMEM_BYTES),
    )(raw, turned, probs, totals, out, grad_out, cosine, sine, gains)


def padded(lanes):
    return (lanes + 127) // 128 * 128


def on_device(
    boundary,
    segments,
    norm_gains,
    qk_gains,
    conv_in,
    conv_kernel,
    conv_out,
    attn_query,
    attn_keyval,
    attn_out,
    ffn_gate_up,
    ffn_down,
):
    is_first = lax.axis_index("section") == 0
    place = lax.axis_index("tensor")
    chips = lax.axis_size("tensor") // 2
    core = place % 2
    chip = place // 2
    steps = [1 << k for k in range(chips.bit_length() - 1)]
    local = boundary[0]
    rows, seq_local, width = local.shape
    seq = segments.shape[1]
    head_dim = qk_gains.shape[1]
    kv_here = attn_keyval.shape[2] // head_dim
    groups = attn_query.shape[1] // head_dim // kv_here
    hidden = ffn_down.shape[2]
    dp = lax.axis_size("dp")
    channels = conv_out.shape[0]
    gains = norm_gains.astype(F32)
    head_gains = qk_gains.astype(F32)
    kernel = conv_kernel.astype(F32)
    up_w = ffn_gate_up[0].transpose(1, 2, 0)
    down_w = ffn_down[0].T
    conv_in_w = conv_in.reshape(width, 3 * channels)
    home_shape = (rows, chips, seq_local, width)
    fused = chips == 2 and dp == 4 and seq_local % TILE == 0

    def mate(values, section):
        return permute(values, section, "tensor", lambda i: i ^ 1)

    def chip_gather(values, section):
        held = values[:, None]
        for step in steps:
            other = permute(held, section, "tensor", lambda i: i ^ (2 * step))
            upper = (chip // step) % 2 == 1
            held = jnp.where(
                upper,
                jnp.concatenate([other, held], axis=1),
                jnp.concatenate([held, other], axis=1),
            )
        return held

    def chip_sum(values, section):
        for step in steps:
            values = values + permute(
                values.astype(BF), section, "tensor", lambda i: i ^ (2 * step)
            ).astype(F32)
        return values

    def chip_scatter(values, section):
        for step in reversed(steps):
            halves = values.reshape((rows, 2, step) + values.shape[2:])
            upper = (chip // step) % 2
            kept = pick(halves, upper, 1)
            sent = pick(halves, 1 - upper, 1).astype(BF)
            values = kept + permute(sent, section, "tensor", lambda i: i ^ (2 * step)).astype(F32)
        return values[:, 0]

    def share(mine, section):
        other = mate(mine, section)
        both = jnp.where(
            core == 0, jnp.stack([mine, other], axis=2), jnp.stack([other, mine], axis=2)
        )
        return both.reshape(rows * seq, width)

    def core_sum(part, section):
        parts = part.reshape(rows, chips, 2, seq_local, width)
        return pick(parts, core, 2).astype(F32) + mate(pick(parts, 1 - core, 2), section).astype(F32)

    def tokens(values):
        return values.reshape(-1, width)

    def homed(values):
        return values.reshape(home_shape)

    def row(gain):
        return gain.reshape(1, width)

    def begin(gain):
        if fused:
            gain = jnp.where(is_first, gain, jnp.ones_like(gain))
            home, full = start_call(0, seq_local, tokens(local), row(gain))
            return homed(home), full
        first = chip_gather(local, 0)
        second = chip_gather(local, 1)
        return (
            jnp.where(is_first, first, second),
            jnp.where(is_first, share(norm(first.astype(F32), gain), 0), share(second, 1)),
        )

    def sum_norm(section, number, part, residual, gain):
        if fused:
            out, full, low = sum_call(
                section, number, False, seq_local, part, row(gain), tokens(residual)
            )
            return homed(out), full, low
        out = residual.astype(F32) + chip_sum(core_sum(part, section), section)
        return out, share(norm(out, gain), section), None

    def sum_back(section, number, part, hidden_in, grad, gain):
        if fused:
            out, full, terms = sum_call(
                section,
                number,
                True,
                seq_local,
                part,
                row(gain),
                tokens(hidden_in),
                tokens(grad),
            )
            return homed(out), full, terms[0]
        dz = chip_sum(core_sum(part, section), section)
        change, terms = norm_back(hidden_in, gain, dz)
        out = grad.astype(F32) + change
        return out, share(out.astype(BF), section), jnp.sum(pick(terms, chip, 1), axis=(0, 1))

    def hop(number, part, hidden_in, gain):
        if fused:
            home, full = hop_call(
                0, number, False, seq_local, part, row(gain), tokens(hidden_in)
            )
            return homed(home), full
        result = pick(hidden_in, chip, 1) + chip_scatter(core_sum(part, 0), 0)
        home = chip_gather(lax.ppermute(result.astype(BF), "section", [(0, 1)]), 1)
        return home, share(norm(home.astype(F32), gain), 1)

    def hop_back(number, part, values, grad, gain):
        if fused:
            home, full, terms = hop_call(
                1,
                number,
                True,
                seq_local,
                part,
                row(gain),
                tokens(values),
                tokens(grad),
            )
            return homed(home), full, terms[0]
        dz = chip_scatter(core_sum(part, 1), 1)
        change, terms = norm_back(pick(values, chip, 1).astype(F32), gain, dz)
        result = pick(grad, chip, 1) + change
        home = chip_gather(lax.ppermute(result.astype(BF), "section", [(1, 0)]), 0)
        return home, share(home, 0), jnp.sum(terms, axis=(0, 1))

    def end(number, first, second):
        if fused:
            return end_call(number, seq_local, first, second).reshape(rows, seq_local, width)
        return jnp.where(
            is_first,
            chip_scatter(core_sum(first, 0), 0),
            chip_scatter(core_sum(second, 1), 1),
        )

    def either(first, first_args, second, second_args):
        def zeros(function, args):
            shapes = jax.eval_shape(function, *args)
            return jax.tree.map(lambda one: jnp.zeros(one.shape, one.dtype), shapes)

        return lax.cond(
            is_first,
            lambda one, two: (first(*one), zeros(second, two)),
            lambda one, two: (zeros(first, one), second(*two)),
            first_args,
            second_args,
        )

    def nothing():
        return ()

    def by_row(values):
        return values.reshape(rows, seq, values.shape[-1])

    def conv_parts(project, masks_list):
        gate_in = project[..., :channels] * project[..., 2 * channels :]
        running = kernel[0] * gate_in
        for lag in range(1, kernel.shape[0]):
            running = running + kernel[lag] * delay_rows(gate_in, lag) * masks_list[lag - 1]
        return gate_in, running

    def conv_forward(full):
        project = by_row(mm("td,de->te", full, conv_in_w))
        unused, running = conv_parts(project, lag_masks(segments, kernel.shape[0]))
        mixed = (project[..., channels : 2 * channels] * running).astype(BF).reshape(-1, channels)
        return mm("te,ed->td", mixed, conv_out, BF), project.astype(BF), mixed

    def conv_backward(grad_full, project, mixed, full):
        masks_list = lag_masks(segments, kernel.shape[0])
        project = project.astype(F32)
        gate_in, running = conv_parts(project, masks_list)
        grad_mixed = by_row(mm("td,ed->te", grad_full, conv_out))
        grad_c = grad_mixed * running
        grad_run = grad_mixed * project[..., channels : 2 * channels]
        grad_in = kernel[0] * grad_run
        grad_kernel = [jnp.sum(grad_run * gate_in, axis=(0, 1))]
        for lag in range(1, kernel.shape[0]):
            mask = masks_list[lag - 1]
            grad_in = grad_in + kernel[lag] * advance_rows(grad_run * mask, lag)
            grad_kernel.append(jnp.sum(grad_run * mask * delay_rows(gate_in, lag), axis=(0, 1)))
        grad_low = jnp.concatenate(
            [grad_in * project[..., 2 * channels :], grad_c, grad_in * project[..., :channels]],
            axis=-1,
        )
        grad_low = grad_low.astype(BF).reshape(-1, 3 * channels)
        part = mm("te,de->td", grad_low, conv_in_w, BF)
        grad_cout = mm("te,td->ed", mixed, grad_full, BF)
        grad_cin = mm("td,te->de", full, grad_low, BF)
        taps = jnp.stack(grad_kernel).astype(BF)
        each = [grad_cin[:, i * channels : (i + 1) * channels] for i in range(3)]
        grad_cout = jnp.concatenate([grad_cout, jnp.pad(taps, ((0, 16 - taps.shape[0]), (0, width - channels)))])
        return part, each + [grad_cout]

    def by_kv(values, axis):
        shape = values.shape[:axis] + (kv_here, -1) + values.shape[axis + 1 :]
        return values.reshape(shape)

    def attn_setup():
        keyval = [by_kv(attn_keyval[:, i], 1) for i in range(2)]
        into = jnp.concatenate([by_kv(attn_query, 1)] + keyval, axis=2)
        used = into.shape[2]
        into = jnp.pad(into, ((0, 0), (0, 0), (0, padded(used) - used)))
        out = by_kv(attn_out, 0)
        used = out.shape[1]
        out = jnp.pad(out, ((0, 0), (0, padded(used) - used), (0, 0)))
        cosine, sine = rope_tables(segments, head_dim // 2)
        twice = lambda table: jnp.concatenate([table, table], axis=-1)
        return into.reshape(width, -1), out.reshape(-1, width), twice(cosine), twice(sine)

    def attn_forward(full, into, outof, cosine, sine):
        raw = by_row(mm("td,de->te", full, into))
        out, probs, totals, turned = attend_call(
            groups, head_dim, kv_here, raw, cosine, sine, segments, head_gains
        )
        flat = out.reshape(rows * seq, -1)
        return mm("te,ed->td", flat, outof, BF), raw, turned, probs, totals, out

    def attn_backward(grad_full, raw, turned, probs, totals, out, into, outof, cosine, sine):
        grad_out = by_row(mm("td,ed->te", grad_full, outof, BF))
        grad_raw, grad_gains = attend_back_call(
            groups,
            head_dim,
            kv_here,
            raw,
            turned,
            probs,
            totals,
            out,
            grad_out,
            cosine,
            sine,
            head_gains,
        )
        grad_raw = grad_raw.reshape(rows * seq, -1)
        return mm("te,de->td", grad_raw, into, BF), grad_raw, grad_gains

    def attn_weights(full, grad_raw, out, grad_full):
        grad_into = by_kv(mm("td,te->de", full, grad_raw, BF), 1)
        grad_out = by_kv(mm("te,td->ed", out.reshape(rows * seq, -1), grad_full, BF), 0)
        cut = groups * head_dim
        grad_keyval = [
            grad_into[:, :, cut + i * head_dim : cut + (i + 1) * head_dim].reshape(width, -1)
            for i in range(2)
        ]
        return (
            grad_into[:, :, :cut].reshape(attn_query.shape),
            jnp.stack(grad_keyval, axis=1),
            grad_out[:, :cut].reshape(attn_out.shape),
        )

    def weights(full, grad_gu, grad_full, act):
        grad_up = mm("tf,td->fd", grad_gu, full, BF)
        grad_down = mm("tf,td->fd", act, grad_full, BF)
        return grad_up.reshape(2, -1, width)[:, :hidden], grad_down[:hidden]

    def choose(function, first_args, second_args):
        return lax.cond(
            is_first,
            lambda one, two: function(*one),
            lambda one, two: function(*two),
            first_args,
            second_args,
        )

    def gather_shards(home_tokens):
        return lax.all_gather(home_tokens, "dp", axis=0, tiled=True)

    def with_mate(mine, sections, *others):
        size = lax.axis_size("tensor")
        pairs = [p for one in sections for p in section_pairs(one, size, lambda i: i ^ 1)]
        mine = hold_call(mine, *others)
        return mine, lax.ppermute(mine, ("section", "tensor"), pairs)

    def after(values, *others):
        return lax.optimization_barrier((values, others))[0]

    start_home, start_full = begin(gains[0, 0])
    (part, project, mixed), setup = either(conv_forward, (start_full,), attn_setup, ())
    h1, full1, low1 = sum_norm(0, 1, part, start_home, gains[0, 1])
    if fused:
        all_a = gather_shards(low1)
    gu1, part = ffn_call(0, seq_local, full1, up_w, down_w)

    x2_home, z3 = hop(2, part, h1, gains[1, 0])
    unused, (part, *saved) = either(nothing, (), attn_forward, (z3,) + setup)
    h3, full2, low2 = sum_norm(1, 3, part, x2_home, gains[1, 1])
    if fused:
        all_b = gather_shards(low2)
    gu2 = ffn_call(1, seq_local, full2, up_w, None)

    grad_gu2, act2, part = ffn_back_call(1, seq_local, start_full, gu2, up_w, down_w)
    if fused:
        all_a = with_mate(all_a, (0, 1), gu2)
        gu_mine = others_up_call(0, seq_local, dp, all_a[0], up_w, None)
        part = hold_call(part, gu_mine)
    gh3, gm3, gain_ffn2 = sum_back(1, 4, part, h3, start_home, gains[1, 1])
    if fused:
        gu_mate = others_up_call(0, seq_local, dp, all_a[1], up_w, None, gm3)
        gm3 = hold_call(gm3, gu_mate)
    unused, (part, grad_raw, head_grads) = either(
        nothing, (), attn_backward, (gm3, *saved) + setup
    )
    g_home, g_full, gain_mix2 = hop_back(5, part, x2_home, gh3, gains[1, 0])
    if fused:
        all_c = gather_shards(tokens(g_home))

    grad_gu1, act1, part = ffn_back_call(0, seq_local, g_full, gu1, up_w, down_w)
    part_out = down_call(1, seq_local, gu2, down_w, g_home)
    if fused:
        all_b = with_mate(all_b, (1,), part_out)
        gu_mine = others_up_call(1, seq_local, dp, all_b[0], up_w, gu_mine, part_out)
        part = hold_call(part, gu_mine)
    gh1, gm1, gain_ffn1 = sum_back(0, 6, part, h1, g_home, gains[0, 1])
    (part, conv_grads), attn_grads = either(
        conv_backward,
        (gm1, project, mixed, start_full),
        attn_weights,
        (z3, grad_raw, saved[-1], gm3),
    )
    if fused:
        gu_mate = others_up_call(1, seq_local, dp, all_b[1], up_w, gu_mate, gm1)
        part_out = hold_call(part_out, gu_mate)
    total = end(7, part, part_out)
    change, terms = norm_back(local.astype(F32), gains[0, 0], total)
    gain_mix1 = jnp.sum(terms, axis=(0, 1))
    boundary_out = jnp.where(is_first, pick(gh1, chip, 1) + change, pick(h3, chip, 1) + total)[None]

    if fused:
        all_c = with_mate(all_c, (0,), total)
        grad_up, grad_down = weight_call(
            seq_local,
            dp,
            (*all_a, *all_c, full1, grad_gu1, g_full, act1),
            (*all_b, *all_a, full2, grad_gu2, start_full, act2),
            (gu_mine, gu_mate),
            down_w,
        )
    else:
        grad_up, grad_down = choose(
            weights, (full1, grad_gu1, g_full, act1), (full2, grad_gu2, start_full, act2)
        )
        grad_up, grad_down = lax.psum((grad_up, grad_down), "dp")
    full_gu = grad_up.astype(F32).transpose(2, 0, 1)[None]
    full_down = grad_down.astype(F32).T[None]

    zero = jnp.zeros_like(gain_mix1)
    first_gains = jnp.concatenate([gain_mix1, gain_ffn1, zero, zero])
    second_gains = jnp.concatenate([zero, zero, gain_mix2, gain_ffn2])
    small = jnp.concatenate([jnp.where(is_first, first_gains, second_gains), head_grads.reshape(-1)])
    if fused:
        small = hold_call(small.reshape(8, -1), grad_down)
        small = total_call(11, small, 4 * chips, dp).reshape(-1)
    else:
        small = lax.psum(small, ("section", "tensor", "dp"))
    mixer_sums = lax.psum(tuple(conv_grads) + tuple(attn_grads), ("section", "dp"))
    mixer_sums = [hold_call(v, small) for v in mixer_sums]
    *sum_cin, sum_cout, sum_aq, sum_akv, sum_aout = [v.astype(F32) for v in mixer_sums]
    sum_kernel = sum_cout[channels : channels + conv_kernel.shape[0], :channels]
    sum_cin = jnp.stack(sum_cin).transpose(1, 0, 2)
    sum_cout = sum_cout[:channels]

    cut = 4 * width
    return (
        boundary_out,
        small[:cut].reshape(norm_gains.shape),
        small[cut:].reshape(qk_gains.shape),
        sum_cin,
        sum_kernel,
        sum_cout,
        sum_aq,
        sum_akv,
        sum_aout,
        full_gu,
        full_down,
    )


def solution(mesh):
    placed = (
        P("section", "dp", "tensor", None),
        P("dp", None),
        P(),
        P(),
        P(None, None, "tensor"),
        P(None, "tensor"),
        P("tensor", None),
        P(None, "tensor"),
        P(None, None, "tensor"),
        P("tensor", None),
        P("section", None, None, "tensor"),
        P("section", None, "tensor"),
    )
    def within(*args):
        with jax.sharding.use_abstract_mesh(mesh.abstract_mesh):
            return mapped(*args)

    mapped = jax.shard_map(
        on_device,
        mesh=mesh,
        in_specs=placed,
        out_specs=(
            P("section", "dp", "tensor", None),
            P(),
            P(),
            P(None, None, "tensor"),
            P(None, "tensor"),
            P("tensor", None),
            P(None, "tensor"),
            P(None, None, "tensor"),
            P("tensor", None),
            P("section", None, None, "tensor"),
            P("section", None, "tensor"),
        ),
        check_vma=False,
    )
    return within
```

```python
import functools

import jax
import jax.numpy as jnp
from jax import lax
from jax.experimental import pallas as pl
from jax.experimental.pallas import tpu as pltpu
from jax.sharding import PartitionSpec as P

EPSILON = 1e-05
THETA = 1000000.0
NEGATIVE = -1e30
BF = jnp.bfloat16
F32 = jnp.float32
MESH = pl.DeviceIdType.MESH
TILE = 32
VMEM_BYTES = 60 * 1024 * 1024
WEIGHT_BYTES = 62 * 1024 * 1024


def mm(spec, left, right, kind=F32):
    return jnp.einsum(spec, left, right, preferred_element_type=F32).astype(kind)


def inverse_rms(values):
    return lax.rsqrt(jnp.mean(values * values, axis=-1, keepdims=True) + EPSILON)


def norm(values, gain):
    return (values * inverse_rms(values) * gain).astype(BF)


def norm_back(values, gain, grad):
    scale = inverse_rms(values)
    normed = values * scale
    weighted = grad * gain
    grad_in = scale * (weighted - normed * jnp.mean(weighted * normed, axis=-1, keepdims=True))
    return grad_in, grad * normed


def section_pairs(section, size, function):
    return [
        (section * size + i, section * size + function(i))
        for i in range(size)
        if 0 <= function(i) < size
    ]


def permute(values, section, axis, function):
    pairs = section_pairs(section, lax.axis_size(axis), function)
    return lax.ppermute(values, ("section", axis), pairs)


def pick(values, index, axis):
    return lax.dynamic_index_in_dim(values, index, axis, keepdims=False)


def delay_rows(values, lag):
    widths = ((0, 0), (lag, 0)) + ((0, 0),) * (values.ndim - 2)
    return jnp.pad(values, widths)[:, : values.shape[1]]


def advance_rows(values, lag):
    widths = ((0, 0), (0, lag)) + ((0, 0),) * (values.ndim - 2)
    return jnp.pad(values, widths)[:, lag:]


def lag_masks(seg_ids, kernel_len):
    masks_list = []
    for lag in range(1, kernel_len):
        shifted = jnp.pad(seg_ids, ((0, 0), (lag, 0)), constant_values=-1)[:, : seg_ids.shape[1]]
        masks_list.append((shifted == seg_ids).astype(F32)[..., None])
    return masks_list


def rope_tables(seg_ids, half_dim):
    starts = jnp.sum((seg_ids[:, None, :] < seg_ids[:, :, None]).astype(jnp.int32), axis=2)
    places = jnp.arange(seg_ids.shape[1], dtype=jnp.int32)[None, :] - starts
    freqs = jnp.power(THETA, -(2.0 * jnp.arange(half_dim, dtype=F32)) / (2.0 * half_dim))
    angles = places.astype(F32)[..., None] * freqs
    return (jnp.cos(angles), jnp.sin(angles))


class Peers:
    def __init__(self):
        self.section = lax.axis_index("section")
        place = lax.axis_index("tensor")
        self.core = place % 2
        self.chip = place // 2
        self.mate = {"tensor": place + 1 - 2 * self.core}
        self.beside = {"tensor": place + 2 - 4 * self.chip}
        self.across = {"section": 1 - self.section}
        self.corner = {"section": 1 - self.section, "tensor": place + 2 - 4 * self.chip}


def greet(signalled, count):
    barrier = pltpu.get_barrier_semaphore()
    for device in signalled:
        pl.semaphore_signal(barrier, inc=1, device_id=device, device_id_type=MESH)
    pl.semaphore_wait(barrier, count)


def remote(source, target, send, receive, device):
    return pltpu.make_async_remote_copy(
        src_ref=source,
        dst_ref=target,
        send_sem=send,
        recv_sem=receive,
        device_id=device,
        device_id_type=MESH,
    )


def loop(count, body):
    lax.fori_loop(0, count, lambda i, unused: (body(i), 0)[1], 0)


def tile_rows(index):
    return pl.ds(pl.multiple_of(index * TILE, TILE), TILE)


def home_tile(j, chip, per_chip):
    each = per_chip // TILE
    return ((j // each) * 2 + chip) * each + j % each


def rms_tile(values):
    return lax.rsqrt(jnp.mean(values * values, axis=-1, keepdims=True) + EPSILON)


def norm_back_tile(values, gain, grad):
    scale = rms_tile(values)
    normed = values * scale
    weighted = grad * gain
    inner = jnp.mean(weighted * normed, axis=-1, keepdims=True)
    return scale * (weighted - normed * inner), grad * normed


def comm_call(kernel, name, number, inputs, outs, scratch, where, micros=52, to=None):
    return pl.pallas_call(
        kernel,
        name=name,
        out_shape=outs,
        in_specs=[pl.BlockSpec(memory_space=space) for space in where],
        out_specs=tuple(
            pl.BlockSpec(memory_space=space) for space in to or [pltpu.VMEM] * len(outs)
        ),
        scratch_shapes=scratch,
        cost_estimate=estimate(micros),
        compiler_params=pltpu.CompilerParams(
            collective_id=number, has_side_effects=True, vmem_limit_bytes=VMEM_BYTES
        ),
    )(*inputs)


def full_tile(i, core, per_chip):
    each = per_chip // TILE
    return ((i // each) * 2 + core) * each + i % each


def sum_tiles(active, backward, per_chip, *refs):
    if backward:
        part, gain, hidden_in, grad_in, out_to, full, gain_out = refs[:7]
        hidden, grad = refs[7:9]
        loads = [(hidden_in, hidden), (grad_in, grad)]
        scratch = refs[9:]
    else:
        part, gain, residual_in, out_to, full, home_low = refs[:6]
        residual = refs[6]
        loads = [(residual_in, residual)]
        scratch = refs[7:]
    out, low, mine, from_mate, summed, from_chip, relayed = scratch[:7]
    own_s, mate_s, mate_r, chip_s, chip_r, relay_s, relay_r, low_s, low_r = scratch[7:16]
    load_s, out_s, full_s, home_s = scratch[16:]
    peers = Peers()
    loads = [
        pltpu.make_async_copy(one, two, load_s.at[k]) for k, (one, two) in enumerate(loads)
    ]
    count = mine.shape[0] // TILE
    pairs = count // 2

    def own_rows(i):
        return tile_rows(full_tile(i, peers.core, per_chip))

    def own_copy(i):
        return pltpu.make_async_copy(part.at[own_rows(i)], mine.at[tile_rows(i)], own_s.at[i])

    def mate_copy(i):
        theirs = tile_rows(full_tile(i, 1 - peers.core, per_chip))
        target = from_mate.at[tile_rows(i)]
        return remote(part.at[theirs], target, mate_s.at[i], mate_r.at[i], peers.mate)

    def direct(i):
        rows = tile_rows(i)
        return remote(summed.at[rows], from_chip.at[rows], chip_s.at[i], chip_r.at[i], peers.beside)

    def detour(p):
        return remote(
            summed.at[tile_rows(2 * p)],
            relayed.at[tile_rows(p)],
            chip_s.at[2 * p],
            relay_r.at[p],
            peers.corner,
        )

    def back(p):
        return remote(
            relayed.at[tile_rows(p)],
            from_chip.at[tile_rows(2 * p)],
            relay_s.at[p],
            chip_r.at[2 * p],
            peers.across,
        )

    def low_copy(i):
        source = low.at[tile_rows(i)]
        return remote(source, full.at[own_rows(i)], low_s.at[i], low_r.at[i], peers.mate)

    def stores(i):
        rows = tile_rows(i)
        copies = [
            pltpu.make_async_copy(out.at[rows], out_to.at[rows], out_s.at[i]),
            pltpu.make_async_copy(low.at[rows], full.at[own_rows(i)], full_s.at[i]),
        ]
        if not backward:
            copies.append(pltpu.make_async_copy(low.at[rows], home_low.at[rows], home_s.at[i]))
        return copies

    def low_wait(i):
        rows = tile_rows(full_tile(i, 1 - peers.core, per_chip))
        source = low.at[tile_rows(i)]
        remote(source, full.at[rows], low_s.at[i], low_r.at[i], peers.mate).wait_recv()

    @pl.when(peers.section == active)
    def work():
        loop(count, lambda i: own_copy(i).start())
        for copy in loads:
            copy.start()
        greet([peers.mate, peers.beside, peers.across], 3)
        loop(count, lambda i: mate_copy(i).start())

        def first(p):
            for k in range(2):
                i = 2 * p + k
                rows = tile_rows(i)
                own_copy(i).wait()
                mate_copy(i).wait_recv()
                total = mine[rows, :].astype(F32) + from_mate[rows, :].astype(F32)
                out[rows, :] = total
                summed[rows, :] = total.astype(BF)
                if k == 0:
                    detour(p).start()
                else:
                    direct(i).start()

        loop(pairs, first)
        for copy in loads:
            copy.wait()
        if backward:
            gain_out[...] = jnp.zeros_like(gain_out)

        def second(i):
            rows = tile_rows(i)
            direct(i).wait_recv()
            total = out[rows, :] + from_chip[rows, :].astype(F32)
            if backward:
                change, terms = norm_back_tile(hidden[rows, :], gain[...], total)
                result = grad[rows, :].astype(F32) + change
                lower = result.astype(BF)
                ours = ((i * TILE) // per_chip) % 2 == peers.chip
                added = jnp.sum(terms, axis=0, keepdims=True)
                gain_out[...] += jnp.where(ours, added, jnp.zeros_like(added))
            else:
                result = residual[rows, :].astype(F32) + total
                lower = (result * rms_tile(result) * gain[...]).astype(BF)
            out[rows, :] = result
            low[rows, :] = lower
            low_copy(i).start()
            for copy in stores(i):
                copy.start()

        loop(count, second)

        def finish(i):
            mate_copy(i).wait_send()
            direct(i).wait_send()
            low_copy(i).wait_send()
            low_wait(i)
            for copy in stores(i):
                copy.wait()

        loop(count, finish)

    @pl.when(peers.section != active)
    def relay():
        greet([peers.corner], 1)

        def step(p):
            detour(p).wait_recv()
            back(p).start()

        loop(pairs, step)
        if not backward:
            for copy in loads:
                copy.start()
                copy.wait()
            copy = pltpu.make_async_copy(residual, home_low, home_s.at[0])
            copy.start()
            copy.wait()
        loop(pairs, lambda p: back(p).wait_send())


def sum_call(active, number, backward, per_chip, part, *rest):
    size, width = part.shape
    size //= 2
    count = size // TILE
    outs = (
        jax.ShapeDtypeStruct((size, width), F32),
        jax.ShapeDtypeStruct((2 * size, width), BF),
    )
    outs += (jax.ShapeDtypeStruct((1, width), F32) if backward else jax.ShapeDtypeStruct((size, width), BF),)
    part, gain, *others = (part,) + rest
    scratch = [pltpu.VMEM((size, width), one.dtype) for one in others]
    scratch += [pltpu.VMEM((size, width), F32)] + [pltpu.VMEM((size, width), BF)] * 5
    scratch += [pltpu.VMEM((size // 2, width), BF)]
    sizes = [count, count, count, count, count, count // 2, count // 2, count, count]
    sizes += [2, count, count, count]
    scratch += [pltpu.SemaphoreType.DMA((n,)) for n in sizes]
    return comm_call(
        functools.partial(sum_tiles, active, backward, per_chip),
        "sum_back" if backward else "sum_norm",
        number,
        (part,) + rest,
        outs,
        scratch,
        [pl.ANY, pltpu.VMEM] + [pl.ANY] * len(others),
        to=[pl.ANY] * 2 + [pltpu.VMEM if backward else pl.ANY],
    )


def spread_tiles(normed, peers, per_chip, gain, home, full, low, sems, arrived, source):
    chip_s, chip_r, low_s, low_r, full_s = sems
    half = home.shape[0] // TILE // 2

    def place(j, chip):
        return home_tile(j, chip, per_chip)

    def chip_copy(j):
        rows = tile_rows(place(j, peers.chip))
        return remote(source(j), home.at[rows], chip_s.at[j], chip_r.at[j], peers.beside)

    def chip_wait(j):
        rows = tile_rows(place(j, 1 - peers.chip))
        remote(source(j), home.at[rows], chip_s.at[j], chip_r.at[j], peers.beside).wait_recv()

    def low_copy(i, k, core):
        rows = tile_rows(full_tile(i, core, per_chip))
        return remote(low.at[tile_rows(i)], full.at[rows], low_s.at[k], low_r.at[k], peers.mate)

    def store(i):
        rows = tile_rows(full_tile(i, peers.core, per_chip))
        return pltpu.make_async_copy(low.at[tile_rows(i)], full.at[rows], full_s.at[i])

    def lower(i, values):
        wide = values.astype(F32)
        if normed == "all":
            wide = wide * rms_tile(wide) * gain[...]
        elif normed == "first":
            scale = rms_tile(wide)
            wide = wide * jnp.where(peers.section == 0, scale, jnp.ones_like(scale)) * gain[...]
        low[tile_rows(i), :] = wide.astype(BF)
        store(i).start()

    def own(j):
        arrived(j)
        chip_copy(j).start()
        i = place(j, peers.chip)
        values = source(j)[...]
        home[tile_rows(i), :] = values
        lower(i, values)
        low_copy(i, j, peers.core).start()

    loop(half, own)

    def other(j):
        chip_wait(j)
        i = place(j, 1 - peers.chip)
        lower(i, home[tile_rows(i), :])
        low_copy(i, half + j, peers.core).start()

    loop(half, other)

    def finish(j):
        chip_copy(j).wait_send()
        low_copy(place(j, peers.chip), j, peers.core).wait_send()
        low_copy(place(j, 1 - peers.chip), half + j, peers.core).wait_send()
        low_copy(place(j, peers.chip), j, 1 - peers.core).wait_recv()
        low_copy(place(j, 1 - peers.chip), half + j, 1 - peers.core).wait_recv()
        store(place(j, peers.chip)).wait()
        store(place(j, 1 - peers.chip)).wait()

    loop(half, finish)


def start_tiles(per_chip, local, gain, home, full, low, *sems):
    peers = Peers()
    greet([peers.mate, peers.beside], 2)
    spread_tiles(
        "first",
        peers,
        per_chip,
        gain,
        home,
        full,
        low,
        sems,
        lambda j: None,
        lambda j: local.at[tile_rows(j)],
    )


def start_call(number, per_chip, local, gain):
    size, width = local.shape
    half = size // TILE
    outs = (
        jax.ShapeDtypeStruct((2 * size, width), BF),
        jax.ShapeDtypeStruct((4 * size, width), BF),
    )
    return comm_call(
        functools.partial(start_tiles, per_chip),
        "start",
        number,
        (local, gain),
        outs,
        [pltpu.VMEM((2 * size, width), BF)]
        + [pltpu.SemaphoreType.DMA((n,)) for n in (half, half, 2 * half, 2 * half, 2 * half)],
        [pltpu.VMEM, pltpu.VMEM],
        to=[pltpu.VMEM, pl.ANY],
    )


def scatter_steps(peers, per_chip, parts, mine, from_mate, summed, from_chip, sems, finished, ready=None):
    own_s, mate_s, mate_r, chip_s, chip_r = sems
    half = mine.shape[0] // TILE // 2

    def rows_of(j, chip, core):
        return tile_rows(full_tile(home_tile(j, chip, per_chip), core, per_chip))

    def slot(j, k):
        return tile_rows(half * k + j)

    def chip_of(k):
        return 1 - peers.chip if k == 0 else peers.chip

    def own_copy(j, k, part=parts[0]):
        source = part.at[rows_of(j, chip_of(k), peers.core)]
        return pltpu.make_async_copy(source, mine.at[slot(j, k)], own_s.at[half * k + j])

    def mate_copy(j, k, part=parts[0]):
        source = part.at[rows_of(j, chip_of(k), 1 - peers.core)]
        index = half * k + j
        target = from_mate.at[slot(j, k)]
        return remote(source, target, mate_s.at[index], mate_r.at[index], peers.mate)

    def chip_copy(j):
        rows = tile_rows(j)
        return remote(summed.at[rows], from_chip.at[rows], chip_s.at[j], chip_r.at[j], peers.beside)

    def begin(part):
        for k in range(2):
            loop(half, lambda j: own_copy(j, k, part).start())
            loop(half, lambda j: mate_copy(j, k, part).start())

    if len(parts) == 1:
        begin(parts[0])
    else:
        for section, part in enumerate(parts):
            pl.when(peers.section == section)(functools.partial(begin, part))

    def both(j, k):
        own_copy(j, k).wait()
        mate_copy(j, k).wait_recv()
        return mine[slot(j, k), :].astype(F32) + from_mate[slot(j, k), :].astype(F32)

    def away(j):
        summed[tile_rows(j), :] = both(j, 0).astype(BF)
        chip_copy(j).start()

    loop(half, away)
    if ready:
        ready()

    def last(j):
        total = both(j, 1)
        chip_copy(j).wait_recv()
        finished(j, total + from_chip[tile_rows(j), :].astype(F32))

    loop(half, last)

    def finish(j):
        mate_copy(j, 0).wait_send()
        mate_copy(j, 1).wait_send()
        chip_copy(j).wait_send()

    loop(half, finish)


def scatter_scratch(size, width):
    half = size // TILE // 2
    buffers = [pltpu.VMEM((size, width), BF)] * 2 + [pltpu.VMEM((size // 2, width), BF)] * 2
    counts = (2 * half, 2 * half, 2 * half, half, half)
    return buffers + [pltpu.SemaphoreType.DMA((n,)) for n in counts]


def end_tiles(per_chip, first, second, out, *scratch):
    peers = Peers()
    greet([peers.mate, peers.beside], 2)

    def finished(j, total):
        out[tile_rows(j), :] = total

    scatter_steps(peers, per_chip, (first, second), *scratch[:4], scratch[4:], finished)


def end_call(number, per_chip, first, second):
    size, width = first.shape
    size //= 2
    return comm_call(
        functools.partial(end_tiles, per_chip),
        "end",
        number,
        (first, second),
        (jax.ShapeDtypeStruct((size // 2, width), F32),),
        scatter_scratch(size, width),
        [pl.ANY, pl.ANY],
    )[0]


def hop_tiles(source, backward, per_chip, *refs):
    if backward:
        part, gain, values_in, grad_in, home, full, gain_out = refs[:7]
        values, grad = refs[7:9]
        loads = [(values_in, values), (grad_in, grad)]
        scratch = refs[9:]
    else:
        part, gain, values_in, home, full = refs[:5]
        values = refs[5]
        loads = [(values_in, values)]
        scratch = refs[6:]
    load_s, low, crossing, landed, cross_s, cross_r = scratch[:6]
    spread_sems = scratch[6:11]
    buffers = scratch[11:15]
    scatter_sems = scratch[15:]
    loads = [
        pltpu.make_async_copy(one, two, load_s.at[k]) for k, (one, two) in enumerate(loads)
    ]
    peers = Peers()
    half = crossing.shape[0] // TILE

    def cross_copy(j):
        rows = tile_rows(j)
        return remote(
            crossing.at[rows], landed.at[rows], cross_s.at[j], cross_r.at[j], peers.across
        )

    @pl.when(peers.section == source)
    def give():
        for copy in loads:
            copy.start()
        greet([peers.mate, peers.beside], 3)
        if backward:
            gain_out[...] = jnp.zeros_like(gain_out)

        def ready():
            for copy in loads:
                copy.wait()

        def finished(j, total):
            own = tile_rows(home_tile(j, peers.chip, per_chip))
            if backward:
                change, terms = norm_back_tile(values[own, :].astype(F32), gain[...], total)
                result = grad[own, :] + change
                gain_out[...] += jnp.sum(terms, axis=0, keepdims=True)
            else:
                result = values[own, :] + total
            crossing[tile_rows(j), :] = result.astype(BF)
            cross_copy(j).start()

        scatter_steps(peers, per_chip, (part,), *buffers, scatter_sems, finished, ready)
        loop(half, lambda j: cross_copy(j).wait_send())

    @pl.when(peers.section != source)
    def take():
        greet([peers.mate, peers.beside, peers.across], 2)
        spread_tiles(
            None if backward else "all",
            peers,
            per_chip,
            gain,
            home,
            full,
            low,
            spread_sems,
            lambda j: cross_copy(j).wait_recv(),
            lambda j: landed.at[tile_rows(j)],
        )


def hop_call(source, number, backward, per_chip, part, *rest):
    size, width = part.shape
    size //= 2
    half = size // TILE // 2
    outs = (
        jax.ShapeDtypeStruct((size, width), BF),
        jax.ShapeDtypeStruct((2 * size, width), BF),
    )
    if backward:
        outs += (jax.ShapeDtypeStruct((1, width), F32),)
    gain, *others = rest
    scratch = [pltpu.VMEM((size, width), one.dtype) for one in others]
    scratch += [pltpu.SemaphoreType.DMA((2,)), pltpu.VMEM((size, width), BF)]
    scratch += [pltpu.VMEM((size // 2, width), BF)] * 2
    sizes = (half, half, half, half, 2 * half, 2 * half, 2 * half)
    scratch += [pltpu.SemaphoreType.DMA((n,)) for n in sizes]
    return comm_call(
        functools.partial(hop_tiles, source, backward, per_chip),
        "hop_back" if backward else "hop",
        number,
        (part,) + rest,
        outs,
        scratch + scatter_scratch(size, width),
        [pl.ANY, pltpu.VMEM] + [pl.ANY] * len(others),
        to=[pltpu.VMEM, pl.ANY] + [pltpu.VMEM] * backward,
    )


def silu_parts(gu):
    lanes = gu.shape[1] // 2
    gate = gu[:, :lanes].astype(F32)
    up = gu[:, lanes:].astype(F32)
    return gate, up, 1.0 / (1.0 + jnp.exp(-gate))


def load_up(up_w, up_v, sems):
    hidden = up_w.shape[1]
    lanes = up_v.shape[0] // 2
    copies = [
        pltpu.make_async_copy(up_w.at[c], up_v.at[pl.ds(c * lanes, hidden)], sems.at[c])
        for c in range(2)
    ]
    for c, copy in enumerate(copies):
        copy.start()
        if lanes > hidden:
            up_v[c * lanes + hidden : (c + 1) * lanes, :] = jnp.zeros(
                (lanes - hidden, up_v.shape[1]), BF
            )
    return copies


def load_down(down_w, down_v, sems):
    hidden = down_w.shape[0]
    lanes = down_v.shape[0]
    copy = pltpu.make_async_copy(down_w, down_v.at[pl.ds(0, hidden)], sems.at[2])
    copy.start()
    if lanes > hidden:
        down_v[hidden:, :] = jnp.zeros((lanes - hidden, down_v.shape[1]), BF)
    return [copy]


def wait_all(copies):
    for copy in copies:
        copy.wait()


def only(active, run):
    if active is None:
        run()
    else:
        pl.when(lax.axis_index("section") == active)(run)


def stream(body, grid, inputs, outs):
    def spec(item):
        ref, rows, place = item
        return pl.BlockSpec((rows, ref.shape[1]), lambda *g: (place(*g), 0))

    pltpu.emit_pipeline(
        body,
        grid=grid,
        in_specs=[spec(item) for item in inputs],
        out_specs=[spec(item) for item in outs],
    )(*[item[0] for item in inputs + outs])


def gate_up_body(up_v):
    def body(z_t, gu_t):
        gu_t[...] = dot(z_t[...], up_v[...], (1, 1)).astype(BF)

    return body


def ffn_tiles(active, tile, with_down, *refs):
    if with_down:
        full, up_w, down_w, gu, part, up_v, down_v, sems = refs
    else:
        full, up_w, gu, up_v, sems = refs

    def run():
        copies = load_up(up_w, up_v, sems)
        if with_down:
            copies += load_down(down_w, down_v, sems)
        wait_all(copies)

        def body(z_t, gu_t, part_t):
            low = dot(z_t[...], up_v[...], (1, 1)).astype(BF)
            gu_t[...] = low
            gate, up, sig = silu_parts(low)
            act = (gate * sig * up).astype(BF)
            part_t[...] = dot(act, down_v[...], (1, 0)).astype(BF)

        here = lambda i: i
        grid = (full.shape[0] // tile,)
        if with_down:
            stream(body, grid, [(full, tile, here)], [(gu, tile, here), (part, tile, here)])
        else:
            stream(gate_up_body(up_v), grid, [(full, tile, here)], [(gu, tile, here)])

    only(active, run)


def down_tiles(active, tile, gu, down_w, *refs):
    part, down_v, sems = refs[-3:]

    def run():
        wait_all(load_down(down_w, down_v, sems))

        def body(gu_t, part_t):
            gate, up, sig = silu_parts(gu_t[...])
            part_t[...] = dot((gate * sig * up).astype(BF), down_v[...], (1, 0)).astype(BF)

        here = lambda i: i
        stream(body, (gu.shape[0] // tile,), [(gu, tile, here)], [(part, tile, here)])

    only(active, run)


def back_body(up_v, down_v):
    def body(g_t, gu_t, grad_t, act_t, *part_t):
        grad_act = dot(g_t[...], down_v[...], (1, 1))
        gate, up, sig = silu_parts(gu_t[...])
        silu = gate * sig
        act_t[...] = (silu * up).astype(BF)
        slope = sig + silu * (1.0 - sig)
        lanes = gate.shape[1]
        grad_t[:, :lanes] = (grad_act * up * slope).astype(BF)
        grad_t[:, lanes:] = (grad_act * silu).astype(BF)
        if part_t:
            part_t[0][...] = dot(grad_t[...], up_v[...], (1, 0)).astype(BF)

    return body


def ffn_back_tiles(active, tile, grad, gu, up_w, down_w, grad_gu, act, part, up_v, down_v, sems):
    def run():
        wait_all(load_down(down_w, down_v, sems) + load_up(up_w, up_v, sems))
        here = lambda i: i
        stream(
            back_body(up_v, down_v),
            (grad.shape[0] // tile,),
            [(ref, tile, here) for ref in (grad, gu)],
            [(ref, tile, here) for ref in (grad_gu, act, part)],
        )

    only(active, run)


def others_up_tiles(active, tile, shards, source, up_w, *refs):
    out, up_v, sems = refs[-3:]

    def run():
        wait_all(load_up(up_w, up_v, sems))
        spot = lax.axis_index("dp")
        count = source.shape[0] // tile // shards
        place = lambda k, i: ((spot + 1 + k) % shards) * count + i
        items = [(source, tile, place)], [(out, tile, place)]
        stream(gate_up_body(up_v), (shards - 1, count), *items)

    only(active, run)


def weight_tiles(tile, shards, chunks, *refs):
    sides = refs[:8], refs[8:16]
    others_gu = refs[16:18]
    down_w, out_up, out_down, up_sum, down_sum, down_v, sems = refs[18:]
    hidden = out_down.shape[0]
    lanes = down_sum.shape[0]
    piece = lanes // chunks
    copies = load_down(down_w, down_v, sems)
    up_sum[...] = jnp.zeros_like(up_sum)
    down_sum[...] = jnp.zeros_like(down_sum)
    spot = lax.axis_index("dp")

    def add(c, z_t, g_t, grad_gate, grad_up, act):
        rows = slice(c * piece, (c + 1) * piece)
        more = slice(lanes + c * piece, lanes + (c + 1) * piece)
        up_sum[rows, :] += dot(grad_gate, z_t[...], (0, 0))
        up_sum[more, :] += dot(grad_up, z_t[...], (0, 0))
        down_sum[rows, :] += dot(act, g_t[...], (0, 0))

    def own_body(z_t, grad_t, g_t, act_t):
        for c in range(chunks):
            rows = slice(c * piece, (c + 1) * piece)
            more = slice(lanes + c * piece, lanes + (c + 1) * piece)
            add(c, z_t, g_t, grad_t[:, rows], grad_t[:, more], act_t[:, rows])

    def body(z_t, g_t, gu_t):
        for c in range(chunks):
            rows = slice(c * piece, (c + 1) * piece)
            more = slice(lanes + c * piece, lanes + (c + 1) * piece)
            grad_act = dot(g_t[...], down_v[rows, :], (1, 1))
            gate = gu_t[:, rows].astype(F32)
            up = gu_t[:, more].astype(F32)
            sig = 1.0 / (1.0 + jnp.exp(-gate))
            silu = gate * sig
            slope = sig + silu * (1.0 - sig)
            add(
                c,
                z_t,
                g_t,
                (grad_act * up * slope).astype(BF),
                (grad_act * silu).astype(BF),
                (silu * up).astype(BF),
            )

    def run(z_mine, z_mate, g_mine, g_mate, full, grad_gu, grad_full, act):
        here = lambda i: i
        items = [(ref, tile, here) for ref in (full, grad_gu, grad_full, act)]
        stream(own_body, (full.shape[0] // tile,), items, [])
        count = z_mine.shape[0] // tile // shards
        place = lambda k, i: ((spot + 1 + k) % shards) * count + i
        for z, g, gu in ((z_mine, g_mine, others_gu[0]), (z_mate, g_mate, others_gu[1])):
            items = [(ref, tile, place) for ref in (z, g, gu)]
            stream(body, (shards - 1, count), items, [])

    wait_all(copies)
    for section in range(2):
        only(section, functools.partial(run, *sides[section]))
    copies = [
        pltpu.make_async_copy(up_sum.at[pl.ds(c * lanes, hidden)], out_up.at[c], sems.at[c])
        for c in range(2)
    ]
    copies += [pltpu.make_async_copy(down_sum.at[pl.ds(0, hidden)], out_down, sems.at[2])]
    for copy in copies:
        copy.start()
    wait_all(copies)


def ffn_pallas(kernel, name, inputs, outs, weights, micros, aliases=None):
    return pl.pallas_call(
        kernel,
        name=name,
        out_shape=tuple(jax.ShapeDtypeStruct(shape, BF) for shape in outs),
        in_specs=[pl.BlockSpec(memory_space=pl.ANY)] * len(inputs),
        out_specs=tuple(pl.BlockSpec(memory_space=pl.ANY) for unused in outs),
        scratch_shapes=[pltpu.VMEM(shape, BF) for shape in weights]
        + [pltpu.SemaphoreType.DMA((3,))],
        input_output_aliases=aliases or {},
        cost_estimate=estimate(micros),
        compiler_params=pltpu.CompilerParams(vmem_limit_bytes=VMEM_BYTES),
    )(*inputs)


def estimate(micros):
    return pl.CostEstimate(flops=0, bytes_accessed=int(micros * 3.3e6), transcendentals=0)


def weight_shapes(up_w):
    lanes = padded(up_w.shape[1])
    return (2 * lanes, up_w.shape[2]), (lanes, up_w.shape[2])


def ffn_call(active, tile, full, up_w, down_w):
    up, down = weight_shapes(up_w)
    gu = (full.shape[0], up[0])
    if down_w is None:
        kernel = functools.partial(ffn_tiles, active, tile, False)
        return ffn_pallas(kernel, "gate_up", (full, up_w), (gu,), (up,), 30)[0]
    kernel = functools.partial(ffn_tiles, active, tile, True)
    return ffn_pallas(kernel, "ffn", (full, up_w, down_w), (gu, full.shape), (up, down), 44)


def down_call(active, tile, gu, down_w, *earlier):
    rows, lanes = gu.shape
    return ffn_pallas(
        functools.partial(down_tiles, active, tile),
        "down",
        (gu, down_w) + earlier,
        ((rows, down_w.shape[1]),),
        ((lanes // 2, down_w.shape[1]),),
        20,
    )[0]


def ffn_back_call(active, tile, grad, gu, up_w, down_w):
    up, down = weight_shapes(up_w)
    return ffn_pallas(
        functools.partial(ffn_back_tiles, active, tile),
        "ffn_back",
        (grad, gu, up_w, down_w),
        (gu.shape, (grad.shape[0], down[0]), grad.shape),
        (up, down),
        48,
    )


def others_up_call(active, tile, shards, source, up_w, into, *earlier):
    up = weight_shapes(up_w)[0]
    more = earlier if into is None else (into,) + earlier
    return ffn_pallas(
        functools.partial(others_up_tiles, active, tile, shards),
        "others_up",
        (source, up_w) + more,
        ((source.shape[0], up[0]),),
        (up,),
        42,
        {} if into is None else {2: 0},
    )[0]


def weight_call(tile, shards, first, second, others_gu, down_w):
    hidden, width = down_w.shape
    lanes = padded(hidden)
    inputs = tuple(first) + tuple(second) + tuple(others_gu) + (down_w,)
    return pl.pallas_call(
        functools.partial(weight_tiles, tile, shards, 1),
        name="weights",
        out_shape=(
            jax.ShapeDtypeStruct((2, hidden, width), F32),
            jax.ShapeDtypeStruct((hidden, width), F32),
        ),
        in_specs=[pl.BlockSpec(memory_space=pl.ANY)] * len(inputs),
        out_specs=(pl.BlockSpec(memory_space=pl.ANY),) * 2,
        scratch_shapes=[
            pltpu.VMEM((2 * lanes, width), F32),
            pltpu.VMEM((lanes, width), F32),
            pltpu.VMEM((lanes, width), BF),
            pltpu.SemaphoreType.DMA((3,)),
        ],
        cost_estimate=estimate(60),
        compiler_params=pltpu.CompilerParams(vmem_limit_bytes=WEIGHT_BYTES),
    )(*inputs)


def hold_call(values, *others):
    if not others:
        return values
    return pl.pallas_call(
        lambda *refs: None,
        name="hold",
        out_shape=jax.ShapeDtypeStruct(values.shape, values.dtype),
        in_specs=[pl.BlockSpec(memory_space=pl.ANY)] * (1 + len(others)),
        out_specs=pl.BlockSpec(memory_space=pl.ANY),
        input_output_aliases={0: 0},
        cost_estimate=estimate(1),
        compiler_params=pltpu.CompilerParams(has_side_effects=True),
    )(values, *others)


def total_tiles(values, out, near, far, sends, receives, far_sends, far_receives):
    section = lax.axis_index("section")
    place = lax.axis_index("tensor")
    spot = lax.axis_index("dp")
    size = near.shape[0]
    chips = size // 2
    shards = far.shape[0]
    own = section * chips + place
    steps = [(a, b) for a in range(2) for b in range(chips) if a + b > 0]
    peers = [{"section": (section + a) % 2, "tensor": (place + b) % chips} for a, b in steps]
    shard_peers = [{"dp": (spot + c) % shards} for c in range(1, shards)]
    greet(peers + shard_peers, len(peers) + len(shard_peers))
    near[own] = values[...]
    copies = [
        remote(near.at[own], near.at[own], sends.at[i], receives.at[own], peer)
        for i, peer in enumerate(peers)
    ]
    for copy in copies:
        copy.start()
    for (a, b), peer in zip(steps, peers):
        theirs = ((section + a) % 2) * chips + (place + b) % chips
        remote(near.at[theirs], near.at[theirs], sends.at[0], receives.at[theirs], peer).wait_recv()
    total = near[0]
    for i in range(1, size):
        total = total + near[i]
    far[spot] = total
    far_copies = [
        remote(far.at[spot], far.at[spot], far_sends.at[i], far_receives.at[spot], peer)
        for i, peer in enumerate(shard_peers)
    ]
    for copy in far_copies:
        copy.start()
    for c, peer in enumerate(shard_peers):
        theirs = (spot + c + 1) % shards
        remote(far.at[theirs], far.at[theirs], far_sends.at[0], far_receives.at[theirs], peer).wait_recv()
    total = far[0]
    for i in range(1, shards):
        total = total + far[i]
    out[...] = total
    for copy in copies + far_copies:
        copy.wait_send()


def total_call(number, values, size, shards):
    return comm_call(
        total_tiles,
        "total",
        number,
        (values,),
        (jax.ShapeDtypeStruct(values.shape, F32),),
        [
            pltpu.VMEM((size,) + values.shape, F32),
            pltpu.VMEM((shards,) + values.shape, F32),
            pltpu.SemaphoreType.DMA((size,)),
            pltpu.SemaphoreType.DMA((size,)),
            pltpu.SemaphoreType.DMA((shards,)),
            pltpu.SemaphoreType.DMA((shards,)),
        ],
        [pltpu.VMEM],
        10,
    )[0]


def rotated(values):
    half = values.shape[-1] // 2
    return jnp.concatenate([-values[:, half:], values[:, :half]], axis=-1)


def dot(left, right, dims):
    return lax.dot_general(left, right, ((dims[:1], dims[1:]), ((), ())), preferred_element_type=F32)


def attend_tiles(groups, size, block, raw, cosine, sine, seg_col, seg_row, gains, out, probs, totals, turned, heads):
    length = raw.shape[1]
    cos_t = cosine[0]
    sin_t = sine[0]
    scaling = size ** (-0.5)

    def prepared(values, gain):
        normed = values * rms_tile(values) * gain
        return normed * cos_t + rotated(normed) * sin_t

    for g in range(groups):
        lanes = slice(g * size, (g + 1) * size)
        query = (prepared(raw[0, :, lanes], gains[0:1, :]).astype(BF) * scaling).astype(BF)
        heads[g] = query
        turned[0, :, lanes] = query
    lanes = slice(groups * size, (groups + 1) * size)
    keyed = prepared(raw[0, :, lanes], gains[1:2, :]).astype(BF)
    turned[0, :, lanes] = keyed
    lanes = slice((groups + 1) * size, (groups + 2) * size)
    valued = raw[0, :, lanes].astype(BF)
    turned[0, :, lanes] = valued
    ones = (lax.broadcasted_iota(jnp.int32, (length, size), 1) == 0).astype(BF)
    widened = jnp.concatenate([valued, ones], axis=1)
    used = (groups + 2) * size
    if used < turned.shape[2]:
        turned[0, :, used:] = jnp.zeros((length, turned.shape[2] - used), BF)
    for i in range(length // block):
        rows = slice(i * block, (i + 1) * block)
        span = (i + 1) * block
        query_pos = i * block + lax.broadcasted_iota(jnp.int32, (block, span), 0)
        key_pos = lax.broadcasted_iota(jnp.int32, (block, span), 1)
        allowed = (key_pos <= query_pos) & (seg_col[0, rows, :] == seg_row[0, :, :span])

        def head(g):
            scores = dot(heads[g, rows, :], keyed[:span], (1, 1))
            expon = jnp.exp(jnp.where(allowed, scores, NEGATIVE)).astype(BF)
            probs[0, 0, g, rows, :span] = expon
            summed = dot(expon, widened[:span], (1, 0))
            total = summed[:, size : size + 1]
            totals[0, 0, g, rows, :] = total
            heads[g, rows, :] = (summed[:, :size] * (1.0 / total)).astype(BF)

        for g in range(groups):
            head(g)
    for g in range(groups):
        out[0, :, g * size : (g + 1) * size] = heads[g]
    if groups * size < out.shape[2]:
        out[0, :, groups * size :] = jnp.zeros((length, out.shape[2] - groups * size), BF)


def attend_back_tiles(
    groups, size, block, raw, turned, probs, totals, out, grad_out, cosine, sine, gains, grad_raw, grad_gains, heads, grads, inner, query_grad, key_grad, val_grad
):
    length = raw.shape[1]
    cos_t = cosine[0]
    sin_t = sine[0]
    scaling = size ** (-0.5)

    @pl.when((pl.program_id(0) == 0) & (pl.program_id(1) == 0))
    def clear():
        grad_gains[...] = jnp.zeros_like(grad_gains)

    blocks = length // block
    for g in range(groups):
        lanes = slice(g * size, (g + 1) * size)
        shared = (grad_out[0, :, lanes].astype(F32) * (1.0 / totals[0, 0, g])).astype(BF)
        mean = jnp.sum(shared.astype(F32) * out[0, :, lanes].astype(F32), axis=-1, keepdims=True)
        for i in range(blocks):
            rows = slice(i * block, (i + 1) * block)
            into = slice(g * block, (g + 1) * block)
            heads[i, into, :] = turned[0, rows, lanes]
            grads[i, into, :] = shared[rows]
            inner[i, into, :] = mean[rows]
    keyed = turned[0, :, groups * size : (groups + 1) * size]
    valued = turned[0, :, (groups + 1) * size : (groups + 2) * size]
    key_grad[...] = jnp.zeros_like(key_grad)
    val_grad[...] = jnp.zeros_like(val_grad)
    for i in range(blocks):
        rows = slice(i * block, (i + 1) * block)
        span = (i + 1) * block
        low = jnp.concatenate([probs[0, 0, g, rows, :span] for g in range(groups)], axis=0)
        grad_probs = dot(grads[i], valued[:span], (1, 1))
        grad_scores = (low.astype(F32) * (grad_probs - inner[i])).astype(BF)
        back_q = dot(grad_scores, keyed[:span], (1, 0)) * scaling
        for g in range(groups):
            query_grad[g, rows, :] = back_q[g * block : (g + 1) * block]
        key_grad[:, :span] += dot(heads[i], grad_scores, (0, 0))
        val_grad[:, :span] += dot(grads[i], low, (0, 0))

    def back(values, gain, grad, which):
        grad = grad * cos_t - rotated(grad) * sin_t
        change, terms = norm_back_tile(values, gain, grad)
        grad_gains[which : which + 1, :] += jnp.sum(terms, axis=0, keepdims=True)
        return change.astype(BF)

    for g in range(groups):
        lanes = slice(g * size, (g + 1) * size)
        grad_raw[0, :, lanes] = back(raw[0, :, lanes], gains[0:1, :], query_grad[g], 0)
    lanes = slice(groups * size, (groups + 1) * size)
    grad_raw[0, :, lanes] = back(raw[0, :, lanes], gains[1:2, :], key_grad[...].T, 1)
    lanes = slice((groups + 1) * size, (groups + 2) * size)
    grad_raw[0, :, lanes] = val_grad[...].T.astype(BF)
    used = (groups + 2) * size
    if used < grad_raw.shape[2]:
        grad_raw[0, :, used:] = jnp.zeros((length, grad_raw.shape[2] - used), BF)


def attend_call(groups, size, kv_heads, raw, cosine, sine, segments, gains):
    rows, length, lanes = raw.shape
    lanes //= kv_heads
    out_lanes = padded(groups * size)
    block = min(256, length)
    whole = lambda r, k: (r, 0, 0)
    part = lambda r, k: (r, 0, k)
    return pl.pallas_call(
        functools.partial(attend_tiles, groups, size, block),
        name="attend",
        grid=(rows, kv_heads),
        in_specs=[
            pl.BlockSpec((1, length, lanes), part),
            pl.BlockSpec((1, length, size), whole),
            pl.BlockSpec((1, length, size), whole),
            pl.BlockSpec((1, length, 1), whole),
            pl.BlockSpec((1, 1, length), whole),
            pl.BlockSpec((2, size), lambda r, k: (0, 0)),
        ],
        out_specs=(
            pl.BlockSpec((1, length, out_lanes), part),
            pl.BlockSpec((1, 1, groups, length, length), lambda r, k: (r, k, 0, 0, 0)),
            pl.BlockSpec((1, 1, groups, length, 1), lambda r, k: (r, k, 0, 0, 0)),
            pl.BlockSpec((1, length, lanes), part),
        ),
        out_shape=(
            jax.ShapeDtypeStruct((rows, length, kv_heads * out_lanes), BF),
            jax.ShapeDtypeStruct((rows, kv_heads, groups, length, length), BF),
            jax.ShapeDtypeStruct((rows, kv_heads, groups, length, 1), F32),
            jax.ShapeDtypeStruct((rows, length, kv_heads * lanes), BF),
        ),
        scratch_shapes=[pltpu.VMEM((groups, length, size), BF)],
        cost_estimate=estimate(27),
        compiler_params=pltpu.CompilerParams(vmem_limit_bytes=VMEM_BYTES),
    )(raw, cosine, sine, segments[:, :, None], segments[:, None, :], gains)


def attend_back_call(groups, size, kv_heads, raw, turned, probs, totals, out, grad_out, cosine, sine, gains):
    rows, length, lanes = raw.shape
    lanes //= kv_heads
    out_lanes = padded(groups * size)
    block = min(256, length)
    whole = lambda r, k: (r, 0, 0)
    part = lambda r, k: (r, 0, k)
    fixed = lambda r, k: (0, 0)
    return pl.pallas_call(
        functools.partial(attend_back_tiles, groups, size, block),
        name="attend_back",
        grid=(rows, kv_heads),
        in_specs=[
            pl.BlockSpec((1, length, lanes), part),
            pl.BlockSpec((1, length, lanes), part),
            pl.BlockSpec((1, 1, groups, length, length), lambda r, k: (r, k, 0, 0, 0)),
            pl.BlockSpec((1, 1, groups, length, 1), lambda r, k: (r, k, 0, 0, 0)),
            pl.BlockSpec((1, length, out_lanes), part),
            pl.BlockSpec((1, length, out_lanes), part),
            pl.BlockSpec((1, length, size), whole),
            pl.BlockSpec((1, length, size), whole),
            pl.BlockSpec((2, size), fixed),
        ],
        out_specs=(
            pl.BlockSpec((1, length, lanes), part),
            pl.BlockSpec((2, size), fixed),
        ),
        out_shape=(
            jax.ShapeDtypeStruct((rows, length, kv_heads * lanes), BF),
            jax.ShapeDtypeStruct((2, size), F32),
        ),
        scratch_shapes=[
            pltpu.VMEM((length // block, groups * block, size), BF),
            pltpu.VMEM((length // block, groups * block, size), BF),
            pltpu.VMEM((length // block, groups * block, 1), F32),
            pltpu.VMEM((groups, length, size), F32),
            pltpu.VMEM((size, length), F32),
            pltpu.VMEM((size, length), F32),
        ],
        cost_estimate=estimate(43),
        compiler_params=pltpu.CompilerParams(vmem_limit_bytes=VMEM_BYTES),
    )(raw, turned, probs, totals, out, grad_out, cosine, sine, gains)


def padded(lanes):
    return (lanes + 127) // 128 * 128


def on_device(
    boundary,
    segments,
    norm_gains,
    qk_gains,
    conv_in,
    conv_kernel,
    conv_out,
    attn_query,
    attn_keyval,
    attn_out,
    ffn_gate_up,
    ffn_down,
):
    is_first = lax.axis_index("section") == 0
    place = lax.axis_index("tensor")
    chips = lax.axis_size("tensor") // 2
    core = place % 2
    chip = place // 2
    steps = [1 << k for k in range(chips.bit_length() - 1)]
    local = boundary[0]
    rows, seq_local, width = local.shape
    seq = segments.shape[1]
    head_dim = qk_gains.shape[1]
    kv_here = attn_keyval.shape[2] // head_dim
    groups = attn_query.shape[1] // head_dim // kv_here
    hidden = ffn_down.shape[2]
    dp = lax.axis_size("dp")
    channels = conv_out.shape[0]
    gains = norm_gains.astype(F32)
    head_gains = qk_gains.astype(F32)
    kernel = conv_kernel.astype(F32)
    up_w = ffn_gate_up[0].transpose(1, 2, 0)
    down_w = ffn_down[0].T
    conv_in_w = conv_in.reshape(width, 3 * channels)
    home_shape = (rows, chips, seq_local, width)
    fused = chips == 2 and dp == 4 and seq_local % TILE == 0

    def mate(values, section):
        return permute(values, section, "tensor", lambda i: i ^ 1)

    def chip_gather(values, section):
        held = values[:, None]
        for step in steps:
            other = permute(held, section, "tensor", lambda i: i ^ (2 * step))
            upper = (chip // step) % 2 == 1
            held = jnp.where(
                upper,
                jnp.concatenate([other, held], axis=1),
                jnp.concatenate([held, other], axis=1),
            )
        return held

    def chip_sum(values, section):
        for step in steps:
            values = values + permute(
                values.astype(BF), section, "tensor", lambda i: i ^ (2 * step)
            ).astype(F32)
        return values

    def chip_scatter(values, section):
        for step in reversed(steps):
            halves = values.reshape((rows, 2, step) + values.shape[2:])
            upper = (chip // step) % 2
            kept = pick(halves, upper, 1)
            sent = pick(halves, 1 - upper, 1).astype(BF)
            values = kept + permute(sent, section, "tensor", lambda i: i ^ (2 * step)).astype(F32)
        return values[:, 0]

    def share(mine, section):
        other = mate(mine, section)
        both = jnp.where(
            core == 0, jnp.stack([mine, other], axis=2), jnp.stack([other, mine], axis=2)
        )
        return both.reshape(rows * seq, width)

    def core_sum(part, section):
        parts = part.reshape(rows, chips, 2, seq_local, width)
        return pick(parts, core, 2).astype(F32) + mate(pick(parts, 1 - core, 2), section).astype(F32)

    def tokens(values):
        return values.reshape(-1, width)

    def homed(values):
        return values.reshape(home_shape)

    def row(gain):
        return gain.reshape(1, width)

    def begin(gain):
        if fused:
            gain = jnp.where(is_first, gain, jnp.ones_like(gain))
            home, full = start_call(0, seq_local, tokens(local), row(gain))
            return homed(home), full
        first = chip_gather(local, 0)
        second = chip_gather(local, 1)
        return (
            jnp.where(is_first, first, second),
            jnp.where(is_first, share(norm(first.astype(F32), gain), 0), share(second, 1)),
        )

    def sum_norm(section, number, part, residual, gain):
        if fused:
            out, full, low = sum_call(
                section, number, False, seq_local, part, row(gain), tokens(residual)
            )
            return homed(out), full, low
        out = residual.astype(F32) + chip_sum(core_sum(part, section), section)
        return out, share(norm(out, gain), section), None

    def sum_back(section, number, part, hidden_in, grad, gain):
        if fused:
            out, full, terms = sum_call(
                section,
                number,
                True,
                seq_local,
                part,
                row(gain),
                tokens(hidden_in),
                tokens(grad),
            )
            return homed(out), full, terms[0]
        dz = chip_sum(core_sum(part, section), section)
        change, terms = norm_back(hidden_in, gain, dz)
        out = grad.astype(F32) + change
        return out, share(out.astype(BF), section), jnp.sum(pick(terms, chip, 1), axis=(0, 1))

    def hop(number, part, hidden_in, gain):
        if fused:
            home, full = hop_call(
                0, number, False, seq_local, part, row(gain), tokens(hidden_in)
            )
            return homed(home), full
        result = pick(hidden_in, chip, 1) + chip_scatter(core_sum(part, 0), 0)
        home = chip_gather(lax.ppermute(result.astype(BF), "section", [(0, 1)]), 1)
        return home, share(norm(home.astype(F32), gain), 1)

    def hop_back(number, part, values, grad, gain):
        if fused:
            home, full, terms = hop_call(
                1,
                number,
                True,
                seq_local,
                part,
                row(gain),
                tokens(values),
                tokens(grad),
            )
            return homed(home), full, terms[0]
        dz = chip_scatter(core_sum(part, 1), 1)
        change, terms = norm_back(pick(values, chip, 1).astype(F32), gain, dz)
        result = pick(grad, chip, 1) + change
        home = chip_gather(lax.ppermute(result.astype(BF), "section", [(1, 0)]), 0)
        return home, share(home, 0), jnp.sum(terms, axis=(0, 1))

    def end(number, first, second):
        if fused:
            return end_call(number, seq_local, first, second).reshape(rows, seq_local, width)
        return jnp.where(
            is_first,
            chip_scatter(core_sum(first, 0), 0),
            chip_scatter(core_sum(second, 1), 1),
        )

    def either(first, first_args, second, second_args):
        def zeros(function, args):
            shapes = jax.eval_shape(function, *args)
            return jax.tree.map(lambda one: jnp.zeros(one.shape, one.dtype), shapes)

        return lax.cond(
            is_first,
            lambda one, two: (first(*one), zeros(second, two)),
            lambda one, two: (zeros(first, one), second(*two)),
            first_args,
            second_args,
        )

    def nothing():
        return ()

    def by_row(values):
        return values.reshape(rows, seq, values.shape[-1])

    def conv_parts(project, masks_list):
        gate_in = project[..., :channels] * project[..., 2 * channels :]
        running = kernel[0] * gate_in
        for lag in range(1, kernel.shape[0]):
            running = running + kernel[lag] * delay_rows(gate_in, lag) * masks_list[lag - 1]
        return gate_in, running

    def conv_forward(full):
        project = by_row(mm("td,de->te", full, conv_in_w))
        unused, running = conv_parts(project, lag_masks(segments, kernel.shape[0]))
        mixed = (project[..., channels : 2 * channels] * running).astype(BF).reshape(-1, channels)
        return mm("te,ed->td", mixed, conv_out, BF), project.astype(BF), mixed

    def conv_backward(grad_full, project, mixed, full):
        masks_list = lag_masks(segments, kernel.shape[0])
        project = project.astype(F32)
        gate_in, running = conv_parts(project, masks_list)
        grad_mixed = by_row(mm("td,ed->te", grad_full, conv_out))
        grad_c = grad_mixed * running
        grad_run = grad_mixed * project[..., channels : 2 * channels]
        grad_in = kernel[0] * grad_run
        grad_kernel = [jnp.sum(grad_run * gate_in, axis=(0, 1))]
        for lag in range(1, kernel.shape[0]):
            mask = masks_list[lag - 1]
            grad_in = grad_in + kernel[lag] * advance_rows(grad_run * mask, lag)
            grad_kernel.append(jnp.sum(grad_run * mask * delay_rows(gate_in, lag), axis=(0, 1)))
        grad_low = jnp.concatenate(
            [grad_in * project[..., 2 * channels :], grad_c, grad_in * project[..., :channels]],
            axis=-1,
        )
        grad_low = grad_low.astype(BF).reshape(-1, 3 * channels)
        part = mm("te,de->td", grad_low, conv_in_w, BF)
        grad_cout = mm("te,td->ed", mixed, grad_full, BF)
        grad_cin = mm("td,te->de", full, grad_low, BF)
        taps = jnp.stack(grad_kernel).astype(BF)
        each = [
            hold_call(grad_cin[:, i * channels : (i + 1) * channels], part) for i in range(3)
        ]
        grad_cout = jnp.concatenate([grad_cout, jnp.pad(taps, ((0, 16 - taps.shape[0]), (0, width - channels)))])
        return part, each + [grad_cout]

    def by_kv(values, axis):
        shape = values.shape[:axis] + (kv_here, -1) + values.shape[axis + 1 :]
        return values.reshape(shape)

    def attn_setup():
        keyval = [by_kv(attn_keyval[:, i], 1) for i in range(2)]
        into = jnp.concatenate([by_kv(attn_query, 1)] + keyval, axis=2)
        used = into.shape[2]
        into = jnp.pad(into, ((0, 0), (0, 0), (0, padded(used) - used)))
        out = by_kv(attn_out, 0)
        used = out.shape[1]
        out = jnp.pad(out, ((0, 0), (0, padded(used) - used), (0, 0)))
        cosine, sine = rope_tables(segments, head_dim // 2)
        twice = lambda table: jnp.concatenate([table, table], axis=-1)
        return into.reshape(width, -1), out.reshape(-1, width), twice(cosine), twice(sine)

    def attn_forward(full, into, outof, cosine, sine):
        raw = by_row(mm("td,de->te", full, into))
        out, probs, totals, turned = attend_call(
            groups, head_dim, kv_here, raw, cosine, sine, segments, head_gains
        )
        flat = out.reshape(rows * seq, -1)
        return mm("te,ed->td", flat, outof, BF), raw, turned, probs, totals, out

    def attn_backward(grad_full, raw, turned, probs, totals, out, into, outof, cosine, sine):
        grad_out = by_row(mm("td,ed->te", grad_full, outof, BF))
        grad_raw, grad_gains = attend_back_call(
            groups,
            head_dim,
            kv_here,
            raw,
            turned,
            probs,
            totals,
            out,
            grad_out,
            cosine,
            sine,
            head_gains,
        )
        grad_raw = grad_raw.reshape(rows * seq, -1)
        return mm("te,de->td", grad_raw, into, BF), grad_raw, grad_gains

    def attn_weights(full, grad_raw, out, grad_full):
        grad_into = by_kv(mm("td,te->de", full, grad_raw, BF), 1)
        grad_out = by_kv(mm("te,td->ed", out.reshape(rows * seq, -1), grad_full, BF), 0)
        cut = groups * head_dim
        grad_keyval = [
            grad_into[:, :, cut + i * head_dim : cut + (i + 1) * head_dim].reshape(width, -1)
            for i in range(2)
        ]
        return (
            grad_into[:, :, :cut].reshape(attn_query.shape),
            jnp.stack(grad_keyval, axis=1),
            grad_out[:, :cut].reshape(attn_out.shape),
        )

    def weights(full, grad_gu, grad_full, act):
        grad_up = mm("tf,td->fd", grad_gu, full, BF)
        grad_down = mm("tf,td->fd", act, grad_full, BF)
        return grad_up.reshape(2, -1, width)[:, :hidden], grad_down[:hidden]

    def choose(function, first_args, second_args):
        return lax.cond(
            is_first,
            lambda one, two: function(*one),
            lambda one, two: function(*two),
            first_args,
            second_args,
        )

    def gather_shards(home_tokens):
        return lax.all_gather(home_tokens, "dp", axis=0, tiled=True)

    def with_mate(mine, sections, *others):
        size = lax.axis_size("tensor")
        pairs = [p for one in sections for p in section_pairs(one, size, lambda i: i ^ 1)]
        mine = hold_call(mine, *others)
        return mine, lax.ppermute(mine, ("section", "tensor"), pairs)

    def after(values, *others):
        return lax.optimization_barrier((values, others))[0]

    start_home, start_full = begin(gains[0, 0])
    (part, project, mixed), setup = either(conv_forward, (start_full,), attn_setup, ())
    h1, full1, low1 = sum_norm(0, 1, part, start_home, gains[0, 1])
    if fused:
        all_a = gather_shards(low1)
    gu1, part = ffn_call(0, seq_local, full1, up_w, down_w)

    x2_home, z3 = hop(2, part, h1, gains[1, 0])
    unused, (part, *saved) = either(nothing, (), attn_forward, (z3,) + setup)
    h3, full2, low2 = sum_norm(1, 3, part, x2_home, gains[1, 1])
    if fused:
        all_b = gather_shards(low2)
    gu2 = ffn_call(1, seq_local, full2, up_w, None)

    grad_gu2, act2, part = ffn_back_call(1, seq_local, start_full, gu2, up_w, down_w)
    if fused:
        all_a = with_mate(all_a, (0, 1), gu2)
        gu_mine = others_up_call(0, seq_local, dp, all_a[0], up_w, None)
        part = hold_call(part, gu_mine)
    gh3, gm3, gain_ffn2 = sum_back(1, 4, part, h3, start_home, gains[1, 1])
    if fused:
        gu_mate = others_up_call(0, seq_local, dp, all_a[1], up_w, None, gm3)
        gm3 = hold_call(gm3, gu_mate)
    unused, (part, grad_raw, head_grads) = either(
        nothing, (), attn_backward, (gm3, *saved) + setup
    )
    g_home, g_full, gain_mix2 = hop_back(5, part, x2_home, gh3, gains[1, 0])
    if fused:
        all_c = gather_shards(tokens(g_home))

    grad_gu1, act1, part = ffn_back_call(0, seq_local, g_full, gu1, up_w, down_w)
    part_out = down_call(1, seq_local, gu2, down_w, g_home)
    if fused:
        all_b = with_mate(all_b, (1,), part_out)
        gu_mine = others_up_call(1, seq_local, dp, all_b[0], up_w, gu_mine, part_out)
        part = hold_call(part, gu_mine)
    gh1, gm1, gain_ffn1 = sum_back(0, 6, part, h1, g_home, gains[0, 1])
    (part, conv_grads), attn_grads = either(
        conv_backward,
        (gm1, project, mixed, start_full),
        attn_weights,
        (z3, grad_raw, saved[-1], gm3),
    )
    if fused:
        gu_mate = others_up_call(1, seq_local, dp, all_b[1], up_w, gu_mate, gm1)
        part_out = hold_call(part_out, gu_mate)
    total = end(7, part, part_out)
    change, terms = norm_back(local.astype(F32), gains[0, 0], total)
    gain_mix1 = jnp.sum(terms, axis=(0, 1))
    boundary_out = jnp.where(is_first, pick(gh1, chip, 1) + change, pick(h3, chip, 1) + total)[None]

    if fused:
        all_c = with_mate(all_c, (0,), total)
        grad_up, grad_down = weight_call(
            seq_local,
            dp,
            (*all_a, *all_c, full1, grad_gu1, g_full, act1),
            (*all_b, *all_a, full2, grad_gu2, start_full, act2),
            (gu_mine, gu_mate),
            down_w,
        )
    else:
        grad_up, grad_down = choose(
            weights, (full1, grad_gu1, g_full, act1), (full2, grad_gu2, start_full, act2)
        )
        grad_up, grad_down = lax.psum((grad_up, grad_down), "dp")
    full_gu = grad_up.astype(F32).transpose(2, 0, 1)[None]
    full_down = grad_down.astype(F32).T[None]

    zero = jnp.zeros_like(gain_mix1)
    first_gains = jnp.concatenate([gain_mix1, gain_ffn1, zero, zero])
    second_gains = jnp.concatenate([zero, zero, gain_mix2, gain_ffn2])
    small = jnp.concatenate([jnp.where(is_first, first_gains, second_gains), head_grads.reshape(-1)])
    if fused:
        small = hold_call(small.reshape(8, -1), grad_down)
        small = total_call(11, small, 4 * chips, dp).reshape(-1)
    else:
        small = lax.psum(small, ("section", "tensor", "dp"))
    mixer_sums = lax.psum(tuple(conv_grads) + tuple(attn_grads), ("section", "dp"))
    mixer_sums = [hold_call(v, small) for v in mixer_sums]
    *sum_cin, sum_cout, sum_aq, sum_akv, sum_aout = [v.astype(F32) for v in mixer_sums]
    sum_kernel = sum_cout[channels : channels + conv_kernel.shape[0], :channels]
    sum_cin = jnp.stack(sum_cin).transpose(1, 0, 2)
    sum_cout = sum_cout[:channels]

    cut = 4 * width
    return (
        boundary_out,
        small[:cut].reshape(norm_gains.shape),
        small[cut:].reshape(qk_gains.shape),
        sum_cin,
        sum_kernel,
        sum_cout,
        sum_aq,
        sum_akv,
        sum_aout,
        full_gu,
        full_down,
    )


def solution(mesh):
    placed = (
        P("section", "dp", "tensor", None),
        P("dp", None),
        P(),
        P(),
        P(None, None, "tensor"),
        P(None, "tensor"),
        P("tensor", None),
        P(None, "tensor"),
        P(None, None, "tensor"),
        P("tensor", None),
        P("section", None, None, "tensor"),
        P("section", None, "tensor"),
    )
    def within(*args):
        with jax.sharding.use_abstract_mesh(mesh.abstract_mesh):
            return mapped(*args)

    mapped = jax.shard_map(
        on_device,
        mesh=mesh,
        in_specs=placed,
        out_specs=(
            P("section", "dp", "tensor", None),
            P(),
            P(),
            P(None, None, "tensor"),
            P(None, "tensor"),
            P("tensor", None),
            P(None, "tensor"),
            P(None, None, "tensor"),
            P("tensor", None),
            P("section", None, None, "tensor"),
            P("section", None, "tensor"),
        ),
        check_vma=False,
    )
    return within
```
